32 devices in a mesh: grp: 4 (over y, x), swap: 8 (over z, core).
Axes of the slice: x: 2, y: 2, z: 4, core: 2. Of those that a mesh axis runs over, the one named last changes fastest.
Arguments:
- tokens: bfloat16 [4, 1024, 8, 512], P('grp', None, 'swap'), may hold values from -6 to 6
- sample_counts: int32 [4], P('grp'), may hold values from 1 to 1024, as said below
- feature_counts: int32 [4], P('grp'), may hold values from 1 to 8, as said below
- attn_in: bfloat16 [2, 512, 1536], replicated, may hold values from -0.25 to 0.25
- attn_out: bfloat16 [2, 512, 512], replicated, may hold values from -1.5 to 1.5
- norm_gain: float32 [3, 512], replicated, may hold values from 0.5 to 1.5
- norm_bias: float32 [3, 512], replicated, may hold values from -1.8 to 1.8
- mlp_in: bfloat16 [512, 2048], replicated, may hold values from -0.25 to 0.25
- mlp_in_bias: float32 [2048], replicated, may hold values from -1.8 to 1.8
- mlp_out: bfloat16 [2048, 512], replicated, may hold values from -0.125 to 0.125
- mlp_out_bias: float32 [512], replicated, may hold values from -1.8 to 1.8
- cotangent: bfloat16 [4, 1024, 8, 512], P('grp', None, 'swap'), may hold values from -6 to 6
Outputs:
- mixed: bfloat16 [4, 1024, 8, 512], P('grp', None, 'swap')
- tokens_grad: bfloat16 [4, 1024, 8, 512], P('grp', None, 'swap')
- attn_in_grad: float32 [2, 512, 1536], P(None, 'swap')
- attn_out_grad: float32 [2, 512, 512], P(None, 'swap')
- norm_gain_grad: float32 [3, 512], P(None, 'swap')
- norm_bias_grad: float32 [3, 512], P(None, 'swap')
- mlp_in_grad: float32 [512, 2048], P('swap')
- mlp_in_bias_grad: float32 [2048], P('swap')
- mlp_out_grad: float32 [2048, 512], P('swap')
- mlp_out_bias_grad: float32 [512], P('swap')
The draws below stay inside these ranges and needn't reach their ends.
Inputs may be any that keep to these rules, and one draw needn't show every extreme that they name: `sample_counts`: the number of real samples of each task; in every draw one task has all 1024. `feature_counts`: the number of real features of each task; in every draw one task has all 8.
All inputs are finite; a program needn't handle non-finite values.
Results may differ from the reference program's by a relative error of at most 0.018.
Values may be sent and summed in bfloat16 or wider, within the bound.
A program may use at most 256 MiB of HBM per device.

```python
import jax
import jax.numpy as jnp
from jax import lax

D = 512
HEADS = 8
HEAD_DIM = 64
FF = 2048
SAMPLES = 1024
FEATURES = 8
TASKS = 4


def ragged_counts(key, full, tasks):
    levels = jax.random.randint(jax.random.fold_in(key, 1), (tasks,), 0, 4)
    ceiling = jnp.maximum(jnp.right_shift(jnp.full((tasks,), full, jnp.int32), levels), 1)
    raw_draw = jax.random.randint(jax.random.fold_in(key, 2), (tasks,), 0, full)
    counts = raw_draw % ceiling + 1
    chosen = jax.random.randint(jax.random.fold_in(key, 3), (), 0, tasks)
    return jnp.where(jnp.arange(tasks) == chosen, full, counts).astype(jnp.int32)


def draw_sample_counts(key, part):
    key = jax.random.fold_in(key, 11)
    return ragged_counts(key, SAMPLES, TASKS)


def draw_feature_counts(key, part):
    key = jax.random.fold_in(key, 23)
    return ragged_counts(key, FEATURES, TASKS)


def block_levels(own_key, shape, split, low, high):
    gain, own = 1.0, jax.random.fold_in(own_key, 6)
    for dim, blocks in split:
        draws = jnp.exp(jax.random.uniform(jax.random.fold_in(own, dim), (blocks,), jnp.float32, low / len(split), high / len(split)))
        gain = gain * jnp.repeat(draws, shape[dim] // blocks).reshape([-1 if axis == dim else 1 for axis in range(len(shape))])
    return gain


def scatter_about(key, dims, scale, reach, pieces=(), kind=jnp.bfloat16):
    values = jax.random.normal(key, dims, jnp.float32) * scale
    if len(pieces) > 0:
        values = block_levels(key, dims, pieces, -0.22, 0.18) * values
    return jnp.clip(values, min=-reach, max=reach).astype(kind)


def setup_inputs(seed: int = 0) -> dict:
    arg_keys = jax.random.split(jax.random.key(seed), 13)
    tokens = scatter_about(arg_keys[0], (TASKS, SAMPLES, FEATURES, D), 1.0, 6.0, ((0, 4), (2, 8)))
    sample_counts = draw_sample_counts(jax.random.fold_in(arg_keys[12], 71), 0)
    feature_counts = draw_feature_counts(jax.random.fold_in(arg_keys[12], 71), 0)
    attn_in = scatter_about(arg_keys[3], (2, D, 3 * D), D ** -0.5, 0.25)
    attn_out = scatter_about(arg_keys[4], (2, D, D), (D // 32) ** -0.5, 1.5)
    norm_gain = jnp.clip(1.0 + 0.1 * jax.random.normal(arg_keys[5], (3, D), jnp.float32), 0.5, 1.5)
    norm_bias = scatter_about(arg_keys[6], (3, D), 0.3, 1.8, (), jnp.float32)
    mlp_in = scatter_about(arg_keys[7], (D, FF), D ** -0.5, 0.25)
    mlp_in_bias = scatter_about(arg_keys[8], (FF,), 0.3, 1.8, (), jnp.float32)
    mlp_out = scatter_about(arg_keys[9], (FF, D), FF ** -0.5, 0.125)
    mlp_out_bias = scatter_about(arg_keys[10], (D,), 0.3, 1.8, (), jnp.float32)
    cotangent = scatter_about(arg_keys[11], (TASKS, SAMPLES, FEATURES, D), 1.0, 6.0, ((0, 4), (2, 8)))
    return dict(tokens=tokens, sample_counts=sample_counts, feature_counts=feature_counts, attn_in=attn_in, attn_out=attn_out, norm_gain=norm_gain, norm_bias=norm_bias, mlp_in=mlp_in, mlp_in_bias=mlp_in_bias, mlp_out=mlp_out, mlp_out_bias=mlp_out_bias, cotangent=cotangent)


@jax.custom_vjp
def low(v):
    return lax.optimization_barrier(v.astype(jnp.bfloat16)).astype(jnp.float32)

@jax.custom_vjp
def low_back(v):
    return v

def low_keep(v):
    return (low(v), None)

def low_pass(kept, grad):
    return (grad,)

def back_keep(v):
    return (v, None)

def back_low(kept, grad):
    return (low(grad),)
low.defvjp(low_keep, low_pass)
low_back.defvjp(back_keep, back_low)
PRECISE = lax.Precision.HIGHEST
EPSILON = 1e-05
MASKED = -1e+30

def matmul(left, right):
    return jnp.dot(left, right, precision=PRECISE)

def layer_norm(values, factor, offset):
    centre = values - lax.optimization_barrier(jnp.mean(values, axis=-1, keepdims=True))
    spread = lax.optimization_barrier(jnp.mean(centre * centre, axis=-1, keepdims=True))
    return centre * lax.rsqrt(spread + EPSILON) * factor + offset

def attend(packed, valid, score_form, out_form):
    leading = packed.shape[:-1]
    query_rows = packed[..., :D].reshape(leading + (HEADS, HEAD_DIM))
    key_rows = packed[..., D:2 * D].reshape(leading + (HEADS, HEAD_DIM))
    value_rows = packed[..., 2 * D:].reshape(leading + (HEADS, HEAD_DIM))
    raw_scores = low_back(jnp.einsum(score_form, query_rows, key_rows, precision=PRECISE) * HEAD_DIM ** (-0.5))
    scores = jnp.where(valid, raw_scores, MASKED)
    probability = low(jax.nn.softmax(scores, axis=-1))
    mixed_rows = jnp.einsum(out_form, probability, value_rows, precision=PRECISE)
    return mixed_rows.reshape(leading + (D,))

def layer_block(task_tokens, task_samples, task_features, weights):
    attn_in, attn_out, norm_gain, norm_bias, mlp_in, mlp_in_bias, mlp_out, mlp_out_bias = weights
    normed_one = low(layer_norm(task_tokens, norm_gain[0], norm_bias[0]))
    packed_one = low_back(low(matmul(normed_one, attn_in[0])))

    def per_feature(sequence):
        return attend(sequence, task_samples, 'qhe,khe->hqk', 'hqk,khe->qhe')
    attn_one = lax.map(jax.checkpoint(per_feature), jnp.transpose(packed_one, (1, 0, 2)))
    attn_one = low_back(low(jnp.transpose(attn_one, (1, 0, 2))))
    first_resid = low_back(low(task_tokens + matmul(attn_one, attn_out[0])))
    normed_two = low(layer_norm(first_resid, norm_gain[1], norm_bias[1]))
    packed_two = low_back(low(matmul(normed_two, attn_in[1])))

    def across_features(packed):
        return attend(packed, task_features, 'sqhe,skhe->shqk', 'shqk,skhe->sqhe')
    attn_two = low_back(low(jax.checkpoint(across_features)(packed_two)))
    second_resid = first_resid + low_back(matmul(attn_two, attn_out[1]))
    normed_three = low(layer_norm(second_resid, norm_gain[2], norm_bias[2]))
    hidden = low_back(matmul(normed_three, mlp_in) + mlp_in_bias)
    active = low(jax.nn.gelu(hidden, approximate=False))
    return second_resid + matmul(active, mlp_out) + mlp_out_bias

def reference(tokens, sample_counts, feature_counts, attn_in, attn_out, norm_gain, norm_bias, mlp_in, mlp_in_bias, mlp_out, mlp_out_bias, cotangent):
    sample_valid = jnp.arange(SAMPLES, dtype=jnp.int32)[None, :] < sample_counts[:, None]
    feature_valid = jnp.arange(FEATURES, dtype=jnp.int32)[None, :] < feature_counts[:, None]
    weights = (attn_in.astype(jnp.float32), attn_out.astype(jnp.float32), norm_gain.astype(jnp.float32), norm_bias.astype(jnp.float32), mlp_in.astype(jnp.float32), mlp_in_bias.astype(jnp.float32), mlp_out.astype(jnp.float32), mlp_out_bias.astype(jnp.float32))
    inputs = tokens.astype(jnp.float32)

    def forward(values, params):

        def per_task(entries):
            return layer_block(entries[0], entries[1], entries[2], params)
        return lax.map(per_task, (values, sample_valid, feature_valid))
    outcome, pullback = jax.vjp(forward, inputs, weights)
    grad_input, grads = pullback(cotangent.astype(jnp.float32))
    return (outcome.astype(jnp.bfloat16), grad_input.astype(jnp.bfloat16), grads[0], grads[1], grads[2], grads[3], grads[4], grads[5], grads[6], grads[7])
```

```python
import jax
import jax.numpy as jnp
from jax import lax
from jax.experimental import pallas as pl
from jax.experimental.pallas import tpu as pltpu
from jax.sharding import PartitionSpec as P

HEADS = 8
HEAD_DIM = 64


EPSILON = 1e-05
MASKED = -1e30
SAMPLE_FORMS = ("tqfhe,tkfhe->tfhqk", "tfhqk,tkfhe->tqfhe", "tfhqk,tqfhe->tkfhe")
FEATURE_FORMS = ("tsqhe,tskhe->tshqk", "tshqk,tskhe->tsqhe", "tshqk,tsqhe->tskhe")


def layer_norm(values, factor, offset):
    centre = values - jnp.mean(values, axis=-1, keepdims=True)
    spread = jnp.mean(centre * centre, axis=-1, keepdims=True)
    return centre * lax.rsqrt(spread + EPSILON) * factor + offset


def exact_gelu(values):
    return jax.nn.gelu(values, approximate=False)


def project(left, weight):
    return jnp.dot(left, weight, preferred_element_type=jnp.float32)


def project_back(grad_rows, weight):
    return jnp.einsum("...c,dc->...d", grad_rows, weight, preferred_element_type=jnp.float32)


def weight_grad(left, grad_rows):
    return jnp.einsum(
        "nd,nc->dc",
        left.reshape(-1, left.shape[-1]),
        grad_rows.reshape(-1, grad_rows.shape[-1]),
        preferred_element_type=jnp.float32,
    )


def split_heads(packed):
    leading = packed.shape[:-1]
    model_width = packed.shape[-1] // 3
    query_rows = packed[..., :model_width].reshape(leading + (HEADS, HEAD_DIM))
    key_rows = packed[..., model_width : 2 * model_width].reshape(leading + (HEADS, HEAD_DIM))
    value_rows = packed[..., 2 * model_width :].reshape(leading + (HEADS, HEAD_DIM))
    return (query_rows, key_rows, value_rows)


def masked_scores(query_rows, key_rows, valid, forms):
    raw_scores = jnp.einsum(
        forms[0], query_rows, key_rows, preferred_element_type=jnp.float32
    ) * HEAD_DIM ** (-0.5)
    return jnp.where(valid[:, None, None, None, :], raw_scores, MASKED)


def attend(packed, valid, forms):
    leading = packed.shape[:-1]
    query_rows, key_rows, value_rows = split_heads(packed)
    scores = masked_scores(query_rows, key_rows, valid, forms)
    row_max = jnp.max(scores, axis=-1, keepdims=True)
    exponent = jnp.exp(scores - row_max)
    row_total = jnp.sum(exponent, axis=-1, keepdims=True)
    probability = (exponent / row_total).astype(jnp.bfloat16)
    mixed_rows = jnp.einsum(forms[1], probability, value_rows, preferred_element_type=jnp.float32)
    return (mixed_rows.reshape(leading + (packed.shape[-1] // 3,)), row_max + jnp.log(row_total))


def attend_back(packed, valid, log_total, grad_out, forms):
    leading = packed.shape[:-1]
    model_width = packed.shape[-1] // 3
    query_rows, key_rows, value_rows = split_heads(packed)
    grad_rows = grad_out.reshape(leading + (HEADS, HEAD_DIM))
    scores = masked_scores(query_rows, key_rows, valid, forms)
    probability = jnp.exp(scores - log_total)
    grad_values = jnp.einsum(
        forms[2], probability.astype(jnp.bfloat16), grad_rows, preferred_element_type=jnp.float32
    )
    grad_probs = jnp.einsum(forms[0], grad_rows, value_rows, preferred_element_type=jnp.float32)
    inner_sum = jnp.sum(probability * grad_probs, axis=-1, keepdims=True)
    grad_scores = (probability * (grad_probs - inner_sum)).astype(jnp.bfloat16)
    grad_query = jnp.einsum(
        forms[1], grad_scores, key_rows, preferred_element_type=jnp.float32
    ) * HEAD_DIM ** (-0.5)
    grad_keys = jnp.einsum(
        forms[2], grad_scores, query_rows, preferred_element_type=jnp.float32
    ) * HEAD_DIM ** (-0.5)
    return jnp.concatenate(
        [
            grad_query.reshape(leading + (model_width,)).astype(jnp.bfloat16),
            grad_keys.reshape(leading + (model_width,)).astype(jnp.bfloat16),
            grad_values.reshape(leading + (model_width,)).astype(jnp.bfloat16),
        ],
        axis=-1,
    )


def local(
    tokens,
    sample_counts,
    feature_counts,
    attn_in,
    attn_out,
    norm_gain,
    norm_bias,
    mlp_in,
    mlp_in_bias,
    mlp_out,
    mlp_out_bias,
    cotangent,
):
    samples = tokens.shape[1]
    sample_valid = jnp.arange(samples, dtype=jnp.int32)[None, :] < sample_counts[:, None]
    inputs = tokens.astype(jnp.float32)
    norm_one, back_one = jax.vjp(layer_norm, inputs, norm_gain[0], norm_bias[0])
    normed_one = norm_one.astype(jnp.bfloat16)
    packed_one = project(normed_one, attn_in[0]).astype(jnp.bfloat16)
    attn_one, log_total_one = attend(packed_one, sample_valid, SAMPLE_FORMS)
    attn_one = attn_one.astype(jnp.bfloat16)
    first_resid = (inputs + project(attn_one, attn_out[0])).astype(jnp.bfloat16)
    moved_rows = lax.all_to_all(first_resid, "swap", split_axis=1, concat_axis=2, tiled=True)
    features = moved_rows.shape[2]
    feature_valid = jnp.arange(features, dtype=jnp.int32)[None, :] < feature_counts[:, None]
    resid_one = moved_rows.astype(jnp.float32)
    norm_two, back_two = jax.vjp(layer_norm, resid_one, norm_gain[1], norm_bias[1])
    normed_two = norm_two.astype(jnp.bfloat16)
    packed_two = project(normed_two, attn_in[1]).astype(jnp.bfloat16)
    attn_two, log_total_two = attend(packed_two, feature_valid, FEATURE_FORMS)
    attn_two = attn_two.astype(jnp.bfloat16)
    resid_two = resid_one + project(attn_two, attn_out[1])
    norm_three, back_three = jax.vjp(layer_norm, resid_two, norm_gain[2], norm_bias[2])
    normed_three = norm_three.astype(jnp.bfloat16)
    hidden = project(normed_three, mlp_in) + mlp_in_bias
    activated, back_gelu = jax.vjp(exact_gelu, hidden)
    active_low = activated.astype(jnp.bfloat16)
    outcome = (resid_two + project(active_low, mlp_out) + mlp_out_bias).astype(jnp.bfloat16)
    mixed_out = lax.all_to_all(outcome, "swap", split_axis=2, concat_axis=1, tiled=True)
    grad_out = lax.all_to_all(cotangent, "swap", split_axis=1, concat_axis=2, tiled=True)
    grad_three = grad_out.astype(jnp.float32)
    grad_mlp_out = weight_grad(active_low, grad_out)
    grad_mlp_out_bias = jnp.sum(grad_three.reshape(-1, grad_three.shape[-1]), axis=0)
    grad_active = project_back(grad_out, mlp_out)
    grad_hidden = back_gelu(grad_active)[0].astype(jnp.bfloat16)
    grad_mlp_in = weight_grad(normed_three, grad_hidden)
    grad_mlp_in_bias = jnp.sum(
        grad_hidden.astype(jnp.float32).reshape(-1, grad_hidden.shape[-1]), axis=0
    )
    grad_resid, gain_three, offset_three = back_three(project_back(grad_hidden, mlp_in))
    grad_second = grad_three + grad_resid
    grad_second_low = grad_second.astype(jnp.bfloat16)
    grad_attn_out_two = weight_grad(attn_two, grad_second_low)
    grad_attn_two = project_back(grad_second_low, attn_out[1]).astype(jnp.bfloat16)
    grad_packed_two = attend_back(
        packed_two, feature_valid, log_total_two, grad_attn_two, FEATURE_FORMS
    )
    grad_attn_in_two = weight_grad(normed_two, grad_packed_two)
    grad_resid_two, gain_two, offset_two = back_two(project_back(grad_packed_two, attn_in[1]))
    grad_first = (grad_second + grad_resid_two).astype(jnp.bfloat16)
    grad_back = lax.all_to_all(grad_first, "swap", split_axis=2, concat_axis=1, tiled=True)
    grad_attn_out_one = weight_grad(attn_one, grad_back)
    grad_attn_one = project_back(grad_back, attn_out[0]).astype(jnp.bfloat16)
    grad_packed_one = attend_back(
        packed_one, sample_valid, log_total_one, grad_attn_one, SAMPLE_FORMS
    )
    grad_attn_in_one = weight_grad(normed_one, grad_packed_one)
    grad_input, gain_one, offset_one = back_one(project_back(grad_packed_one, attn_in[0]))
    tokens_grad = (grad_back.astype(jnp.float32) + grad_input).astype(jnp.bfloat16)
    stack_in = jnp.stack([grad_attn_in_one, grad_attn_in_two])
    stack_out = jnp.stack([grad_attn_out_one, grad_attn_out_two])
    stack_gain = jnp.stack([gain_one, gain_two, gain_three])
    stack_offset = jnp.stack([offset_one, offset_two, offset_three])
    (
        part_in,
        part_out,
        part_gain,
        part_offset,
        part_mlp_in,
        part_mlp_in_bias,
        part_mlp_out,
        part_mlp_out_bias,
    ) = (
        lax.psum_scatter(stack_in, "swap", scatter_dimension=1, tiled=True),
        lax.psum_scatter(stack_out, "swap", scatter_dimension=1, tiled=True),
        lax.psum_scatter(stack_gain, "swap", scatter_dimension=1, tiled=True),
        lax.psum_scatter(stack_offset, "swap", scatter_dimension=1, tiled=True),
        lax.psum_scatter(grad_mlp_in, "swap", scatter_dimension=0, tiled=True),
        lax.psum_scatter(grad_mlp_in_bias, "swap", scatter_dimension=0, tiled=True),
        lax.psum_scatter(grad_mlp_out, "swap", scatter_dimension=0, tiled=True),
        lax.psum_scatter(grad_mlp_out_bias, "swap", scatter_dimension=0, tiled=True),
    )
    (
        share_in,
        share_out,
        share_gain,
        share_offset,
        share_mlp_in,
        share_mlp_in_bias,
        share_mlp_out,
        share_mlp_out_bias,
    ) = (
        lax.psum(part_in.astype(jnp.bfloat16), "grp").astype(jnp.float32),
        lax.psum(part_out.astype(jnp.bfloat16), "grp").astype(jnp.float32),
        lax.psum(part_gain.astype(jnp.bfloat16), "grp").astype(jnp.float32),
        lax.psum(part_offset.astype(jnp.bfloat16), "grp").astype(jnp.float32),
        lax.psum(part_mlp_in.astype(jnp.bfloat16), "grp").astype(jnp.float32),
        lax.psum(part_mlp_in_bias.astype(jnp.bfloat16), "grp").astype(jnp.float32),
        lax.psum(part_mlp_out.astype(jnp.bfloat16), "grp").astype(jnp.float32),
        lax.psum(part_mlp_out_bias.astype(jnp.bfloat16), "grp").astype(jnp.float32),
    )
    return (
        mixed_out,
        tokens_grad,
        share_in,
        share_out,
        share_gain,
        share_offset,
        share_mlp_in,
        share_mlp_in_bias,
        share_mlp_out,
        share_mlp_out_bias,
    )


MESH = pl.DeviceIdType.MESH
VMEM_LIMIT = 60 * 1024 * 1024
SCALE = HEAD_DIM ** (-0.5)
LOG2E = 1.4426950408889634
LN2 = 0.6931471805599453
BF = jnp.bfloat16
F32 = jnp.float32
NT = (((1,), (1,)), ((), ()))
NN = (((1,), (0,)), ((), ()))
TN = (((0,), (0,)), ((), ()))
CHUNKS = 4
BLOCK = 256
SWAP = 8
GRP = 4
PIECE = BLOCK // SWAP
PAIRS = 4
WIDTH = 512
MID_ROWS = 192
END_ROWS = 64


def mm(left, right, form=NN):
    return lax.dot_general(left, right, form, preferred_element_type=F32)


def norm_stats(values):
    centre = values - jnp.mean(values, axis=-1, keepdims=True)
    inverse = lax.rsqrt(jnp.mean(centre * centre, axis=-1, keepdims=True) + EPSILON)
    return centre * inverse, inverse


def norm_back(grad, vhat, inverse, gain):
    scaled = grad * gain
    mean_one = jnp.mean(scaled, axis=-1, keepdims=True)
    mean_two = jnp.mean(scaled * vhat, axis=-1, keepdims=True)
    return inverse * (scaled - mean_one - vhat * mean_two)


def lanes(rows=BLOCK):
    return lax.broadcasted_iota(jnp.int32, (rows, 128), 1)


def split_three(values):
    high = values.astype(BF).astype(F32)
    rest = values - high
    middle = rest.astype(BF).astype(F32)
    low = rest - middle
    place = lanes(values.shape[0]) & 63
    terms = jnp.where(place == 0, high, jnp.where(place == 1, middle, jnp.where(place == 2, low, 0.0)))
    return terms.astype(BF)


def attention_forward(query, key, value, bias, put):
    def score(head):
        raw = mm(query(head // 2), key(head), NT)
        return raw if bias is None else raw + bias

    current = score(0)
    for pair in range(PAIRS):
        total = None
        tops = []
        for half in range(2):
            head = 2 * pair + half
            following = score(head + 1) if head + 1 < HEADS else None
            top = jnp.max(current, axis=-1, keepdims=True)
            weight = jnp.exp2(current - top).astype(BF)
            term = mm(weight, value(head))
            total = term if total is None else total + term
            tops.append(top)
            current = following
        row_total = total[:, 128:]
        out = (total[:, :128] / row_total).astype(BF)
        top_pair = jnp.where(lanes() < 64, tops[0], tops[1])
        put(pair, out, split_three(-(top_pair + jnp.log(row_total) * LOG2E)))


def attention_back(query, grad, key, value, bias):
    left = lanes() < 64
    grad_query = grad_key = grad_value = None
    for half in range(2):
        keys = key(half)
        score = mm(query, keys, NT)
        if bias is not None:
            score = score + bias
        weight = jnp.exp2(score)
        slope = mm(grad, value(half), NT)
        grad_score = (weight * slope).astype(BF)
        weight = weight.astype(BF)
        mine = left if half == 0 else jnp.logical_not(left)
        nothing = jnp.zeros((BLOCK, 128), BF)
        terms = (
            mm(grad_score, keys[:, :128]),
            mm(grad_score, jnp.where(mine, query[:, :128], nothing), TN),
            mm(weight, jnp.where(mine, grad[:, :128], nothing), TN),
        )
        if half == 0:
            grad_query, grad_key, grad_value = terms
        else:
            grad_query, grad_key, grad_value = (
                grad_query + terms[0],
                grad_key + terms[1],
                grad_value + terms[2],
            )
    return grad_query, grad_key, grad_value


def fused_kernel(
    tokens,
    cotangent,
    sample_counts,
    feature_counts,
    attn_in_hbm,
    attn_out_hbm,
    norm_gain,
    norm_bias,
    mlp_in_hbm,
    mlp_in_bias,
    mlp_out_hbm,
    mlp_out_bias,
    mixed,
    tokens_grad,
    mid_out,
    end_out,
    gain_out,
    offset_out,
    hidden_bias_out,
    out_bias_out,
    attn_in,
    attn_out,
    mlp_in,
    mlp_out,
    x_rows,
    normed_one,
    query_one,
    key_one,
    value_one,
    ones_key,
    ones_value,
    attn_one,
    first_send,
    first_recv,
    cot_recv,
    grad_recv,
    normed_two,
    attn_two,
    normed_three,
    active,
    grad_hidden,
    grad_packed,
    grad_low,
    query_two,
    key_two,
    value_two,
    feature_bias,
    key_zero,
    grad_key,
    grad_value,
    head_sum,
    vectors,
    vec_pair,
    vec_grp,
    vec_z,
    mid_part,
    mid_one,
    mid_two,
    mid_three,
    mid_done,
    load_sem,
    first_ss,
    first_rs,
    cot_ss,
    cot_rs,
    mixed_ss,
    mixed_rs,
    grad_ss,
    grad_rs,
    out_sem,
    mid_ss,
    mid_rs,
    end_ss,
    end_rs,
    vec_ss,
    vec_rs,
):
    grp = lax.axis_index("grp")
    me = lax.axis_index("swap")
    chip = me // 2
    core = me % 2
    samples = sample_counts[0]
    features = feature_counts[0]

    def swap_peer(k):
        return (me + k) % SWAP

    def grp_peer(k):
        return (grp + k) % GRP

    def z_peer(k):
        return ((chip + k) % 4) * 2 + core

    loads = [pltpu.make_async_copy(tokens.at[:, c], x_rows.at[c], load_sem.at[c]) for c in range(CHUNKS)]
    for index, (source, target) in enumerate(
        (
            (attn_in_hbm.at[0], attn_in.at[0]),
            (attn_out_hbm.at[0], attn_out.at[0]),
            (attn_in_hbm.at[1], attn_in.at[1]),
            (attn_out_hbm.at[1], attn_out.at[1]),
            (mlp_in_hbm, mlp_in),
            (mlp_out_hbm, mlp_out),
        )
    ):
        loads.append(pltpu.make_async_copy(source, target, load_sem.at[CHUNKS + index]))
    for copy in loads:
        copy.start()

    barrier = pltpu.get_barrier_semaphore()
    for k in range(1, SWAP):
        pl.semaphore_signal(barrier, inc=1, device_id={"swap": swap_peer(k)}, device_id_type=MESH)
    for k in range(1, GRP):
        pl.semaphore_signal(barrier, inc=1, device_id={"grp": grp_peer(k)}, device_id_type=MESH)
    pl.semaphore_wait(barrier, SWAP - 1 + GRP - 1)

    def exchange(source, target, send, recv):
        def copy(c, d, peer):
            return pltpu.make_async_remote_copy(
                src_ref=source(c, d),
                dst_ref=target(c, peer),
                send_sem=send.at[c, d],
                recv_sem=recv.at[c, peer],
                device_id={"swap": d},
                device_id_type=MESH,
            )

        def start(c):
            for k in range(1, SWAP):
                copy(c, swap_peer(k), me).start()

        def wait_send(c):
            for k in range(1, SWAP):
                copy(c, swap_peer(k), me).wait_send()

        def wait_recv(c):
            for k in range(1, SWAP):
                copy(c, swap_peer(k), swap_peer(k)).wait_recv()

        return start, wait_send, wait_recv

    first_start, first_wait_send, first_wait_recv = exchange(
        lambda c, d: first_send.at[c, d], lambda c, d: first_recv.at[c, d], first_ss, first_rs
    )
    cot_start, cot_wait_send, cot_wait_recv = exchange(
        lambda c, d: cotangent.at[d, c], lambda c, d: cot_recv.at[c, d], cot_ss, cot_rs
    )
    mixed_start, mixed_wait_send, mixed_wait_recv = exchange(
        lambda c, d: first_send.at[c, d], lambda c, d: mixed.at[d, c], mixed_ss, mixed_rs
    )
    grad_start, grad_wait_send, grad_wait_recv = exchange(
        lambda c, d: first_recv.at[c, d], lambda c, d: grad_recv.at[c, d], grad_ss, grad_rs
    )

    def own_cot(c):
        return pltpu.make_async_copy(cotangent.at[me, c], cot_recv.at[c, me], cot_rs.at[c, me])

    def own_mixed(c):
        return pltpu.make_async_copy(first_send.at[c, me], mixed.at[me, c], mixed_rs.at[c, me])

    def cot_begin(c):
        own_cot(c).start()
        cot_start(c)

    cot_begin(0)

    vectors[...] = jnp.zeros((16, WIDTH), F32)
    low_half = lax.broadcasted_iota(jnp.int32, (CHUNKS, BLOCK, 128), 2) < 64
    ones_key[0] = jnp.where(low_half, 1.0, 0.0).astype(BF)
    ones_key[1] = jnp.where(low_half, 0.0, 1.0).astype(BF)
    head_sum[...] = jnp.where(
        ((lax.broadcasted_iota(jnp.int32, (256, 128), 0) // 64) & 1)
        == (lax.broadcasted_iota(jnp.int32, (256, 128), 1) // 64),
        1.0,
        0.0,
    ).astype(BF)
    row_cell = lax.broadcasted_iota(jnp.int32, (BLOCK, BLOCK), 0)
    col_cell = lax.broadcasted_iota(jnp.int32, (BLOCK, BLOCK), 1)
    seen = jnp.logical_and((row_cell % PIECE) == (col_cell % PIECE), (col_cell // PIECE) < features)
    feature_bias[...] = jnp.where(seen, 0.0, MASKED).astype(F32)

    def valid_rows(c):
        row = lax.broadcasted_iota(jnp.int32, (BLOCK, 1), 0)
        return (row // PIECE) * (CHUNKS * PIECE) + c * PIECE + row % PIECE < samples

    def half_of(values, half):
        mine = (lanes(values.shape[0]) < 64) == (half == 0)
        return jnp.where(mine, values, jnp.zeros_like(values))

    def add_row(row, values):
        vectors[row : row + 1, :] += jnp.sum(values, axis=0, keepdims=True)

    def block(ref, c):
        return ref[c].reshape(BLOCK, WIDTH)

    loads[CHUNKS].wait()

    @pl.loop(0, CHUNKS)
    def _(c):
        pltpu.make_async_copy(tokens.at[:, c], x_rows.at[c], load_sem.at[c]).wait()
        vhat, _ = norm_stats(block(x_rows, c).astype(F32))
        normed = (vhat * norm_gain[0:1, :] + norm_bias[0:1, :]).astype(BF)
        normed_one[c] = normed
        valid = valid_rows(c)
        queries = mm(normed, attn_in[0, :, :WIDTH]) * (SCALE * LOG2E)
        for pair in range(PAIRS):
            query_one[c, pair, :, :128] = queries[:, 128 * pair : 128 * pair + 128].astype(BF)
        keys = mm(normed, attn_in[0, :, WIDTH : 2 * WIDTH])

        @pl.when(c == 0)
        def _():
            key_zero[...] = keys[0:8, :]

        keys = jnp.where(valid, keys, key_zero[0:1, :]).astype(BF)
        values = mm(normed, attn_in[0, :, 2 * WIDTH :])
        values = jnp.where(valid, values, 0.0).astype(BF)
        for head in range(HEADS):
            pair, half = head // 2, head % 2
            cut = slice(128 * pair, 128 * pair + 128)
            key_one[head, c] = half_of(keys[:, cut], half)
            value_one[head, c] = half_of(values[:, cut], half)
        for half in range(2):
            mine = (lanes() < 64) == (half == 0)
            ones_value[half, c] = jnp.where(jnp.logical_and(mine, valid), 1.0, 0.0).astype(BF)

    cells = CHUNKS * BLOCK

    def key_all(head):
        return key_one[head].reshape(cells, 128)

    def key_wide(head):
        return jnp.concatenate([key_all(head), ones_key[head % 2].reshape(cells, 128)], axis=1)

    def value_wide(head):
        return jnp.concatenate(
            [value_one[head].reshape(cells, 128), ones_value[head % 2].reshape(cells, 128)], axis=1
        )

    loads[CHUNKS + 1].wait()

    @pl.loop(0, CHUNKS)
    def _(c):
        def put(pair, out, extra):
            attn_one[c, :, 128 * pair : 128 * pair + 128] = out
            query_one[c, pair, :, 128:] = extra

        attention_forward(
            lambda pair: query_one[c, pair, :, :128], key_all, value_wide, None, put
        )
        first = block(x_rows, c).astype(F32) + mm(attn_one[c], attn_out[0])
        first_send[c] = first.astype(BF).reshape(SWAP, PIECE, WIDTH)
        first_recv[c, me] = first_send[c, me]
        first_start(c)

        @pl.when(c < CHUNKS - 1)
        def _():
            cot_begin(c + 1)

    for index in range(2, 6):
        loads[CHUNKS + index].wait()

    def delta_of(grad, out):
        product = grad.astype(F32) * out.astype(F32)
        high = product.astype(BF)
        low = (product - high.astype(F32)).astype(BF)
        return split_three(-mm(jnp.concatenate([high, low], axis=1), head_sum[...]))

    @pl.loop(0, CHUNKS)
    def _(c):
        first_wait_recv(c)
        resid_one = block(first_recv, c).astype(F32)
        vhat_two, inverse_two = norm_stats(resid_one)
        normed = (vhat_two * norm_gain[1:2, :] + norm_bias[1:2, :]).astype(BF)
        normed_two[c] = normed
        queries = mm(normed, attn_in[1, :, :WIDTH]) * (SCALE * LOG2E)
        keys = mm(normed, attn_in[1, :, WIDTH : 2 * WIDTH]).astype(BF)
        values = mm(normed, attn_in[1, :, 2 * WIDTH :]).astype(BF)
        for pair in range(PAIRS):
            cut = slice(128 * pair, 128 * pair + 128)
            query_two[pair, :, :128] = queries[:, cut].astype(BF)
            for half in range(2):
                key_two[2 * pair + half, :, :128] = half_of(keys[:, cut], half)
                key_two[2 * pair + half, :, 128:] = ones_key[half, 0]
                value_two[2 * pair + half, :, :128] = half_of(values[:, cut], half)
                value_two[2 * pair + half, :, 128:] = ones_key[half, 0]

        def put(pair, out, extra):
            attn_two[c, :, 128 * pair : 128 * pair + 128] = out
            query_two[pair, :, 128:] = extra

        attention_forward(
            lambda pair: query_two[pair, :, :128],
            lambda head: key_two[head, :, :128],
            lambda head: value_two[head],
            feature_bias[...],
            put,
        )
        second = resid_one + mm(attn_two[c], attn_out[1])
        vhat_three, inverse_three = norm_stats(second)
        normed = (vhat_three * norm_gain[2:3, :] + norm_bias[2:3, :]).astype(BF)
        normed_three[c] = normed
        own_cot(c).wait()
        cot_wait_recv(c)
        cot_low = block(cot_recv, c)
        cot = cot_low.astype(F32)
        add_row(10, cot)
        outcome = second + mlp_out_bias[...]
        grad_normed = jnp.zeros((BLOCK, WIDTH), F32)
        for part in range(4):
            cut = slice(WIDTH * part, WIDTH * part + WIDTH)
            hidden = mm(normed, mlp_in[:, cut]) + mlp_in_bias[:, cut]
            weight_out = mlp_out[part].reshape(WIDTH, WIDTH)
            grad_active = mm(cot_low, weight_out, NT)
            below = 0.5 + 0.5 * lax.erf(hidden * 0.7071067811865476)
            act = (hidden * below).astype(BF)
            density = jnp.exp2(hidden * hidden * (-0.5 * LOG2E)) * 0.3989422804014327
            grad_hid = ((below + hidden * density) * grad_active).astype(BF)
            active[part, c] = act
            grad_hidden[part, c] = grad_hid.reshape(GRP, END_ROWS, WIDTH)
            add_row(6 + part, grad_hid.astype(F32))
            outcome = outcome + mm(act, weight_out)
            grad_normed = grad_normed + mm(grad_hid, mlp_in[:, cut], NT)
        first_wait_send(c)
        first_send[c] = outcome.astype(BF).reshape(SWAP, PIECE, WIDTH)
        add_row(2, grad_normed * vhat_three)
        add_row(5, grad_normed)
        grad_second = cot + norm_back(grad_normed, vhat_three, inverse_three, norm_gain[2:3, :])
        grad_second_low = grad_second.astype(BF)
        grad_low[c] = grad_second_low
        grad_attn = mm(grad_second_low, attn_out[1], NT).astype(BF)
        for pair in range(PAIRS):
            cut = slice(128 * pair, 128 * pair + 128)
            piece = grad_attn[:, cut]
            wide = jnp.concatenate([piece, delta_of(piece, attn_two[c, :, cut])], axis=1)
            grad_q, grad_k, grad_v = attention_back(
                query_two[pair],
                wide,
                lambda half: key_two[2 * pair + half],
                lambda half: value_two[2 * pair + half],
                feature_bias[...],
            )
            grad_packed[c, :, 128 * pair : 128 * pair + 128] = (grad_q * SCALE).astype(BF)
            grad_packed[c, :, WIDTH + 128 * pair : WIDTH + 128 * pair + 128] = (grad_k * LN2).astype(BF)
            grad_packed[c, :, 2 * WIDTH + 128 * pair : 2 * WIDTH + 128 * pair + 128] = grad_v.astype(BF)
        grad_normed = mm(grad_packed[c], attn_in[1], NT)
        add_row(1, grad_normed * vhat_two)
        add_row(4, grad_normed)
        grad_first = grad_second + norm_back(grad_normed, vhat_two, inverse_two, norm_gain[1:2, :])
        first_recv[c] = grad_first.astype(BF).reshape(SWAP, PIECE, WIDTH)
        grad_recv[c, me] = first_recv[c, me]
        grad_start(c)
        own_mixed(c).start()
        mixed_start(c)

    def rows_of(ref):
        return ref[...].reshape(cells, WIDTH)

    def shares(values, rows):
        return values.astype(BF).reshape(4, 2, GRP, rows, WIDTH)

    for part in range(4):
        cut = slice(WIDTH * part, WIDTH * part + WIDTH)
        tile = mm(rows_of(normed_three), grad_hidden[part].reshape(cells, WIDTH), TN)
        mid_part[:, :, :, 16 * part : 16 * part + 16, :] = shares(tile, 16)
        tile = mm(active[part].reshape(cells, WIDTH), rows_of(cot_recv), TN)
        mid_part[part, :, :, 64:128, :] = tile.astype(BF).reshape(2, GRP, 64, WIDTH)
    for part in range(3):
        cut = slice(WIDTH * part, WIDTH * part + WIDTH)
        tile = mm(rows_of(normed_two), grad_packed[:, :, cut].reshape(cells, WIDTH), TN)
        mid_part[:, :, :, 128 + 16 * part : 144 + 16 * part, :] = shares(tile, 16)
    tile = mm(rows_of(attn_two), rows_of(grad_low), TN)
    mid_part[:, :, :, 176:192, :] = shares(tile, 16)

    def reduction(part, one, two, three, done, out, send, recv):
        def remote(source, target, index, where):
            return pltpu.make_async_remote_copy(
                src_ref=source,
                dst_ref=target,
                send_sem=send.at[index],
                recv_sem=recv.at[index],
                device_id=where,
                device_id_type=MESH,
            )

        step_one = [remote(part.at[:, 1 - core], one, 0, {"swap": me + 1 - 2 * core})]
        step_two = [
            remote(one.at[:, grp_peer(k)], two.at[k - 1], k, {"grp": grp_peer(k)}) for k in range(1, GRP)
        ]
        step_three = [
            remote(one.at[(chip + k) % 4, grp], three.at[k - 1], 3 + k, {"swap": z_peer(k)}) for k in range(1, 4)
        ]
        step_four = [remote(done, out.at[grp], 6 + k, {"grp": grp_peer(k)}) for k in range(1, GRP)]
        own = pltpu.make_async_copy(done, out.at[grp], recv.at[10])

        def begin():
            for copy in step_one:
                copy.start()

        def after_one():
            for copy in step_one:
                copy.wait_recv()

            @pl.loop(0, 4)
            def _(a):
                one[a] = (one[a].astype(F32) + part[a, core].astype(F32)).astype(BF)

            for copy in step_two:
                copy.start()

        def after_two():
            for copy in step_two:
                copy.wait_recv()

            @pl.loop(0, 4)
            def _(a):
                total = one[a, grp].astype(F32)
                for k in range(3):
                    total = total + two[k, a].astype(F32)
                one[a, grp] = total.astype(BF)

            for copy in step_three:
                copy.start()

        def after_three():
            for copy in step_three:
                copy.wait_recv()
            total = one[chip, grp].astype(F32)
            for k in range(3):
                total = total + three[k].astype(F32)
            done[...] = total.astype(BF)
            own.start()
            for copy in step_four:
                copy.start()

        def finish():
            own.wait()
            for copy in step_four:
                copy.wait_recv()
            for copy in step_one + step_two + step_three + step_four:
                copy.wait_send()

        return begin, after_one, after_two, after_three, finish

    mid = reduction(mid_part, mid_one, mid_two, mid_three, mid_done, mid_out, mid_ss, mid_rs)
    end = reduction(
        mlp_out,
        grad_hidden.at[0],
        grad_hidden.at[1, 0:3],
        grad_hidden.at[2, 0, 0:3],
        grad_hidden.at[2, 1, 0],
        end_out,
        end_ss,
        end_rs,
    )
    mid[0]()

    @pl.loop(0, CHUNKS)
    def _(c):
        grad_wait_recv(c)
        grad_attn = mm(block(grad_recv, c), attn_out[0], NT).astype(BF)
        for pair in range(PAIRS):
            cut = slice(128 * pair, 128 * pair + 128)
            piece = grad_attn[:, cut]
            active[pair, c, :, :128] = piece
            active[pair, c, :, 128:256] = delta_of(piece, attn_one[c, :, cut])

    tile = mm(rows_of(attn_one), rows_of(grad_recv), TN)
    mlp_out[:, :, :, 0:16, :] = shares(tile, 16)

    for pair in range(PAIRS):
        grad_key[...] = jnp.zeros((cells, 128), F32)
        grad_value[...] = jnp.zeros((cells, 128), F32)

        @pl.loop(0, CHUNKS)
        def _(c):
            grad_q, grad_k, grad_v = attention_back(
                query_one[c, pair],
                active[pair, c, :, :256],
                lambda half: key_wide(2 * pair + half),
                lambda half: value_wide(2 * pair + half),
                None,
            )
            grad_packed[c, :, 128 * pair : 128 * pair + 128] = (grad_q * SCALE).astype(BF)
            grad_key[...] += grad_k
            grad_value[...] += grad_v

        for c in range(CHUNKS):
            rows = slice(BLOCK * c, BLOCK * c + BLOCK)
            grad_packed[c, :, WIDTH + 128 * pair : WIDTH + 128 * pair + 128] = (grad_key[rows, :] * LN2).astype(BF)
            grad_packed[c, :, 2 * WIDTH + 128 * pair : 2 * WIDTH + 128 * pair + 128] = jnp.where(
                valid_rows(c), grad_value[rows, :], 0.0
            ).astype(BF)
        for part in range(3):
            cut = slice(WIDTH * part + 128 * pair, WIDTH * part + 128 * pair + 128)
            tile = mm(rows_of(normed_one), grad_packed[:, :, cut].reshape(cells, 128), TN)
            mlp_out[:, :, :, 16 + 16 * part : 32 + 16 * part, 128 * pair : 128 * pair + 128] = (
                tile.astype(BF).reshape(4, 2, GRP, 16, 128)
            )
        if pair < 3:
            mid[pair + 1]()

    end[0]()

    @pl.loop(0, CHUNKS)
    def _(c):
        grad_normed = mm(grad_packed[c], attn_in[0], NT)
        vhat, inverse = norm_stats(block(x_rows, c).astype(F32))
        add_row(0, grad_normed * vhat)
        add_row(3, grad_normed)
        result = block(grad_recv, c).astype(F32) + norm_back(grad_normed, vhat, inverse, norm_gain[0:1, :])
        normed_one[c] = result.astype(BF)
        pltpu.make_async_copy(
            normed_one.at[c].reshape(SWAP, PIECE, WIDTH), tokens_grad.at[:, c], out_sem.at[c]
        ).start()

    def vec_copy(source, target, index, where):
        return pltpu.make_async_remote_copy(
            src_ref=source,
            dst_ref=target,
            send_sem=vec_ss.at[index],
            recv_sem=vec_rs.at[index],
            device_id=where,
            device_id_type=MESH,
        )

    vec_one = vec_copy(vectors, vec_pair, 0, {"swap": me + 1 - 2 * core})
    vec_two = [vec_copy(vec_grp.at[grp], vec_grp.at[grp], k, {"grp": grp_peer(k)}) for k in range(1, GRP)]
    vec_two_in = [
        vec_copy(vec_grp.at[grp_peer(-k)], vec_grp.at[grp_peer(-k)], k, {"grp": grp_peer(-k)}) for k in range(1, GRP)
    ]
    vec_three = [vec_copy(vec_z.at[chip], vec_z.at[chip], 3 + k, {"swap": z_peer(k)}) for k in range(1, 4)]
    vec_three_in = [
        vec_copy(vec_z.at[(chip - k) % 4], vec_z.at[(chip - k) % 4], 3 + k, {"swap": z_peer(-k)}) for k in range(1, 4)
    ]
    vec_one.start()
    end[1]()
    vec_one.wait_recv()
    vec_grp[grp] = vectors[...] + vec_pair[...]
    for copy in vec_two:
        copy.start()
    end[2]()
    for copy in vec_two_in:
        copy.wait_recv()
    vec_z[chip] = (vec_grp[0] + vec_grp[1]) + (vec_grp[2] + vec_grp[3])
    for copy in vec_three:
        copy.start()
    end[3]()
    for copy in vec_three_in:
        copy.wait_recv()
    whole = (vec_z[0] + vec_z[1]) + (vec_z[2] + vec_z[3])

    def share(rows, width, step):
        result = None
        for index in range(WIDTH // width):
            piece = whole[rows, index * width : index * width + width]
            mine = step == index
            result = jnp.where(mine, piece, 0.0 if result is None else result)
        return result

    gain_out[...] = share(slice(0, 3), 64, me)
    offset_out[...] = share(slice(3, 6), 64, me)
    out_bias_out[...] = share(slice(10, 11), 64, me)
    bias_row = None
    for index in range(4):
        piece = share(slice(6 + index, 7 + index), 256, core)
        bias_row = jnp.where(chip == index, piece, 0.0 if bias_row is None else bias_row)
    hidden_bias_out[...] = bias_row

    mid[4]()
    end[4]()
    vec_one.wait_send()
    for copy in vec_two + vec_three:
        copy.wait_send()

    @pl.loop(0, CHUNKS)
    def _(c):
        own_mixed(c).wait()
        mixed_wait_recv(c)
        mixed_wait_send(c)
        cot_wait_send(c)
        grad_wait_send(c)
        pltpu.make_async_copy(
            normed_one.at[c].reshape(SWAP, PIECE, WIDTH), tokens_grad.at[:, c], out_sem.at[c]
        ).wait()


def fused_local(
    tokens,
    sample_counts,
    feature_counts,
    attn_in,
    attn_out,
    norm_gain,
    norm_bias,
    mlp_in,
    mlp_in_bias,
    mlp_out,
    mlp_out_bias,
    cotangent,
):
    cells = (SWAP, CHUNKS, PIECE, WIDTH)
    blocks = (CHUNKS, SWAP, PIECE, WIDTH)
    rows = (CHUNKS, BLOCK, WIDTH)
    anywhere = pl.BlockSpec(memory_space=pl.ANY)
    scalar = pl.BlockSpec(memory_space=pltpu.SMEM)
    vector = pl.BlockSpec(memory_space=pltpu.VMEM)
    sem = pltpu.SemaphoreType.DMA

    def buffer(*shape, kind=BF):
        return pltpu.VMEM(shape, kind)

    mixed, tokens_grad, mid, end, gain, offset, hidden_bias, out_bias = pl.pallas_call(
        fused_kernel,
        name="layer",
        out_shape=(
            jax.ShapeDtypeStruct(cells, BF),
            jax.ShapeDtypeStruct(cells, BF),
            jax.ShapeDtypeStruct((GRP, MID_ROWS, WIDTH), BF),
            jax.ShapeDtypeStruct((GRP, END_ROWS, WIDTH), BF),
            jax.ShapeDtypeStruct((3, 64), F32),
            jax.ShapeDtypeStruct((3, 64), F32),
            jax.ShapeDtypeStruct((1, 256), F32),
            jax.ShapeDtypeStruct((1, 64), F32),
        ),
        in_specs=[
            anywhere,
            anywhere,
            scalar,
            scalar,
            anywhere,
            anywhere,
            vector,
            vector,
            anywhere,
            vector,
            anywhere,
            vector,
        ],
        out_specs=(anywhere, anywhere, anywhere, anywhere, vector, vector, vector, vector),
        scratch_shapes=[
            buffer(2, WIDTH, 3 * WIDTH),
            buffer(2, WIDTH, WIDTH),
            buffer(WIDTH, 4 * WIDTH),
            buffer(4, 2, GRP, END_ROWS, WIDTH),
            buffer(*blocks),
            buffer(*rows),
            buffer(CHUNKS, PAIRS, BLOCK, 256),
            buffer(HEADS, CHUNKS, BLOCK, 128),
            buffer(HEADS, CHUNKS, BLOCK, 128),
            buffer(2, CHUNKS, BLOCK, 128),
            buffer(2, CHUNKS, BLOCK, 128),
            buffer(*rows),
            buffer(*blocks),
            buffer(*blocks),
            buffer(*blocks),
            buffer(*blocks),
            buffer(*rows),
            buffer(*rows),
            buffer(*rows),
            buffer(4, *rows),
            buffer(4, CHUNKS, GRP, END_ROWS, WIDTH),
            buffer(CHUNKS, BLOCK, 3 * WIDTH),
            buffer(*rows),
            buffer(PAIRS, BLOCK, 256),
            buffer(HEADS, BLOCK, 256),
            buffer(HEADS, BLOCK, 256),
            buffer(BLOCK, BLOCK, kind=F32),
            buffer(8, WIDTH, kind=F32),
            buffer(CHUNKS * BLOCK, 128, kind=F32),
            buffer(CHUNKS * BLOCK, 128, kind=F32),
            buffer(256, 128),
            buffer(16, WIDTH, kind=F32),
            buffer(16, WIDTH, kind=F32),
            buffer(GRP, 16, WIDTH, kind=F32),
            buffer(4, 16, WIDTH, kind=F32),
            buffer(4, 2, GRP, MID_ROWS, WIDTH),
            buffer(4, GRP, MID_ROWS, WIDTH),
            buffer(3, 4, MID_ROWS, WIDTH),
            buffer(3, MID_ROWS, WIDTH),
            buffer(MID_ROWS, WIDTH),
            sem((CHUNKS + 6,)),
        ]
        + [sem((CHUNKS, SWAP))] * 8
        + [sem((CHUNKS,))]
        + [sem((11,))] * 4
        + [sem((7,))] * 2,
        compiler_params=pltpu.CompilerParams(
            collective_id=0, has_side_effects=True, vmem_limit_bytes=VMEM_LIMIT
        ),
    )(
        tokens.reshape(cells),
        cotangent.reshape(cells),
        sample_counts,
        feature_counts,
        attn_in,
        attn_out,
        norm_gain,
        norm_bias,
        mlp_in,
        mlp_in_bias.reshape(1, -1),
        mlp_out.reshape(4, 2, GRP, END_ROWS, WIDTH),
        mlp_out_bias.reshape(1, -1),
    )

    def columns(shares, first, count):
        piece = shares[:, first : first + 16 * count].reshape(GRP, count, 16, WIDTH)
        return jnp.transpose(piece, (0, 2, 1, 3)).reshape(64, count * WIDTH).astype(F32)

    return (
        mixed.reshape(tokens.shape),
        tokens_grad.reshape(tokens.shape),
        jnp.stack([columns(end, 16, 3), columns(mid, 128, 3)]),
        jnp.stack([columns(end, 0, 1), columns(mid, 176, 1)]),
        gain,
        offset,
        columns(mid, 0, 4),
        hidden_bias.reshape(-1),
        mid[:, 64:128].reshape(256, WIDTH).astype(F32),
        out_bias.reshape(-1),
    )


def solution(mesh):
    placed = (
        P("grp", None, "swap", None),
        P("grp"),
        P("grp"),
        P(),
        P(),
        P(),
        P(),
        P(),
        P(),
        P(),
        P(),
        P("grp", None, "swap", None),
    )
    def layer(*args):
        tokens, mlp_in = args[0], args[7]
        fits = (
            (mesh.shape["swap"], mesh.shape["grp"]) == (SWAP, GRP)
            and tokens.shape == (1, CHUNKS * BLOCK, 1, WIDTH)
            and mlp_in.shape == (WIDTH, 4 * WIDTH)
        )
        return fused_local(*args) if fits else local(*args)

    return jax.shard_map(
        layer,
        mesh=mesh,
        in_specs=placed,
        out_specs=(
            P("grp", None, "swap", None),
            P("grp", None, "swap", None),
            P(None, "swap", None),
            P(None, "swap", None),
            P(None, "swap"),
            P(None, "swap"),
            P("swap", None),
            P("swap"),
            P("swap", None),
            P("swap"),
        ),
        check_vma=False,
    )
```

```python
import jax
import jax.numpy as jnp
from jax import lax
from jax.experimental import pallas as pl
from jax.experimental.pallas import tpu as pltpu
from jax.sharding import PartitionSpec as P

HEADS = 8
HEAD_DIM = 64


EPSILON = 1e-05
MASKED = -1e30
SAMPLE_FORMS = ("tqfhe,tkfhe->tfhqk", "tfhqk,tkfhe->tqfhe", "tfhqk,tqfhe->tkfhe")
FEATURE_FORMS = ("tsqhe,tskhe->tshqk", "tshqk,tskhe->tsqhe", "tshqk,tsqhe->tskhe")


def layer_norm(values, factor, offset):
    centre = values - jnp.mean(values, axis=-1, keepdims=True)
    spread = jnp.mean(centre * centre, axis=-1, keepdims=True)
    return centre * lax.rsqrt(spread + EPSILON) * factor + offset


def exact_gelu(values):
    return jax.nn.gelu(values, approximate=False)


def project(left, weight):
    return jnp.dot(left, weight, preferred_element_type=jnp.float32)


def project_back(grad_rows, weight):
    return jnp.einsum("...c,dc->...d", grad_rows, weight, preferred_element_type=jnp.float32)


def weight_grad(left, grad_rows):
    return jnp.einsum(
        "nd,nc->dc",
        left.reshape(-1, left.shape[-1]),
        grad_rows.reshape(-1, grad_rows.shape[-1]),
        preferred_element_type=jnp.float32,
    )


def split_heads(packed):
    leading = packed.shape[:-1]
    model_width = packed.shape[-1] // 3
    query_rows = packed[..., :model_width].reshape(leading + (HEADS, HEAD_DIM))
    key_rows = packed[..., model_width : 2 * model_width].reshape(leading + (HEADS, HEAD_DIM))
    value_rows = packed[..., 2 * model_width :].reshape(leading + (HEADS, HEAD_DIM))
    return (query_rows, key_rows, value_rows)


def masked_scores(query_rows, key_rows, valid, forms):
    raw_scores = jnp.einsum(
        forms[0], query_rows, key_rows, preferred_element_type=jnp.float32
    ) * HEAD_DIM ** (-0.5)
    return jnp.where(valid[:, None, None, None, :], raw_scores, MASKED)


def attend(packed, valid, forms):
    leading = packed.shape[:-1]
    query_rows, key_rows, value_rows = split_heads(packed)
    scores = masked_scores(query_rows, key_rows, valid, forms)
    row_max = jnp.max(scores, axis=-1, keepdims=True)
    exponent = jnp.exp(scores - row_max)
    row_total = jnp.sum(exponent, axis=-1, keepdims=True)
    probability = (exponent / row_total).astype(jnp.bfloat16)
    mixed_rows = jnp.einsum(forms[1], probability, value_rows, preferred_element_type=jnp.float32)
    return (mixed_rows.reshape(leading + (packed.shape[-1] // 3,)), row_max + jnp.log(row_total))


def attend_back(packed, valid, log_total, grad_out, forms):
    leading = packed.shape[:-1]
    model_width = packed.shape[-1] // 3
    query_rows, key_rows, value_rows = split_heads(packed)
    grad_rows = grad_out.reshape(leading + (HEADS, HEAD_DIM))
    scores = masked_scores(query_rows, key_rows, valid, forms)
    probability = jnp.exp(scores - log_total)
    grad_values = jnp.einsum(
        forms[2], probability.astype(jnp.bfloat16), grad_rows, preferred_element_type=jnp.float32
    )
    grad_probs = jnp.einsum(forms[0], grad_rows, value_rows, preferred_element_type=jnp.float32)
    inner_sum = jnp.sum(probability * grad_probs, axis=-1, keepdims=True)
    grad_scores = (probability * (grad_probs - inner_sum)).astype(jnp.bfloat16)
    grad_query = jnp.einsum(
        forms[1], grad_scores, key_rows, preferred_element_type=jnp.float32
    ) * HEAD_DIM ** (-0.5)
    grad_keys = jnp.einsum(
        forms[2], grad_scores, query_rows, preferred_element_type=jnp.float32
    ) * HEAD_DIM ** (-0.5)
    return jnp.concatenate(
        [
            grad_query.reshape(leading + (model_width,)).astype(jnp.bfloat16),
            grad_keys.reshape(leading + (model_width,)).astype(jnp.bfloat16),
            grad_values.reshape(leading + (model_width,)).astype(jnp.bfloat16),
        ],
        axis=-1,
    )


def local(
    tokens,
    sample_counts,
    feature_counts,
    attn_in,
    attn_out,
    norm_gain,
    norm_bias,
    mlp_in,
    mlp_in_bias,
    mlp_out,
    mlp_out_bias,
    cotangent,
):
    samples = tokens.shape[1]
    sample_valid = jnp.arange(samples, dtype=jnp.int32)[None, :] < sample_counts[:, None]
    inputs = tokens.astype(jnp.float32)
    norm_one, back_one = jax.vjp(layer_norm, inputs, norm_gain[0], norm_bias[0])
    normed_one = norm_one.astype(jnp.bfloat16)
    packed_one = project(normed_one, attn_in[0]).astype(jnp.bfloat16)
    attn_one, log_total_one = attend(packed_one, sample_valid, SAMPLE_FORMS)
    attn_one = attn_one.astype(jnp.bfloat16)
    first_resid = (inputs + project(attn_one, attn_out[0])).astype(jnp.bfloat16)
    moved_rows = lax.all_to_all(first_resid, "swap", split_axis=1, concat_axis=2, tiled=True)
    features = moved_rows.shape[2]
    feature_valid = jnp.arange(features, dtype=jnp.int32)[None, :] < feature_counts[:, None]
    resid_one = moved_rows.astype(jnp.float32)
    norm_two, back_two = jax.vjp(layer_norm, resid_one, norm_gain[1], norm_bias[1])
    normed_two = norm_two.astype(jnp.bfloat16)
    packed_two = project(normed_two, attn_in[1]).astype(jnp.bfloat16)
    attn_two, log_total_two = attend(packed_two, feature_valid, FEATURE_FORMS)
    attn_two = attn_two.astype(jnp.bfloat16)
    resid_two = resid_one + project(attn_two, attn_out[1])
    norm_three, back_three = jax.vjp(layer_norm, resid_two, norm_gain[2], norm_bias[2])
    normed_three = norm_three.astype(jnp.bfloat16)
    hidden = project(normed_three, mlp_in) + mlp_in_bias
    activated, back_gelu = jax.vjp(exact_gelu, hidden)
    active_low = activated.astype(jnp.bfloat16)
    outcome = (resid_two + project(active_low, mlp_out) + mlp_out_bias).astype(jnp.bfloat16)
    mixed_out = lax.all_to_all(outcome, "swap", split_axis=2, concat_axis=1, tiled=True)
    grad_out = lax.all_to_all(cotangent, "swap", split_axis=1, concat_axis=2, tiled=True)
    grad_three = grad_out.astype(jnp.float32)
    grad_mlp_out = weight_grad(active_low, grad_out)
    grad_mlp_out_bias = jnp.sum(grad_three.reshape(-1, grad_three.shape[-1]), axis=0)
    grad_active = project_back(grad_out, mlp_out)
    grad_hidden = back_gelu(grad_active)[0].astype(jnp.bfloat16)
    grad_mlp_in = weight_grad(normed_three, grad_hidden)
    grad_mlp_in_bias = jnp.sum(
        grad_hidden.astype(jnp.float32).reshape(-1, grad_hidden.shape[-1]), axis=0
    )
    grad_resid, gain_three, offset_three = back_three(project_back(grad_hidden, mlp_in))
    grad_second = grad_three + grad_resid
    grad_second_low = grad_second.astype(jnp.bfloat16)
    grad_attn_out_two = weight_grad(attn_two, grad_second_low)
    grad_attn_two = project_back(grad_second_low, attn_out[1]).astype(jnp.bfloat16)
    grad_packed_two = attend_back(
        packed_two, feature_valid, log_total_two, grad_attn_two, FEATURE_FORMS
    )
    grad_attn_in_two = weight_grad(normed_two, grad_packed_two)
    grad_resid_two, gain_two, offset_two = back_two(project_back(grad_packed_two, attn_in[1]))
    grad_first = (grad_second + grad_resid_two).astype(jnp.bfloat16)
    grad_back = lax.all_to_all(grad_first, "swap", split_axis=2, concat_axis=1, tiled=True)
    grad_attn_out_one = weight_grad(attn_one, grad_back)
    grad_attn_one = project_back(grad_back, attn_out[0]).astype(jnp.bfloat16)
    grad_packed_one = attend_back(
        packed_one, sample_valid, log_total_one, grad_attn_one, SAMPLE_FORMS
    )
    grad_attn_in_one = weight_grad(normed_one, grad_packed_one)
    grad_input, gain_one, offset_one = back_one(project_back(grad_packed_one, attn_in[0]))
    tokens_grad = (grad_back.astype(jnp.float32) + grad_input).astype(jnp.bfloat16)
    stack_in = jnp.stack([grad_attn_in_one, grad_attn_in_two])
    stack_out = jnp.stack([grad_attn_out_one, grad_attn_out_two])
    stack_gain = jnp.stack([gain_one, gain_two, gain_three])
    stack_offset = jnp.stack([offset_one, offset_two, offset_three])
    (
        part_in,
        part_out,
        part_gain,
        part_offset,
        part_mlp_in,
        part_mlp_in_bias,
        part_mlp_out,
        part_mlp_out_bias,
    ) = (
        lax.psum_scatter(stack_in, "swap", scatter_dimension=1, tiled=True),
        lax.psum_scatter(stack_out, "swap", scatter_dimension=1, tiled=True),
        lax.psum_scatter(stack_gain, "swap", scatter_dimension=1, tiled=True),
        lax.psum_scatter(stack_offset, "swap", scatter_dimension=1, tiled=True),
        lax.psum_scatter(grad_mlp_in, "swap", scatter_dimension=0, tiled=True),
        lax.psum_scatter(grad_mlp_in_bias, "swap", scatter_dimension=0, tiled=True),
        lax.psum_scatter(grad_mlp_out, "swap", scatter_dimension=0, tiled=True),
        lax.psum_scatter(grad_mlp_out_bias, "swap", scatter_dimension=0, tiled=True),
    )
    (
        share_in,
        share_out,
        share_gain,
        share_offset,
        share_mlp_in,
        share_mlp_in_bias,
        share_mlp_out,
        share_mlp_out_bias,
    ) = (
        lax.psum(part_in.astype(jnp.bfloat16), "grp").astype(jnp.float32),
        lax.psum(part_out.astype(jnp.bfloat16), "grp").astype(jnp.float32),
        lax.psum(part_gain.astype(jnp.bfloat16), "grp").astype(jnp.float32),
        lax.psum(part_offset.astype(jnp.bfloat16), "grp").astype(jnp.float32),
        lax.psum(part_mlp_in.astype(jnp.bfloat16), "grp").astype(jnp.float32),
        lax.psum(part_mlp_in_bias.astype(jnp.bfloat16), "grp").astype(jnp.float32),
        lax.psum(part_mlp_out.astype(jnp.bfloat16), "grp").astype(jnp.float32),
        lax.psum(part_mlp_out_bias.astype(jnp.bfloat16), "grp").astype(jnp.float32),
    )
    return (
        mixed_out,
        tokens_grad,
        share_in,
        share_out,
        share_gain,
        share_offset,
        share_mlp_in,
        share_mlp_in_bias,
        share_mlp_out,
        share_mlp_out_bias,
    )


MESH = pl.DeviceIdType.MESH
VMEM_LIMIT = 60 * 1024 * 1024
SCALE = HEAD_DIM ** (-0.5)
LOG2E = 1.4426950408889634
LN2 = 0.6931471805599453
BF = jnp.bfloat16
F32 = jnp.float32
NT = (((1,), (1,)), ((), ()))
NN = (((1,), (0,)), ((), ()))
TN = (((0,), (0,)), ((), ()))
CHUNKS = 4
BLOCK = 256
SWAP = 8
GRP = 4
PIECE = BLOCK // SWAP
PAIRS = 4
WIDTH = 512
SHARE = 64
SUMS = 4


def mm(left, right, form=NN):
    return lax.dot_general(left, right, form, preferred_element_type=F32)


def norm_stats(values):
    centre = values - jnp.mean(values, axis=-1, keepdims=True)
    inverse = lax.rsqrt(jnp.mean(centre * centre, axis=-1, keepdims=True) + EPSILON)
    return centre * inverse, inverse


def norm_back(grad, vhat, inverse, gain):
    scaled = grad * gain
    mean_one = jnp.mean(scaled, axis=-1, keepdims=True)
    mean_two = jnp.mean(scaled * vhat, axis=-1, keepdims=True)
    return inverse * (scaled - mean_one - vhat * mean_two)


def lanes(rows=BLOCK):
    return lax.broadcasted_iota(jnp.int32, (rows, 128), 1)


def split_three(values):
    high = values.astype(BF).astype(F32)
    rest = values - high
    middle = rest.astype(BF).astype(F32)
    low = rest - middle
    place = lanes(values.shape[0]) & 63
    terms = jnp.where(place == 0, high, jnp.where(place == 1, middle, jnp.where(place == 2, low, 0.0)))
    return terms.astype(BF)


def attention_forward(query, key, value, bias, put):
    def score(head):
        raw = mm(query(head // 2), key(head), NT)
        return raw if bias is None else raw + bias

    current = score(0)
    for pair in range(PAIRS):
        total = None
        tops = []
        for half in range(2):
            head = 2 * pair + half
            following = score(head + 1) if head + 1 < HEADS else None
            top = jnp.max(current, axis=-1, keepdims=True)
            weight = jnp.exp2(current - top).astype(BF)
            term = mm(weight, value(head))
            total = term if total is None else total + term
            tops.append(top)
            current = following
        row_total = total[:, 128:]
        out = (total[:, :128] / row_total).astype(BF)
        top_pair = jnp.where(lanes() < 64, tops[0], tops[1])
        put(pair, out, split_three(-(top_pair + jnp.log(row_total) * LOG2E)))


def attention_back(query, grad, key, value, bias):
    left = lanes() < 64
    grad_query = grad_key = grad_value = None
    for half in range(2):
        keys = key(half)
        score = mm(query, keys, NT)
        if bias is not None:
            score = score + bias
        weight = jnp.exp2(score)
        slope = mm(grad, value(half), NT)
        grad_score = (weight * slope).astype(BF)
        weight = weight.astype(BF)
        mine = left if half == 0 else jnp.logical_not(left)
        nothing = jnp.zeros((BLOCK, 128), BF)
        terms = (
            mm(grad_score, keys[:, :128]),
            mm(grad_score, jnp.where(mine, query[:, :128], nothing), TN),
            mm(weight, jnp.where(mine, grad[:, :128], nothing), TN),
        )
        if half == 0:
            grad_query, grad_key, grad_value = terms
        else:
            grad_query, grad_key, grad_value = (
                grad_query + terms[0],
                grad_key + terms[1],
                grad_value + terms[2],
            )
    return grad_query, grad_key, grad_value


def fused_kernel(
    tokens,
    cotangent,
    sample_counts,
    feature_counts,
    attn_in_hbm,
    attn_out_hbm,
    norm_gain_hbm,
    norm_bias_hbm,
    mlp_in_hbm,
    mlp_in_bias_hbm,
    mlp_out_hbm,
    mlp_out_bias_hbm,
    mixed,
    tokens_grad,
    sums,
    small,
    attn_in,
    attn_out,
    norm_gain,
    norm_bias,
    mlp_in,
    mlp_in_bias,
    mlp_out,
    mlp_out_bias,
    x_rows,
    normed_one,
    query_one,
    key_one,
    value_one,
    ones_key,
    ones_value,
    attn_one,
    first_send,
    first_recv,
    cot_recv,
    grad_recv,
    normed_two,
    attn_two,
    normed_three,
    active,
    grad_hidden,
    grad_packed,
    grad_low,
    query_two,
    key_two,
    value_two,
    feature_bias,
    key_zero,
    grad_key,
    grad_value,
    head_sum,
    vectors,
    vec_pair,
    vec_grp,
    vec_z,
    part_sum,
    one_sum,
    two_sum,
    three_sum,
    done_sum,
    load_sem,
    first_ss,
    first_rs,
    cot_ss,
    cot_rs,
    mixed_ss,
    mixed_rs,
    grad_ss,
    grad_rs,
    out_sem,
    sum_ss,
    sum_rs,
    vec_ss,
    vec_rs,
):
    grp = lax.axis_index("grp")
    me = lax.axis_index("swap")
    chip = me // 2
    core = me % 2
    samples = sample_counts[0]
    features = feature_counts[0]

    def swap_peer(k):
        return (me + k) % SWAP

    def grp_peer(k):
        return (grp + k) % GRP

    def z_peer(k):
        return ((chip + k) % 4) * 2 + core

    loads = [pltpu.make_async_copy(tokens.at[:, c], x_rows.at[c], load_sem.at[c]) for c in range(CHUNKS)]
    for index, (source, target) in enumerate(
        (
            (attn_in_hbm.at[0], attn_in.at[0]),
            (attn_out_hbm.at[0], attn_out.at[0]),
            (norm_gain_hbm, norm_gain),
            (norm_bias_hbm, norm_bias),
            (mlp_in_bias_hbm, mlp_in_bias),
            (mlp_out_bias_hbm, mlp_out_bias),
            (attn_in_hbm.at[1], attn_in.at[1]),
            (attn_out_hbm.at[1], attn_out.at[1]),
            (mlp_in_hbm, mlp_in),
            (mlp_out_hbm, mlp_out),
        )
    ):
        loads.append(pltpu.make_async_copy(source, target, load_sem.at[CHUNKS + index]))
    for copy in loads:
        copy.start()

    barrier = pltpu.get_barrier_semaphore()
    for k in range(1, SWAP):
        pl.semaphore_signal(barrier, inc=1, device_id={"swap": swap_peer(k)}, device_id_type=MESH)
    for k in range(1, GRP):
        pl.semaphore_signal(barrier, inc=1, device_id={"grp": grp_peer(k)}, device_id_type=MESH)
    pl.semaphore_wait(barrier, SWAP - 1 + GRP - 1)

    def exchange(source, target, send, recv):
        def copy(c, d, peer):
            return pltpu.make_async_remote_copy(
                src_ref=source(c, d),
                dst_ref=target(c, peer),
                send_sem=send.at[c, d],
                recv_sem=recv.at[c, peer],
                device_id={"swap": d},
                device_id_type=MESH,
            )

        def start(c):
            for k in range(1, SWAP):
                copy(c, swap_peer(k), me).start()

        def wait_send(c):
            for k in range(1, SWAP):
                copy(c, swap_peer(k), me).wait_send()

        def wait_recv(c):
            for k in range(1, SWAP):
                copy(c, swap_peer(k), swap_peer(k)).wait_recv()

        return start, wait_send, wait_recv

    first_start, first_wait_send, first_wait_recv = exchange(
        lambda c, d: first_send.at[c, d], lambda c, d: first_recv.at[c, d], first_ss, first_rs
    )
    cot_start, cot_wait_send, cot_wait_recv = exchange(
        lambda c, d: cotangent.at[d, c], lambda c, d: cot_recv.at[c, d], cot_ss, cot_rs
    )
    mixed_start, mixed_wait_send, mixed_wait_recv = exchange(
        lambda c, d: first_send.at[c, d], lambda c, d: mixed.at[d, c], mixed_ss, mixed_rs
    )
    grad_start, grad_wait_send, grad_wait_recv = exchange(
        lambda c, d: first_recv.at[c, d], lambda c, d: grad_recv.at[c, d], grad_ss, grad_rs
    )

    def own_cot(c):
        return pltpu.make_async_copy(cotangent.at[me, c], cot_recv.at[c, me], cot_rs.at[c, me])

    def own_mixed(c):
        return pltpu.make_async_copy(first_send.at[c, me], mixed.at[me, c], mixed_rs.at[c, me])

    def cot_begin(c):
        own_cot(c).start()
        cot_start(c)

    cot_begin(0)

    vectors[...] = jnp.zeros((16, WIDTH), F32)
    low_half = lax.broadcasted_iota(jnp.int32, (CHUNKS, BLOCK, 128), 2) < 64
    ones_key[0] = jnp.where(low_half, 1.0, 0.0).astype(BF)
    ones_key[1] = jnp.where(low_half, 0.0, 1.0).astype(BF)
    head_sum[...] = jnp.where(
        ((lax.broadcasted_iota(jnp.int32, (256, 128), 0) // 64) & 1)
        == (lax.broadcasted_iota(jnp.int32, (256, 128), 1) // 64),
        1.0,
        0.0,
    ).astype(BF)
    row_cell = lax.broadcasted_iota(jnp.int32, (BLOCK, BLOCK), 0)
    col_cell = lax.broadcasted_iota(jnp.int32, (BLOCK, BLOCK), 1)
    seen = jnp.logical_and((row_cell % PIECE) == (col_cell % PIECE), (col_cell // PIECE) < features)
    feature_bias[...] = jnp.where(seen, 0.0, MASKED).astype(F32)

    def valid_rows(c):
        row = lax.broadcasted_iota(jnp.int32, (BLOCK, 1), 0)
        return (row // PIECE) * (CHUNKS * PIECE) + c * PIECE + row % PIECE < samples

    def half_of(values, half):
        mine = (lanes(values.shape[0]) < 64) == (half == 0)
        return jnp.where(mine, values, jnp.zeros_like(values))

    def add_row(row, values):
        vectors[row : row + 1, :] += jnp.sum(values, axis=0, keepdims=True)

    def block(ref, c):
        return ref[c].reshape(BLOCK, WIDTH)

    for index in (0, 2, 3):
        loads[CHUNKS + index].wait()

    @pl.loop(0, CHUNKS)
    def _(c):
        pltpu.make_async_copy(tokens.at[:, c], x_rows.at[c], load_sem.at[c]).wait()
        vhat, _ = norm_stats(block(x_rows, c).astype(F32))
        normed = (vhat * norm_gain[0:1, :] + norm_bias[0:1, :]).astype(BF)
        normed_one[c] = normed
        valid = valid_rows(c)
        queries = mm(normed, attn_in[0, :, :WIDTH]) * (SCALE * LOG2E)
        for pair in range(PAIRS):
            query_one[c, pair, :, :128] = queries[:, 128 * pair : 128 * pair + 128].astype(BF)
        keys = mm(normed, attn_in[0, :, WIDTH : 2 * WIDTH])

        @pl.when(c == 0)
        def _():
            key_zero[...] = keys[0:8, :]

        keys = jnp.where(valid, keys, key_zero[0:1, :]).astype(BF)
        values = mm(normed, attn_in[0, :, 2 * WIDTH :])
        values = jnp.where(valid, values, 0.0).astype(BF)
        for head in range(HEADS):
            pair, half = head // 2, head % 2
            cut = slice(128 * pair, 128 * pair + 128)
            key_one[head, c] = half_of(keys[:, cut], half)
            value_one[head, c] = half_of(values[:, cut], half)
        for half in range(2):
            mine = (lanes() < 64) == (half == 0)
            ones_value[half, c] = jnp.where(jnp.logical_and(mine, valid), 1.0, 0.0).astype(BF)

    cells = CHUNKS * BLOCK

    def key_all(head):
        return key_one[head].reshape(cells, 128)

    def key_wide(head):
        return jnp.concatenate([key_all(head), ones_key[head % 2].reshape(cells, 128)], axis=1)

    def value_wide(head):
        return jnp.concatenate(
            [value_one[head].reshape(cells, 128), ones_value[head % 2].reshape(cells, 128)], axis=1
        )

    loads[CHUNKS + 1].wait()

    @pl.loop(0, CHUNKS)
    def _(c):
        def put(pair, out, extra):
            attn_one[c, :, 128 * pair : 128 * pair + 128] = out
            query_one[c, pair, :, 128:] = extra

        attention_forward(
            lambda pair: query_one[c, pair, :, :128], key_all, value_wide, None, put
        )
        first = block(x_rows, c).astype(F32) + mm(attn_one[c], attn_out[0])
        first_send[c] = first.astype(BF).reshape(SWAP, PIECE, WIDTH)
        first_recv[c, me] = first_send[c, me]
        first_start(c)

        @pl.when(c < CHUNKS - 1)
        def _():
            cot_begin(c + 1)

    for index in range(4, 10):
        loads[CHUNKS + index].wait()

    def delta_of(grad, out):
        product = grad.astype(F32) * out.astype(F32)
        high = product.astype(BF)
        low = (product - high.astype(F32)).astype(BF)
        return split_three(-mm(jnp.concatenate([high, low], axis=1), head_sum[...]))

    @pl.loop(0, CHUNKS)
    def _(c):
        first_wait_recv(c)
        resid_one = block(first_recv, c).astype(F32)
        vhat_two, inverse_two = norm_stats(resid_one)
        normed = (vhat_two * norm_gain[1:2, :] + norm_bias[1:2, :]).astype(BF)
        normed_two[c] = normed
        queries = mm(normed, attn_in[1, :, :WIDTH]) * (SCALE * LOG2E)
        keys = mm(normed, attn_in[1, :, WIDTH : 2 * WIDTH]).astype(BF)
        values = mm(normed, attn_in[1, :, 2 * WIDTH :]).astype(BF)
        for pair in range(PAIRS):
            cut = slice(128 * pair, 128 * pair + 128)
            query_two[pair, :, :128] = queries[:, cut].astype(BF)
            for half in range(2):
                key_two[2 * pair + half, :, :128] = half_of(keys[:, cut], half)
                key_two[2 * pair + half, :, 128:] = ones_key[half, 0]
                value_two[2 * pair + half, :, :128] = half_of(values[:, cut], half)
                value_two[2 * pair + half, :, 128:] = ones_key[half, 0]

        def put(pair, out, extra):
            attn_two[c, :, 128 * pair : 128 * pair + 128] = out
            query_two[pair, :, 128:] = extra

        attention_forward(
            lambda pair: query_two[pair, :, :128],
            lambda head: key_two[head, :, :128],
            lambda head: value_two[head],
            feature_bias[...],
            put,
        )
        second = resid_one + mm(attn_two[c], attn_out[1])
        vhat_three, inverse_three = norm_stats(second)
        normed = (vhat_three * norm_gain[2:3, :] + norm_bias[2:3, :]).astype(BF)
        normed_three[c] = normed
        own_cot(c).wait()
        cot_wait_recv(c)
        cot_low = block(cot_recv, c)
        cot = cot_low.astype(F32)
        add_row(10, cot)
        outcome = second + mlp_out_bias[...]
        grad_normed = jnp.zeros((BLOCK, WIDTH), F32)
        for part in range(4):
            cut = slice(WIDTH * part, WIDTH * part + WIDTH)
            hidden = mm(normed, mlp_in[:, cut]) + mlp_in_bias[:, cut]
            weight_out = mlp_out[part].reshape(WIDTH, WIDTH)
            grad_active = mm(cot_low, weight_out, NT)
            below = 0.5 + 0.5 * lax.erf(hidden * 0.7071067811865476)
            act = (hidden * below).astype(BF)
            density = jnp.exp2(hidden * hidden * (-0.5 * LOG2E)) * 0.3989422804014327
            grad_hid = ((below + hidden * density) * grad_active).astype(BF)
            active[part, c] = act
            grad_hidden[part, c] = grad_hid.reshape(GRP, SHARE, WIDTH)
            add_row(6 + part, grad_hid.astype(F32))
            outcome = outcome + mm(act, weight_out)
            grad_normed = grad_normed + mm(grad_hid, mlp_in[:, cut], NT)
        first_wait_send(c)
        first_send[c] = outcome.astype(BF).reshape(SWAP, PIECE, WIDTH)
        add_row(2, grad_normed * vhat_three)
        add_row(5, grad_normed)
        grad_second = cot + norm_back(grad_normed, vhat_three, inverse_three, norm_gain[2:3, :])
        grad_second_low = grad_second.astype(BF)
        grad_low[c] = grad_second_low
        grad_attn = mm(grad_second_low, attn_out[1], NT).astype(BF)
        for pair in range(PAIRS):
            cut = slice(128 * pair, 128 * pair + 128)
            piece = grad_attn[:, cut]
            wide = jnp.concatenate([piece, delta_of(piece, attn_two[c, :, cut])], axis=1)
            grad_q, grad_k, grad_v = attention_back(
                query_two[pair],
                wide,
                lambda half: key_two[2 * pair + half],
                lambda half: value_two[2 * pair + half],
                feature_bias[...],
            )
            grad_packed[c, :, 128 * pair : 128 * pair + 128] = (grad_q * SCALE).astype(BF)
            grad_packed[c, :, WIDTH + 128 * pair : WIDTH + 128 * pair + 128] = (grad_k * LN2).astype(BF)
            grad_packed[c, :, 2 * WIDTH + 128 * pair : 2 * WIDTH + 128 * pair + 128] = grad_v.astype(BF)
        grad_normed = mm(grad_packed[c], attn_in[1], NT)
        add_row(1, grad_normed * vhat_two)
        add_row(4, grad_normed)
        grad_first = grad_second + norm_back(grad_normed, vhat_two, inverse_two, norm_gain[1:2, :])
        first_recv[c] = grad_first.astype(BF).reshape(SWAP, PIECE, WIDTH)
        grad_recv[c, me] = first_recv[c, me]
        grad_start(c)
        own_mixed(c).start()

    for c in range(CHUNKS):
        mixed_start(c)

    def rows_of(ref):
        return ref[...].reshape(cells, WIDTH)

    def shares(values):
        return values.astype(BF).reshape(4, 2, GRP, 16, values.shape[1])

    def reduction(number, part, one, two, three, done, cut):
        def remote(source, target, index, where):
            return pltpu.make_async_remote_copy(
                src_ref=source,
                dst_ref=target,
                send_sem=sum_ss.at[number, index],
                recv_sem=sum_rs.at[number, index],
                device_id=where,
                device_id_type=MESH,
            )

        out = sums.at[min(number, SUMS - 1), grp, :, cut]
        step_one = [
            remote(part.at[:, 1 - core, :, :, cut], one.at[:, :, :, cut], 0, {"swap": me + 1 - 2 * core})
        ]
        step_two = [
            remote(one.at[:, grp_peer(k), :, cut], two.at[k - 1, :, :, cut], k, {"grp": grp_peer(k)})
            for k in range(1, GRP)
        ]
        step_three = [
            remote(one.at[(chip + k) % 4, grp, :, cut], three.at[k - 1, :, cut], 3 + k, {"swap": z_peer(k)})
            for k in range(1, 4)
        ]
        step_four = [
            remote(done.at[:, cut], out, 6 + k, {"grp": grp_peer(k)}) for k in range(1, GRP)
        ]
        own = pltpu.make_async_copy(done.at[:, cut], out, sum_rs.at[number, 10])

        def begin():
            for copy in step_one:
                copy.start()

        def after_one():
            for copy in step_one:
                copy.wait_recv()

            @pl.loop(0, 4)
            def _(a):
                total = one[a, :, :, cut].astype(F32) + part[a, core, :, :, cut].astype(F32)
                one[a, :, :, cut] = total.astype(BF)

            for copy in step_two:
                copy.start()

        def after_two():
            for copy in step_two:
                copy.wait_recv()

            @pl.loop(0, 4)
            def _(a):
                total = one[a, grp, :, cut].astype(F32)
                for k in range(3):
                    total = total + two[k, a, :, cut].astype(F32)
                one[a, grp, :, cut] = total.astype(BF)

            for copy in step_three:
                copy.start()

        def after_three():
            for copy in step_three:
                copy.wait_recv()
            total = one[chip, grp, :, cut].astype(F32)
            for k in range(3):
                total = total + three[k, :, cut].astype(F32)
            done[:, cut] = total.astype(BF)
            own.start()
            for copy in step_four:
                copy.start()

        def finish():
            own.wait()
            for copy in step_four:
                copy.wait_recv()
            for copy in step_one + step_two + step_three + step_four:
                copy.wait_send()

        return [begin, after_one, after_two, after_three, finish]

    every = slice(0, WIDTH)
    mid = [
        reduction(
            number,
            part_sum.at[number],
            one_sum.at[number],
            two_sum.at[number],
            three_sum.at[number],
            done_sum.at[number],
            every,
        )
        for number in range(3)
    ]
    end = [
        reduction(
            3 + half,
            mlp_out,
            grad_hidden.at[0],
            grad_hidden.at[1, 0:3],
            grad_hidden.at[2, 0, 0:3],
            grad_hidden.at[2, 1, 0],
            slice(256 * half, 256 * half + 256),
        )
        for half in range(2)
    ]

    for part in range(4):
        tile = mm(rows_of(normed_three), grad_hidden[part].reshape(cells, WIDTH), TN)
        part_sum[0, :, :, :, 16 * part : 16 * part + 16, :] = shares(tile)
    mid[0][0]()
    for part in range(4):
        tile = mm(active[part].reshape(cells, WIDTH), rows_of(cot_recv), TN)
        part_sum[1, part] = tile.astype(BF).reshape(2, GRP, SHARE, WIDTH)
    mid[1][0]()
    mid[0][1]()
    for part in range(3):
        cut = slice(WIDTH * part, WIDTH * part + WIDTH)
        tile = mm(rows_of(normed_two), grad_packed[:, :, cut].reshape(cells, WIDTH), TN)
        part_sum[2, :, :, :, 16 * part : 16 * part + 16, :] = shares(tile)
    tile = mm(rows_of(attn_two), rows_of(grad_low), TN)
    part_sum[2, :, :, :, 48:64, :] = shares(tile)
    mid[2][0]()
    mid[1][1]()

    def run(hooks, c):
        for when, call in hooks:

            @pl.when(c == when)
            def _():
                call()

    hooks = (
        ((0, mid[2][1]), (3, mid[0][2])),
        ((0, mid[1][2]), (1, end[0][1]), (2, mid[0][3]), (3, mid[2][2])),
        ((0, end[0][2]), (1, mid[1][3]), (2, end[1][1])),
    )
    for half in range(2):
        pairs = (2 * half, 2 * half + 1)
        grad_key[...] = jnp.zeros((2, cells, 128), F32)
        grad_value[...] = jnp.zeros((2, cells, 128), F32)

        @pl.loop(0, CHUNKS)
        def _(c):
            if half == 0:
                grad_wait_recv(c)
                grad_attn = mm(block(grad_recv, c), attn_out[0], NT).astype(BF)
                for pair in range(PAIRS):
                    cut = slice(128 * pair, 128 * pair + 128)
                    piece = grad_attn[:, cut]
                    active[pair, c, :, :128] = piece
                    active[pair, c, :, 128:256] = delta_of(piece, attn_one[c, :, cut])
            for pair in pairs:
                grad_q, grad_k, grad_v = attention_back(
                    query_one[c, pair],
                    active[pair, c, :, :256],
                    lambda side: key_wide(2 * pair + side),
                    lambda side: value_wide(2 * pair + side),
                    None,
                )
                grad_packed[c, :, 128 * pair : 128 * pair + 128] = (grad_q * SCALE).astype(BF)
                grad_key[pair % 2] += grad_k
                grad_value[pair % 2] += grad_v
            run(hooks[half], c)

        for pair in pairs:
            for c in range(CHUNKS):
                rows = slice(BLOCK * c, BLOCK * c + BLOCK)
                grad_packed[c, :, WIDTH + 128 * pair : WIDTH + 128 * pair + 128] = (
                    grad_key[pair % 2, rows, :] * LN2
                ).astype(BF)
                grad_packed[c, :, 2 * WIDTH + 128 * pair : 2 * WIDTH + 128 * pair + 128] = jnp.where(
                    valid_rows(c), grad_value[pair % 2, rows, :], 0.0
                ).astype(BF)
        if half == 0:
            tile = mm(rows_of(attn_one), rows_of(grad_recv), TN)
            mlp_out[:, :, :, 0:16, :] = shares(tile)
        for part in range(3):
            cut = slice(WIDTH * part + 256 * half, WIDTH * part + 256 * half + 256)
            tile = mm(rows_of(normed_one), grad_packed[:, :, cut].reshape(cells, 256), TN)
            mlp_out[:, :, :, 16 + 16 * part : 32 + 16 * part, 256 * half : 256 * half + 256] = shares(tile)
        end[half][0]()

    @pl.loop(0, CHUNKS)
    def _(c):
        grad_normed = mm(grad_packed[c], attn_in[0], NT)
        vhat, inverse = norm_stats(block(x_rows, c).astype(F32))
        add_row(0, grad_normed * vhat)
        add_row(3, grad_normed)
        result = block(grad_recv, c).astype(F32) + norm_back(grad_normed, vhat, inverse, norm_gain[0:1, :])
        normed_one[c] = result.astype(BF)
        pltpu.make_async_copy(
            normed_one.at[c].reshape(SWAP, PIECE, WIDTH), tokens_grad.at[:, c], out_sem.at[c]
        ).start()
        run(hooks[2], c)

    def vec_copy(source, target, index, where):
        return pltpu.make_async_remote_copy(
            src_ref=source,
            dst_ref=target,
            send_sem=vec_ss.at[index],
            recv_sem=vec_rs.at[index],
            device_id=where,
            device_id_type=MESH,
        )

    vec_one = vec_copy(vectors, vec_pair, 0, {"swap": me + 1 - 2 * core})
    vec_two = [vec_copy(vec_grp.at[grp], vec_grp.at[grp], k, {"grp": grp_peer(k)}) for k in range(1, GRP)]
    vec_two_in = [
        vec_copy(vec_grp.at[grp_peer(-k)], vec_grp.at[grp_peer(-k)], k, {"grp": grp_peer(-k)}) for k in range(1, GRP)
    ]
    vec_three = [vec_copy(vec_z.at[chip], vec_z.at[chip], 3 + k, {"swap": z_peer(k)}) for k in range(1, 4)]
    vec_three_in = [
        vec_copy(vec_z.at[(chip - k) % 4], vec_z.at[(chip - k) % 4], 3 + k, {"swap": z_peer(-k)}) for k in range(1, 4)
    ]
    vec_one.start()
    end[0][3]()
    vec_one.wait_recv()
    vec_grp[grp] = vectors[...] + vec_pair[...]
    for copy in vec_two:
        copy.start()
    end[1][2]()
    for copy in vec_two_in:
        copy.wait_recv()
    vec_z[chip] = (vec_grp[0] + vec_grp[1]) + (vec_grp[2] + vec_grp[3])
    for copy in vec_three:
        copy.start()
    mid[2][3]()
    end[1][3]()
    for copy in vec_three_in:
        copy.wait_recv()
    whole = (vec_z[0] + vec_z[1]) + (vec_z[2] + vec_z[3])

    def share(rows, width, step):
        result = None
        for index in range(WIDTH // width):
            piece = whole[rows, index * width : index * width + width]
            mine = step == index
            result = jnp.where(mine, piece, 0.0 if result is None else result)
        return result

    small[0:3, 0:64] = share(slice(0, 3), 64, me)
    small[3:6, 0:64] = share(slice(3, 6), 64, me)
    bias_row = None
    for index in range(4):
        piece = share(slice(6 + index, 7 + index), 256, core)
        bias_row = jnp.where(chip == index, piece, 0.0 if bias_row is None else bias_row)
    small[6:7, :] = bias_row
    small[7:8, 0:64] = share(slice(10, 11), 64, me)

    for steps in mid + end:
        steps[4]()
    vec_one.wait_send()
    for copy in vec_two + vec_three:
        copy.wait_send()

    @pl.loop(0, CHUNKS)
    def _(c):
        own_mixed(c).wait()
        mixed_wait_recv(c)
        mixed_wait_send(c)
        cot_wait_send(c)
        grad_wait_send(c)
        pltpu.make_async_copy(
            normed_one.at[c].reshape(SWAP, PIECE, WIDTH), tokens_grad.at[:, c], out_sem.at[c]
        ).wait()


def finish_kernel(mixed, tokens_grad, sums, small, *refs):
    outs, row_sem = refs[:10], refs[10]
    copies = [
        pltpu.make_async_copy(mixed, outs[0], row_sem.at[0]),
        pltpu.make_async_copy(tokens_grad, outs[1], row_sem.at[1]),
    ]
    for copy in copies:
        copy.start()
    for grp in range(GRP):
        rows = slice(16 * grp, 16 * grp + 16)
        for part in range(4):
            cut = slice(WIDTH * part, WIDTH * part + WIDTH)
            piece = slice(16 * part, 16 * part + 16)
            outs[6][rows, cut] = sums[0, grp, piece].astype(F32)
            if part < 3:
                outs[2][1, rows, cut] = sums[2, grp, piece].astype(F32)
                outs[2][0, rows, cut] = sums[3, grp, 16 * part + 16 : 16 * part + 32].astype(F32)
        outs[8][SHARE * grp : SHARE * grp + SHARE] = sums[1, grp].astype(F32)
        outs[3][1, rows] = sums[2, grp, 48:64].astype(F32)
        outs[3][0, rows] = sums[3, grp, 0:16].astype(F32)
    outs[4][...] = small[0:3, 0:64]
    outs[5][...] = small[3:6, 0:64]
    outs[7][...] = small[6:7, 0:256]
    outs[9][...] = small[7:8, 0:64]
    for copy in copies:
        copy.wait()


def fused_local(
    tokens,
    sample_counts,
    feature_counts,
    attn_in,
    attn_out,
    norm_gain,
    norm_bias,
    mlp_in,
    mlp_in_bias,
    mlp_out,
    mlp_out_bias,
    cotangent,
):
    cells = (SWAP, CHUNKS, PIECE, WIDTH)
    blocks = (CHUNKS, SWAP, PIECE, WIDTH)
    rows = (CHUNKS, BLOCK, WIDTH)
    anywhere = pl.BlockSpec(memory_space=pl.ANY)
    scalar = pl.BlockSpec(memory_space=pltpu.SMEM)
    vector = pl.BlockSpec(memory_space=pltpu.VMEM)
    sem = pltpu.SemaphoreType.DMA

    def buffer(*shape, kind=BF):
        return pltpu.VMEM(shape, kind)

    def result(shape, kind=F32):
        return jax.ShapeDtypeStruct(shape, kind)

    mixed, tokens_grad, sums, small = pl.pallas_call(
        fused_kernel,
        name="layer",
        out_shape=(
            result(cells, BF),
            result(cells, BF),
            result((SUMS, GRP, SHARE, WIDTH), BF),
            result((8, 256)),
        ),
        in_specs=[anywhere, anywhere, scalar, scalar] + [anywhere] * 8,
        out_specs=(anywhere, anywhere, anywhere, vector),
        scratch_shapes=[
            buffer(2, WIDTH, 3 * WIDTH),
            buffer(2, WIDTH, WIDTH),
            buffer(3, WIDTH, kind=F32),
            buffer(3, WIDTH, kind=F32),
            buffer(WIDTH, 4 * WIDTH),
            buffer(1, 4 * WIDTH, kind=F32),
            buffer(4, 2, GRP, SHARE, WIDTH),
            buffer(1, WIDTH, kind=F32),
            buffer(*blocks),
            buffer(*rows),
            buffer(CHUNKS, PAIRS, BLOCK, 256),
            buffer(HEADS, CHUNKS, BLOCK, 128),
            buffer(HEADS, CHUNKS, BLOCK, 128),
            buffer(2, CHUNKS, BLOCK, 128),
            buffer(2, CHUNKS, BLOCK, 128),
            buffer(*rows),
            buffer(*blocks),
            buffer(*blocks),
            buffer(*blocks),
            buffer(*blocks),
            buffer(*rows),
            buffer(*rows),
            buffer(*rows),
            buffer(4, *rows),
            buffer(4, CHUNKS, GRP, SHARE, WIDTH),
            buffer(CHUNKS, BLOCK, 3 * WIDTH),
            buffer(*rows),
            buffer(PAIRS, BLOCK, 256),
            buffer(HEADS, BLOCK, 256),
            buffer(HEADS, BLOCK, 256),
            buffer(BLOCK, BLOCK, kind=F32),
            buffer(8, WIDTH, kind=F32),
            buffer(2, CHUNKS * BLOCK, 128, kind=F32),
            buffer(2, CHUNKS * BLOCK, 128, kind=F32),
            buffer(256, 128),
            buffer(16, WIDTH, kind=F32),
            buffer(16, WIDTH, kind=F32),
            buffer(GRP, 16, WIDTH, kind=F32),
            buffer(4, 16, WIDTH, kind=F32),
            buffer(3, 4, 2, GRP, SHARE, WIDTH),
            buffer(3, 4, GRP, SHARE, WIDTH),
            buffer(3, 3, 4, SHARE, WIDTH),
            buffer(3, 3, SHARE, WIDTH),
            buffer(3, SHARE, WIDTH),
            sem((CHUNKS + 10,)),
        ]
        + [sem((CHUNKS, SWAP))] * 8
        + [sem((CHUNKS,))]
        + [sem((5, 11))] * 2
        + [sem((7,))] * 2,
        compiler_params=pltpu.CompilerParams(
            collective_id=0, has_side_effects=True, vmem_limit_bytes=VMEM_LIMIT
        ),
    )(
        tokens.reshape(cells),
        cotangent.reshape(cells),
        sample_counts,
        feature_counts,
        attn_in,
        attn_out,
        norm_gain,
        norm_bias,
        mlp_in,
        mlp_in_bias.reshape(1, -1),
        mlp_out.reshape(4, 2, GRP, SHARE, WIDTH),
        mlp_out_bias.reshape(1, -1),
    )
    shapes = (
        result(cells, BF),
        result(cells, BF),
        result((2, 64, 3 * WIDTH)),
        result((2, 64, WIDTH)),
        result((3, 64)),
        result((3, 64)),
        result((64, 4 * WIDTH)),
        result((1, 256)),
        result((256, WIDTH)),
        result((1, 64)),
    )
    outs = pl.pallas_call(
        finish_kernel,
        name="results",
        out_shape=shapes,
        in_specs=[anywhere, anywhere, vector, vector],
        out_specs=(anywhere, anywhere) + (vector,) * 8,
        scratch_shapes=[sem((2,))],
        compiler_params=pltpu.CompilerParams(vmem_limit_bytes=16 * 1024 * 1024),
    )(mixed, tokens_grad, sums, small)
    return (
        outs[0].reshape(tokens.shape),
        outs[1].reshape(tokens.shape),
        *outs[2:7],
        outs[7].reshape(-1),
        outs[8],
        outs[9].reshape(-1),
    )


def solution(mesh):
    placed = (
        P("grp", None, "swap", None),
        P("grp"),
        P("grp"),
        P(),
        P(),
        P(),
        P(),
        P(),
        P(),
        P(),
        P(),
        P("grp", None, "swap", None),
    )
    def layer(*args):
        tokens, mlp_in = args[0], args[7]
        fits = (
            (mesh.shape["swap"], mesh.shape["grp"]) == (SWAP, GRP)
            and tokens.shape == (1, CHUNKS * BLOCK, 1, WIDTH)
            and mlp_in.shape == (WIDTH, 4 * WIDTH)
        )
        return fused_local(*args) if fits else local(*args)

    return jax.shard_map(
        layer,
        mesh=mesh,
        in_specs=placed,
        out_specs=(
            P("grp", None, "swap", None),
            P("grp", None, "swap", None),
            P(None, "swap", None),
            P(None, "swap", None),
            P(None, "swap"),
            P(None, "swap"),
            P("swap", None),
            P("swap"),
            P("swap", None),
            P("swap"),
        ),
        check_vma=False,
    )
```

```python
import jax
import jax.numpy as jnp
from jax import lax
from jax.experimental import pallas as pl
from jax.experimental.pallas import tpu as pltpu
from jax.sharding import PartitionSpec as P

HEADS = 8
HEAD_DIM = 64


EPSILON = 1e-05
MASKED = -1e30
SAMPLE_FORMS = ("tqfhe,tkfhe->tfhqk", "tfhqk,tkfhe->tqfhe", "tfhqk,tqfhe->tkfhe")
FEATURE_FORMS = ("tsqhe,tskhe->tshqk", "tshqk,tskhe->tsqhe", "tshqk,tsqhe->tskhe")


def layer_norm(values, factor, offset):
    centre = values - jnp.mean(values, axis=-1, keepdims=True)
    spread = jnp.mean(centre * centre, axis=-1, keepdims=True)
    return centre * lax.rsqrt(spread + EPSILON) * factor + offset


def exact_gelu(values):
    return jax.nn.gelu(values, approximate=False)


def project(left, weight):
    return jnp.dot(left, weight, preferred_element_type=jnp.float32)


def project_back(grad_rows, weight):
    return jnp.einsum("...c,dc->...d", grad_rows, weight, preferred_element_type=jnp.float32)


def weight_grad(left, grad_rows):
    return jnp.einsum(
        "nd,nc->dc",
        left.reshape(-1, left.shape[-1]),
        grad_rows.reshape(-1, grad_rows.shape[-1]),
        preferred_element_type=jnp.float32,
    )


def split_heads(packed):
    leading = packed.shape[:-1]
    model_width = packed.shape[-1] // 3
    query_rows = packed[..., :model_width].reshape(leading + (HEADS, HEAD_DIM))
    key_rows = packed[..., model_width : 2 * model_width].reshape(leading + (HEADS, HEAD_DIM))
    value_rows = packed[..., 2 * model_width :].reshape(leading + (HEADS, HEAD_DIM))
    return (query_rows, key_rows, value_rows)


def masked_scores(query_rows, key_rows, valid, forms):
    raw_scores = jnp.einsum(
        forms[0], query_rows, key_rows, preferred_element_type=jnp.float32
    ) * HEAD_DIM ** (-0.5)
    return jnp.where(valid[:, None, None, None, :], raw_scores, MASKED)


def attend(packed, valid, forms):
    leading = packed.shape[:-1]
    query_rows, key_rows, value_rows = split_heads(packed)
    scores = masked_scores(query_rows, key_rows, valid, forms)
    row_max = jnp.max(scores, axis=-1, keepdims=True)
    exponent = jnp.exp(scores - row_max)
    row_total = jnp.sum(exponent, axis=-1, keepdims=True)
    probability = (exponent / row_total).astype(jnp.bfloat16)
    mixed_rows = jnp.einsum(forms[1], probability, value_rows, preferred_element_type=jnp.float32)
    return (mixed_rows.reshape(leading + (packed.shape[-1] // 3,)), row_max + jnp.log(row_total))


def attend_back(packed, valid, log_total, grad_out, forms):
    leading = packed.shape[:-1]
    model_width = packed.shape[-1] // 3
    query_rows, key_rows, value_rows = split_heads(packed)
    grad_rows = grad_out.reshape(leading + (HEADS, HEAD_DIM))
    scores = masked_scores(query_rows, key_rows, valid, forms)
    probability = jnp.exp(scores - log_total)
    grad_values = jnp.einsum(
        forms[2], probability.astype(jnp.bfloat16), grad_rows, preferred_element_type=jnp.float32
    )
    grad_probs = jnp.einsum(forms[0], grad_rows, value_rows, preferred_element_type=jnp.float32)
    inner_sum = jnp.sum(probability * grad_probs, axis=-1, keepdims=True)
    grad_scores = (probability * (grad_probs - inner_sum)).astype(jnp.bfloat16)
    grad_query = jnp.einsum(
        forms[1], grad_scores, key_rows, preferred_element_type=jnp.float32
    ) * HEAD_DIM ** (-0.5)
    grad_keys = jnp.einsum(
        forms[2], grad_scores, query_rows, preferred_element_type=jnp.float32
    ) * HEAD_DIM ** (-0.5)
    return jnp.concatenate(
        [
            grad_query.reshape(leading + (model_width,)).astype(jnp.bfloat16),
            grad_keys.reshape(leading + (model_width,)).astype(jnp.bfloat16),
            grad_values.reshape(leading + (model_width,)).astype(jnp.bfloat16),
        ],
        axis=-1,
    )


def local(
    tokens,
    sample_counts,
    feature_counts,
    attn_in,
    attn_out,
    norm_gain,
    norm_bias,
    mlp_in,
    mlp_in_bias,
    mlp_out,
    mlp_out_bias,
    cotangent,
):
    samples = tokens.shape[1]
    sample_valid = jnp.arange(samples, dtype=jnp.int32)[None, :] < sample_counts[:, None]
    inputs = tokens.astype(jnp.float32)
    norm_one, back_one = jax.vjp(layer_norm, inputs, norm_gain[0], norm_bias[0])
    normed_one = norm_one.astype(jnp.bfloat16)
    packed_one = project(normed_one, attn_in[0]).astype(jnp.bfloat16)
    attn_one, log_total_one = attend(packed_one, sample_valid, SAMPLE_FORMS)
    attn_one = attn_one.astype(jnp.bfloat16)
    first_resid = (inputs + project(attn_one, attn_out[0])).astype(jnp.bfloat16)
    moved_rows = lax.all_to_all(first_resid, "swap", split_axis=1, concat_axis=2, tiled=True)
    features = moved_rows.shape[2]
    feature_valid = jnp.arange(features, dtype=jnp.int32)[None, :] < feature_counts[:, None]
    resid_one = moved_rows.astype(jnp.float32)
    norm_two, back_two = jax.vjp(layer_norm, resid_one, norm_gain[1], norm_bias[1])
    normed_two = norm_two.astype(jnp.bfloat16)
    packed_two = project(normed_two, attn_in[1]).astype(jnp.bfloat16)
    attn_two, log_total_two = attend(packed_two, feature_valid, FEATURE_FORMS)
    attn_two = attn_two.astype(jnp.bfloat16)
    resid_two = resid_one + project(attn_two, attn_out[1])
    norm_three, back_three = jax.vjp(layer_norm, resid_two, norm_gain[2], norm_bias[2])
    normed_three = norm_three.astype(jnp.bfloat16)
    hidden = project(normed_three, mlp_in) + mlp_in_bias
    activated, back_gelu = jax.vjp(exact_gelu, hidden)
    active_low = activated.astype(jnp.bfloat16)
    outcome = (resid_two + project(active_low, mlp_out) + mlp_out_bias).astype(jnp.bfloat16)
    mixed_out = lax.all_to_all(outcome, "swap", split_axis=2, concat_axis=1, tiled=True)
    grad_out = lax.all_to_all(cotangent, "swap", split_axis=1, concat_axis=2, tiled=True)
    grad_three = grad_out.astype(jnp.float32)
    grad_mlp_out = weight_grad(active_low, grad_out)
    grad_mlp_out_bias = jnp.sum(grad_three.reshape(-1, grad_three.shape[-1]), axis=0)
    grad_active = project_back(grad_out, mlp_out)
    grad_hidden = back_gelu(grad_active)[0].astype(jnp.bfloat16)
    grad_mlp_in = weight_grad(normed_three, grad_hidden)
    grad_mlp_in_bias = jnp.sum(
        grad_hidden.astype(jnp.float32).reshape(-1, grad_hidden.shape[-1]), axis=0
    )
    grad_resid, gain_three, offset_three = back_three(project_back(grad_hidden, mlp_in))
    grad_second = grad_three + grad_resid
    grad_second_low = grad_second.astype(jnp.bfloat16)
    grad_attn_out_two = weight_grad(attn_two, grad_second_low)
    grad_attn_two = project_back(grad_second_low, attn_out[1]).astype(jnp.bfloat16)
    grad_packed_two = attend_back(
        packed_two, feature_valid, log_total_two, grad_attn_two, FEATURE_FORMS
    )
    grad_attn_in_two = weight_grad(normed_two, grad_packed_two)
    grad_resid_two, gain_two, offset_two = back_two(project_back(grad_packed_two, attn_in[1]))
    grad_first = (grad_second + grad_resid_two).astype(jnp.bfloat16)
    grad_back = lax.all_to_all(grad_first, "swap", split_axis=2, concat_axis=1, tiled=True)
    grad_attn_out_one = weight_grad(attn_one, grad_back)
    grad_attn_one = project_back(grad_back, attn_out[0]).astype(jnp.bfloat16)
    grad_packed_one = attend_back(
        packed_one, sample_valid, log_total_one, grad_attn_one, SAMPLE_FORMS
    )
    grad_attn_in_one = weight_grad(normed_one, grad_packed_one)
    grad_input, gain_one, offset_one = back_one(project_back(grad_packed_one, attn_in[0]))
    tokens_grad = (grad_back.astype(jnp.float32) + grad_input).astype(jnp.bfloat16)
    stack_in = jnp.stack([grad_attn_in_one, grad_attn_in_two])
    stack_out = jnp.stack([grad_attn_out_one, grad_attn_out_two])
    stack_gain = jnp.stack([gain_one, gain_two, gain_three])
    stack_offset = jnp.stack([offset_one, offset_two, offset_three])
    (
        part_in,
        part_out,
        part_gain,
        part_offset,
        part_mlp_in,
        part_mlp_in_bias,
        part_mlp_out,
        part_mlp_out_bias,
    ) = (
        lax.psum_scatter(stack_in, "swap", scatter_dimension=1, tiled=True),
        lax.psum_scatter(stack_out, "swap", scatter_dimension=1, tiled=True),
        lax.psum_scatter(stack_gain, "swap", scatter_dimension=1, tiled=True),
        lax.psum_scatter(stack_offset, "swap", scatter_dimension=1, tiled=True),
        lax.psum_scatter(grad_mlp_in, "swap", scatter_dimension=0, tiled=True),
        lax.psum_scatter(grad_mlp_in_bias, "swap", scatter_dimension=0, tiled=True),
        lax.psum_scatter(grad_mlp_out, "swap", scatter_dimension=0, tiled=True),
        lax.psum_scatter(grad_mlp_out_bias, "swap", scatter_dimension=0, tiled=True),
    )
    (
        share_in,
        share_out,
        share_gain,
        share_offset,
        share_mlp_in,
        share_mlp_in_bias,
        share_mlp_out,
        share_mlp_out_bias,
    ) = (
        lax.psum(part_in.astype(jnp.bfloat16), "grp").astype(jnp.float32),
        lax.psum(part_out.astype(jnp.bfloat16), "grp").astype(jnp.float32),
        lax.psum(part_gain.astype(jnp.bfloat16), "grp").astype(jnp.float32),
        lax.psum(part_offset.astype(jnp.bfloat16), "grp").astype(jnp.float32),
        lax.psum(part_mlp_in.astype(jnp.bfloat16), "grp").astype(jnp.float32),
        lax.psum(part_mlp_in_bias.astype(jnp.bfloat16), "grp").astype(jnp.float32),
        lax.psum(part_mlp_out.astype(jnp.bfloat16), "grp").astype(jnp.float32),
        lax.psum(part_mlp_out_bias.astype(jnp.bfloat16), "grp").astype(jnp.float32),
    )
    return (
        mixed_out,
        tokens_grad,
        share_in,
        share_out,
        share_gain,
        share_offset,
        share_mlp_in,
        share_mlp_in_bias,
        share_mlp_out,
        share_mlp_out_bias,
    )


MESH = pl.DeviceIdType.MESH
VMEM_LIMIT = 60 * 1024 * 1024
SCALE = HEAD_DIM ** (-0.5)
LOG2E = 1.4426950408889634
LN2 = 0.6931471805599453
BF = jnp.bfloat16
F32 = jnp.float32
NT = (((1,), (1,)), ((), ()))
NN = (((1,), (0,)), ((), ()))
TN = (((0,), (0,)), ((), ()))
CHUNKS = 4
BLOCK = 256
SWAP = 8
GRP = 4
PIECE = BLOCK // SWAP
PAIRS = 4
WIDTH = 512
SHARE = 64
SUMS = 4


def mm(left, right, form=NN):
    return lax.dot_general(left, right, form, preferred_element_type=F32)


def norm_stats(values):
    centre = values - jnp.mean(values, axis=-1, keepdims=True)
    inverse = lax.rsqrt(jnp.mean(centre * centre, axis=-1, keepdims=True) + EPSILON)
    return centre * inverse, inverse


def norm_back(grad, vhat, inverse, gain):
    scaled = grad * gain
    mean_one = jnp.mean(scaled, axis=-1, keepdims=True)
    mean_two = jnp.mean(scaled * vhat, axis=-1, keepdims=True)
    return inverse * (scaled - mean_one - vhat * mean_two)


def lanes(rows=BLOCK):
    return lax.broadcasted_iota(jnp.int32, (rows, 128), 1)


def split_three(values):
    high = values.astype(BF).astype(F32)
    rest = values - high
    middle = rest.astype(BF).astype(F32)
    low = rest - middle
    place = lanes(values.shape[0]) & 63
    terms = jnp.where(place == 0, high, jnp.where(place == 1, middle, jnp.where(place == 2, low, 0.0)))
    return terms.astype(BF)


def attention_forward(query, key, value, bias, put):
    def score(head):
        raw = mm(query(head // 2), key(head), NT)
        return raw if bias is None else raw + bias

    current = score(0)
    for pair in range(PAIRS):
        total = None
        tops = []
        for half in range(2):
            head = 2 * pair + half
            following = score(head + 1) if head + 1 < HEADS else None
            top = jnp.max(current, axis=-1, keepdims=True)
            weight = jnp.exp2(current - top).astype(BF)
            term = mm(weight, value(head))
            total = term if total is None else total + term
            tops.append(top)
            current = following
        row_total = total[:, 128:]
        out = (total[:, :128] / row_total).astype(BF)
        top_pair = jnp.where(lanes() < 64, tops[0], tops[1])
        put(pair, out, split_three(-(top_pair + jnp.log(row_total) * LOG2E)))


def attention_back(query, grad, key, value, bias):
    left = lanes() < 64
    grad_query = grad_key = grad_value = None
    for half in range(2):
        keys = key(half)
        score = mm(query, keys, NT)
        if bias is not None:
            score = score + bias
        weight = jnp.exp2(score)
        slope = mm(grad, value(half), NT)
        grad_score = (weight * slope).astype(BF)
        weight = weight.astype(BF)
        mine = left if half == 0 else jnp.logical_not(left)
        nothing = jnp.zeros((BLOCK, 128), BF)
        terms = (
            mm(grad_score, keys[:, :128]),
            mm(grad_score, jnp.where(mine, query[:, :128], nothing), TN),
            mm(weight, jnp.where(mine, grad[:, :128], nothing), TN),
        )
        if half == 0:
            grad_query, grad_key, grad_value = terms
        else:
            grad_query, grad_key, grad_value = (
                grad_query + terms[0],
                grad_key + terms[1],
                grad_value + terms[2],
            )
    return grad_query, grad_key, grad_value


def fused_kernel(
    tokens,
    cotangent,
    sample_counts,
    feature_counts,
    attn_in_hbm,
    attn_out_hbm,
    norm_gain_hbm,
    norm_bias_hbm,
    mlp_in_hbm,
    mlp_in_bias_hbm,
    mlp_out_hbm,
    mlp_out_bias_hbm,
    mixed,
    tokens_grad,
    sums,
    small,
    attn_in,
    attn_out,
    norm_gain,
    norm_bias,
    mlp_in,
    mlp_in_bias,
    mlp_out,
    mlp_out_bias,
    x_rows,
    normed_one,
    query_one,
    key_one,
    value_one,
    ones_key,
    ones_value,
    attn_one,
    first_send,
    first_recv,
    cot_recv,
    grad_recv,
    normed_two,
    attn_two,
    normed_three,
    active,
    grad_hidden,
    grad_packed,
    grad_low,
    query_two,
    key_two,
    value_two,
    feature_bias,
    key_zero,
    grad_key,
    grad_value,
    head_sum,
    vectors,
    vec_pair,
    vec_grp,
    vec_z,
    part_sum,
    one_sum,
    two_sum,
    three_sum,
    done_sum,
    load_sem,
    first_ss,
    first_rs,
    cot_ss,
    cot_rs,
    mixed_ss,
    mixed_rs,
    grad_ss,
    grad_rs,
    out_sem,
    sum_ss,
    sum_rs,
    vec_ss,
    vec_rs,
):
    grp = lax.axis_index("grp")
    me = lax.axis_index("swap")
    chip = me // 2
    core = me % 2
    col = grp % 2
    row = grp // 2
    odd = chip % 2
    upper = chip // 2
    samples = sample_counts[0]
    features = feature_counts[0]

    def swap_peer(k):
        return (me + k) % SWAP

    def grp_peer(k):
        return (grp + k) % GRP

    def z_peer(k):
        return ((chip + k) % 4) * 2 + core

    loads = [pltpu.make_async_copy(tokens.at[:, c], x_rows.at[c], load_sem.at[c]) for c in range(CHUNKS)]
    for index, (source, target) in enumerate(
        (
            (attn_in_hbm.at[0], attn_in.at[0]),
            (attn_out_hbm.at[0], attn_out.at[0]),
            (norm_gain_hbm, norm_gain),
            (norm_bias_hbm, norm_bias),
            (mlp_in_bias_hbm, mlp_in_bias),
            (mlp_out_bias_hbm, mlp_out_bias),
            (attn_in_hbm.at[1], attn_in.at[1]),
            (attn_out_hbm.at[1], attn_out.at[1]),
            (mlp_in_hbm, mlp_in),
            (mlp_out_hbm, mlp_out),
        )
    ):
        loads.append(pltpu.make_async_copy(source, target, load_sem.at[CHUNKS + index]))
    for copy in loads:
        copy.start()

    barrier = pltpu.get_barrier_semaphore()
    for k in range(1, SWAP):
        pl.semaphore_signal(barrier, inc=1, device_id={"swap": swap_peer(k)}, device_id_type=MESH)
    for k in range(1, GRP):
        pl.semaphore_signal(barrier, inc=1, device_id={"grp": grp_peer(k)}, device_id_type=MESH)
    pl.semaphore_wait(barrier, SWAP - 1 + GRP - 1)

    def exchange(source, target, send, recv):
        def copy(c, d, peer):
            return pltpu.make_async_remote_copy(
                src_ref=source(c, d),
                dst_ref=target(c, peer),
                send_sem=send.at[c, d],
                recv_sem=recv.at[c, peer],
                device_id={"swap": d},
                device_id_type=MESH,
            )

        def start(c):
            for k in range(1, SWAP):
                copy(c, swap_peer(k), me).start()

        def wait_send(c):
            for k in range(1, SWAP):
                copy(c, swap_peer(k), me).wait_send()

        def wait_recv(c):
            for k in range(1, SWAP):
                copy(c, swap_peer(k), swap_peer(k)).wait_recv()

        return start, wait_send, wait_recv

    first_start, first_wait_send, first_wait_recv = exchange(
        lambda c, d: first_send.at[c, d], lambda c, d: first_recv.at[c, d], first_ss, first_rs
    )
    cot_start, cot_wait_send, cot_wait_recv = exchange(
        lambda c, d: cotangent.at[d, c], lambda c, d: cot_recv.at[c, d], cot_ss, cot_rs
    )
    mixed_start, mixed_wait_send, mixed_wait_recv = exchange(
        lambda c, d: first_send.at[c, d], lambda c, d: mixed.at[d, c], mixed_ss, mixed_rs
    )
    grad_start, grad_wait_send, grad_wait_recv = exchange(
        lambda c, d: first_recv.at[c, d], lambda c, d: grad_recv.at[c, d], grad_ss, grad_rs
    )

    def own_cot(c):
        return pltpu.make_async_copy(cotangent.at[me, c], cot_recv.at[c, me], cot_rs.at[c, me])

    def own_mixed(c):
        return pltpu.make_async_copy(first_send.at[c, me], mixed.at[me, c], mixed_rs.at[c, me])

    def cot_begin(c):
        own_cot(c).start()
        cot_start(c)

    cot_begin(0)
    cot_begin(1)

    vectors[...] = jnp.zeros((16, WIDTH), F32)
    low_half = lax.broadcasted_iota(jnp.int32, (CHUNKS, BLOCK, 128), 2) < 64
    ones_key[0] = jnp.where(low_half, 1.0, 0.0).astype(BF)
    ones_key[1] = jnp.where(low_half, 0.0, 1.0).astype(BF)
    head_sum[...] = jnp.where(
        ((lax.broadcasted_iota(jnp.int32, (256, 128), 0) // 64) & 1)
        == (lax.broadcasted_iota(jnp.int32, (256, 128), 1) // 64),
        1.0,
        0.0,
    ).astype(BF)
    row_cell = lax.broadcasted_iota(jnp.int32, (BLOCK, BLOCK), 0)
    col_cell = lax.broadcasted_iota(jnp.int32, (BLOCK, BLOCK), 1)
    seen = jnp.logical_and((row_cell % PIECE) == (col_cell % PIECE), (col_cell // PIECE) < features)
    feature_bias[...] = jnp.where(seen, 0.0, MASKED).astype(F32)

    def valid_rows(c):
        row = lax.broadcasted_iota(jnp.int32, (BLOCK, 1), 0)
        return (row // PIECE) * (CHUNKS * PIECE) + c * PIECE + row % PIECE < samples

    def half_of(values, half):
        mine = (lanes(values.shape[0]) < 64) == (half == 0)
        return jnp.where(mine, values, jnp.zeros_like(values))

    def add_row(row, values):
        vectors[row : row + 1, :] += jnp.sum(values, axis=0, keepdims=True)

    def block(ref, c):
        return ref[c].reshape(BLOCK, WIDTH)

    for index in (0, 2, 3):
        loads[CHUNKS + index].wait()

    @pl.loop(0, CHUNKS)
    def _(c):
        pltpu.make_async_copy(tokens.at[:, c], x_rows.at[c], load_sem.at[c]).wait()
        vhat, _ = norm_stats(block(x_rows, c).astype(F32))
        normed = (vhat * norm_gain[0:1, :] + norm_bias[0:1, :]).astype(BF)
        normed_one[c] = normed
        valid = valid_rows(c)
        queries = mm(normed, attn_in[0, :, :WIDTH]) * (SCALE * LOG2E)
        for pair in range(PAIRS):
            query_one[c, pair, :, :128] = queries[:, 128 * pair : 128 * pair + 128].astype(BF)
        keys = mm(normed, attn_in[0, :, WIDTH : 2 * WIDTH])

        @pl.when(c == 0)
        def _():
            key_zero[...] = keys[0:8, :]

        keys = jnp.where(valid, keys, key_zero[0:1, :]).astype(BF)
        values = mm(normed, attn_in[0, :, 2 * WIDTH :])
        values = jnp.where(valid, values, 0.0).astype(BF)
        for head in range(HEADS):
            pair, half = head // 2, head % 2
            cut = slice(128 * pair, 128 * pair + 128)
            key_one[head, c] = half_of(keys[:, cut], half)
            value_one[head, c] = half_of(values[:, cut], half)
        for half in range(2):
            mine = (lanes() < 64) == (half == 0)
            ones_value[half, c] = jnp.where(jnp.logical_and(mine, valid), 1.0, 0.0).astype(BF)

    cells = CHUNKS * BLOCK

    def key_all(head):
        return key_one[head].reshape(cells, 128)

    def key_wide(head):
        return jnp.concatenate([key_all(head), ones_key[head % 2].reshape(cells, 128)], axis=1)

    def value_wide(head):
        return jnp.concatenate(
            [value_one[head].reshape(cells, 128), ones_value[head % 2].reshape(cells, 128)], axis=1
        )

    loads[CHUNKS + 1].wait()

    @pl.loop(0, CHUNKS)
    def _(c):
        def put(pair, out, extra):
            attn_one[c, :, 128 * pair : 128 * pair + 128] = out
            query_one[c, pair, :, 128:] = extra

        attention_forward(
            lambda pair: query_one[c, pair, :, :128], key_all, value_wide, None, put
        )
        first = block(x_rows, c).astype(F32) + mm(attn_one[c], attn_out[0])
        first_send[c] = first.astype(BF).reshape(SWAP, PIECE, WIDTH)
        first_recv[c, me] = first_send[c, me]
        first_start(c)

        @pl.when(c == 1)
        def _():
            cot_begin(2)

        @pl.when(c == 3)
        def _():
            cot_begin(3)

    def reduction(number, part, one, two, three, done, cut):
        def remote(source, target, index, where):
            return pltpu.make_async_remote_copy(
                src_ref=source,
                dst_ref=target,
                send_sem=sum_ss.at[number, index],
                recv_sem=sum_rs.at[number, index],
                device_id=where,
                device_id_type=MESH,
            )

        beside = {"grp": grp + 1 - 2 * col}
        above = {"grp": grp + 2 - 4 * row}
        out = sums.at[min(number, SUMS - 1), grp, :, cut]
        step_one = [
            remote(part.at[:, 1 - core, :, :, :, cut], one.at[:, :, :, :, cut], 0, {"swap": me + 1 - 2 * core})
        ]
        step_two = [
            remote(one.at[0:2, :, 1 - col, :, cut], two.at[0, :, :, :, cut], 1, beside),
            remote(one.at[2:4, 1 - row, :, :, cut], two.at[1, :, :, :, cut], 2, above),
        ]
        step_three = [
            remote(one.at[0:2, 1 - row, col, :, cut], two.at[2, 0, :, :, cut], 3, above),
            remote(one.at[2:4, row, 1 - col, :, cut], two.at[2, 1, :, :, cut], 4, beside),
        ]
        step_four = [
            remote(one.at[2 * k + 1 - odd, row, col, :, cut], three.at[k, :, cut], 5 + k, {"swap": me + 2 - 4 * odd})
            for k in range(2)
        ]
        step_five = [
            remote(
                one.at[2 - 2 * upper + odd, row, col, :, cut], three.at[2, :, cut], 7, {"swap": me + 4 - 8 * upper}
            )
        ]
        step_six = [remote(done.at[:, cut], out, 7 + k, {"grp": grp_peer(k)}) for k in range(1, GRP)]
        own = pltpu.make_async_copy(done.at[:, cut], out, sum_rs.at[number, 11])

        def begin():
            for copy in step_one:
                copy.start()

        def after_one():
            for copy in step_one:
                copy.wait_recv()

            @pl.loop(0, 4)
            def _(a):
                total = one[a, :, :, :, cut].astype(F32) + part[a, core, :, :, :, cut].astype(F32)
                one[a, :, :, :, cut] = total.astype(BF)

            for copy in step_two:
                copy.start()

        def after_two():
            for copy in step_two:
                copy.wait_recv()
            for a in range(2):
                total = one[a, :, col, :, cut].astype(F32) + two[0, a, :, :, cut].astype(F32)
                one[a, :, col, :, cut] = total.astype(BF)
                total = one[2 + a, row, :, :, cut].astype(F32) + two[1, a, :, :, cut].astype(F32)
                one[2 + a, row, :, :, cut] = total.astype(BF)
            for copy in step_three:
                copy.start()

        def after_three():
            for copy in step_three:
                copy.wait_recv()
            for a in range(4):
                total = one[a, row, col, :, cut].astype(F32) + two[2, a // 2, a % 2, :, cut].astype(F32)
                one[a, row, col, :, cut] = total.astype(BF)
            for copy in step_four:
                copy.start()

        def after_four():
            for copy in step_four:
                copy.wait_recv()
            for k in range(2):
                total = one[2 * k + odd, row, col, :, cut].astype(F32) + three[k, :, cut].astype(F32)
                one[2 * k + odd, row, col, :, cut] = total.astype(BF)
            for copy in step_five:
                copy.start()

        def after_five():
            for copy in step_five:
                copy.wait_recv()
            total = one[chip, row, col, :, cut].astype(F32) + three[2, :, cut].astype(F32)
            done[:, cut] = total.astype(BF)
            own.start()
            for copy in step_six:
                copy.start()

        def finish():
            own.wait()
            for copy in step_six:
                copy.wait_recv()
            for copy in step_one + step_two + step_three + step_four + step_five + step_six:
                copy.wait_send()

        return [begin, after_one, after_two, after_three, after_four, after_five, finish]

    every = slice(0, WIDTH)
    mid = [
        reduction(
            number,
            part_sum.at[number],
            one_sum.at[number],
            two_sum.at[number],
            three_sum.at[number],
            done_sum.at[number],
            every,
        )
        for number in range(3)
    ]
    end = [
        reduction(
            3 + half,
            mlp_out,
            grad_hidden.at[0],
            grad_hidden.at[1, 0:3],
            grad_hidden.at[2, 0:3, 0, 0],
            grad_hidden.at[3, 0, 0, 0],
            slice(256 * half, 256 * half + 256),
        )
        for half in range(2)
    ]

    def rows_of(ref):
        return ref[...].reshape(cells, WIDTH)

    def shares(values):
        return values.astype(BF).reshape(4, 2, 2, 2, 16, values.shape[1])

    def put_shares(number, piece, tile):
        part_sum[number, :, :, :, :, 16 * piece : 16 * piece + 16, :] = shares(tile)

    def grads_in(part):
        put_shares(0, part, mm(rows_of(normed_three), grad_hidden[part].reshape(cells, WIDTH), TN))

    def grads_out(part):
        tile = mm(active[part].reshape(cells, WIDTH), rows_of(cot_recv), TN)
        part_sum[1, part] = tile.astype(BF).reshape(2, 2, 2, SHARE, WIDTH)

    def wide_grads(part):
        cut = slice(WIDTH * part, WIDTH * part + WIDTH)
        put_shares(2, part, mm(rows_of(normed_two), grad_packed[:, :, cut].reshape(cells, WIDTH), TN))
        if part == 2:
            put_shares(2, 3, mm(rows_of(attn_two), rows_of(grad_low), TN))

    for index in range(4, 10):
        loads[CHUNKS + index].wait()

    def delta_of(grad, out):
        product = grad.astype(F32) * out.astype(F32)
        high = product.astype(BF)
        low = (product - high.astype(F32)).astype(BF)
        return split_three(-mm(jnp.concatenate([high, low], axis=1), head_sum[...]))

    @pl.loop(0, CHUNKS)
    def _(c):
        first_wait_recv(c)

        @pl.when(c == 3)
        def _():
            grad_start(1)

        resid_one = block(first_recv, c).astype(F32)
        vhat_two, inverse_two = norm_stats(resid_one)
        normed = (vhat_two * norm_gain[1:2, :] + norm_bias[1:2, :]).astype(BF)
        normed_two[c] = normed
        queries = mm(normed, attn_in[1, :, :WIDTH]) * (SCALE * LOG2E)
        keys = mm(normed, attn_in[1, :, WIDTH : 2 * WIDTH]).astype(BF)
        values = mm(normed, attn_in[1, :, 2 * WIDTH :]).astype(BF)
        for pair in range(PAIRS):
            cut = slice(128 * pair, 128 * pair + 128)
            query_two[pair, :, :128] = queries[:, cut].astype(BF)
            for half in range(2):
                key_two[2 * pair + half, :, :128] = half_of(keys[:, cut], half)
                key_two[2 * pair + half, :, 128:] = ones_key[half, 0]
                value_two[2 * pair + half, :, :128] = half_of(values[:, cut], half)
                value_two[2 * pair + half, :, 128:] = ones_key[half, 0]

        def put(pair, out, extra):
            attn_two[c, :, 128 * pair : 128 * pair + 128] = out
            query_two[pair, :, 128:] = extra

        attention_forward(
            lambda pair: query_two[pair, :, :128],
            lambda head: key_two[head, :, :128],
            lambda head: value_two[head],
            feature_bias[...],
            put,
        )
        second = resid_one + mm(attn_two[c], attn_out[1])
        vhat_three, inverse_three = norm_stats(second)
        normed = (vhat_three * norm_gain[2:3, :] + norm_bias[2:3, :]).astype(BF)
        normed_three[c] = normed
        own_cot(c).wait()
        cot_wait_recv(c)
        cot_low = block(cot_recv, c)
        cot = cot_low.astype(F32)
        add_row(10, cot)

        @pl.when(c == 2)
        def _():
            grad_start(0)


        @pl.when(c == 3)
        def _():
            grad_start(2)

        outcome = second + mlp_out_bias[...]
        grad_normed = jnp.zeros((BLOCK, WIDTH), F32)
        for part in range(4):
            cut = slice(WIDTH * part, WIDTH * part + WIDTH)
            hidden = mm(normed, mlp_in[:, cut]) + mlp_in_bias[:, cut]
            weight_out = mlp_out[part].reshape(WIDTH, WIDTH)
            grad_active = mm(cot_low, weight_out, NT)
            below = 0.5 + 0.5 * lax.erf(hidden * 0.7071067811865476)
            act = (hidden * below).astype(BF)
            density = jnp.exp2(hidden * hidden * (-0.5 * LOG2E)) * 0.3989422804014327
            grad_hid = ((below + hidden * density) * grad_active).astype(BF)
            active[part, c] = act
            grad_hidden[part, c] = grad_hid.reshape(2, 2, SHARE, WIDTH)
            add_row(6 + part, grad_hid.astype(F32))
            outcome = outcome + mm(act, weight_out)
            grad_normed = grad_normed + mm(grad_hid, mlp_in[:, cut], NT)

        @pl.when(c == CHUNKS - 1)
        def _():
            for part in range(4):
                grads_in(part)
            mid[0][0]()
            for part in range(4):
                grads_out(part)
            mid[1][0]()

        first_wait_send(c)
        first_send[c] = outcome.astype(BF).reshape(SWAP, PIECE, WIDTH)
        add_row(2, grad_normed * vhat_three)
        add_row(5, grad_normed)
        grad_second = cot + norm_back(grad_normed, vhat_three, inverse_three, norm_gain[2:3, :])
        grad_second_low = grad_second.astype(BF)
        grad_low[c] = grad_second_low
        grad_attn = mm(grad_second_low, attn_out[1], NT).astype(BF)
        for pair in range(PAIRS):
            cut = slice(128 * pair, 128 * pair + 128)
            piece = grad_attn[:, cut]
            wide = jnp.concatenate([piece, delta_of(piece, attn_two[c, :, cut])], axis=1)
            grad_q, grad_k, grad_v = attention_back(
                query_two[pair],
                wide,
                lambda half: key_two[2 * pair + half],
                lambda half: value_two[2 * pair + half],
                feature_bias[...],
            )
            grad_packed[c, :, 128 * pair : 128 * pair + 128] = (grad_q * SCALE).astype(BF)
            grad_packed[c, :, WIDTH + 128 * pair : WIDTH + 128 * pair + 128] = (grad_k * LN2).astype(BF)
            grad_packed[c, :, 2 * WIDTH + 128 * pair : 2 * WIDTH + 128 * pair + 128] = grad_v.astype(BF)
        grad_normed = mm(grad_packed[c], attn_in[1], NT)
        add_row(1, grad_normed * vhat_two)
        add_row(4, grad_normed)
        grad_first = grad_second + norm_back(grad_normed, vhat_two, inverse_two, norm_gain[1:2, :])
        first_recv[c] = grad_first.astype(BF).reshape(SWAP, PIECE, WIDTH)
        grad_recv[c, me] = first_recv[c, me]
        own_mixed(c).start()

        @pl.when(c == CHUNKS - 1)
        def _():
            grad_start(c)

    mid[0][1]()

    for part in range(3):
        wide_grads(part)
    mid[2][0]()
    mid[1][1]()

    def run(hooks, c):
        for when, call in hooks:

            @pl.when(c == when)
            def _():
                call()

    hooks = (
        (),
        ((0, mid[2][1]), (2, mid[0][2]), (3, mid[1][2]), ),
        (),
        ((0, mid[2][2]), (1, mid[0][3]), (1, end[0][1]), (2, mid[1][3]), (3, mid[0][4]), (3, mid[2][3]), (3, end[0][2]), ),
        ((0, mid[1][4]), (0, end[1][1]), (1, mid[0][5]), (1, mid[2][4]), (2, end[0][3]), (2, end[1][2]), (3, mid[1][5]), ),
    )
    for half in range(2):
        pairs = (2 * half, 2 * half + 1)
        grad_key[...] = jnp.zeros((2, cells, 128), F32)
        grad_value[...] = jnp.zeros((2, cells, 128), F32)

        @pl.loop(0, CHUNKS)
        def _(c):
            if half == 0:
                grad_wait_recv(c)
                mixed_start(c)
                grad_attn = mm(block(grad_recv, c), attn_out[0], NT).astype(BF)
                for pair in range(PAIRS):
                    cut = slice(128 * pair, 128 * pair + 128)
                    piece = grad_attn[:, cut]
                    active[pair, c, :, :128] = piece
                    active[pair, c, :, 128:256] = delta_of(piece, attn_one[c, :, cut])
            for pair in pairs:
                grad_q, grad_k, grad_v = attention_back(
                    query_one[c, pair],
                    active[pair, c, :, :256],
                    lambda side: key_wide(2 * pair + side),
                    lambda side: value_wide(2 * pair + side),
                    None,
                )
                grad_packed[c, :, 128 * pair : 128 * pair + 128] = (grad_q * SCALE).astype(BF)
                grad_key[pair % 2] += grad_k
                grad_value[pair % 2] += grad_v
                run(hooks[pair], c)

        for pair in pairs:
            for c in range(CHUNKS):
                rows = slice(BLOCK * c, BLOCK * c + BLOCK)
                grad_packed[c, :, WIDTH + 128 * pair : WIDTH + 128 * pair + 128] = (
                    grad_key[pair % 2, rows, :] * LN2
                ).astype(BF)
                grad_packed[c, :, 2 * WIDTH + 128 * pair : 2 * WIDTH + 128 * pair + 128] = jnp.where(
                    valid_rows(c), grad_value[pair % 2, rows, :], 0.0
                ).astype(BF)
        if half == 0:
            grad_rows = grad_recv[...].reshape(cells, WIDTH)
            mlp_out[:, :, :, :, 0:16, :] = shares(mm(rows_of(attn_one), grad_rows, TN))
        for part in range(3):
            cut = slice(WIDTH * part + 256 * half, WIDTH * part + 256 * half + 256)
            tile = mm(rows_of(normed_one), grad_packed[:, :, cut].reshape(cells, 256), TN)
            mlp_out[:, :, :, :, 16 + 16 * part : 32 + 16 * part, 256 * half : 256 * half + 256] = shares(tile)
        end[half][0]()

    @pl.loop(0, CHUNKS)
    def _(c):
        grad_normed = mm(grad_packed[c], attn_in[0], NT)
        vhat, inverse = norm_stats(block(x_rows, c).astype(F32))
        add_row(0, grad_normed * vhat)
        add_row(3, grad_normed)
        result = block(grad_recv, c).astype(F32) + norm_back(grad_normed, vhat, inverse, norm_gain[0:1, :])
        normed_one[c] = result.astype(BF)
        pltpu.make_async_copy(
            normed_one.at[c].reshape(SWAP, PIECE, WIDTH), tokens_grad.at[:, c], out_sem.at[c]
        ).start()
        run(hooks[4], c)

    def vec_copy(source, target, index, where):
        return pltpu.make_async_remote_copy(
            src_ref=source,
            dst_ref=target,
            send_sem=vec_ss.at[index],
            recv_sem=vec_rs.at[index],
            device_id=where,
            device_id_type=MESH,
        )

    vec_one = vec_copy(vectors, vec_pair, 0, {"swap": me + 1 - 2 * core})
    vec_two = [vec_copy(vec_grp.at[grp], vec_grp.at[grp], k, {"grp": grp_peer(k)}) for k in range(1, GRP)]
    vec_two_in = [
        vec_copy(vec_grp.at[grp_peer(-k)], vec_grp.at[grp_peer(-k)], k, {"grp": grp_peer(-k)}) for k in range(1, GRP)
    ]
    vec_three = [vec_copy(vec_z.at[chip], vec_z.at[chip], 3 + k, {"swap": z_peer(k)}) for k in range(1, 4)]
    vec_three_in = [
        vec_copy(vec_z.at[(chip - k) % 4], vec_z.at[(chip - k) % 4], 3 + k, {"swap": z_peer(-k)}) for k in range(1, 4)
    ]
    vec_one.start()
    mid[2][5]()
    end[0][4]()
    end[1][3]()
    vec_one.wait_recv()
    vec_grp[grp] = vectors[...] + vec_pair[...]
    for copy in vec_two:
        copy.start()
    end[0][5]()
    end[1][4]()
    for copy in vec_two_in:
        copy.wait_recv()
    vec_z[chip] = (vec_grp[0] + vec_grp[1]) + (vec_grp[2] + vec_grp[3])
    for copy in vec_three:
        copy.start()
    end[1][5]()
    for copy in vec_three_in:
        copy.wait_recv()
    whole = (vec_z[0] + vec_z[1]) + (vec_z[2] + vec_z[3])

    def share(rows, width, step):
        result = None
        for index in range(WIDTH // width):
            piece = whole[rows, index * width : index * width + width]
            mine = step == index
            result = jnp.where(mine, piece, 0.0 if result is None else result)
        return result

    small[0:3, 0:64] = share(slice(0, 3), 64, me)
    small[3:6, 0:64] = share(slice(3, 6), 64, me)
    bias_row = None
    for index in range(4):
        piece = share(slice(6 + index, 7 + index), 256, core)
        bias_row = jnp.where(chip == index, piece, 0.0 if bias_row is None else bias_row)
    small[6:7, :] = bias_row
    small[7:8, 0:64] = share(slice(10, 11), 64, me)

    for steps in mid + end:
        steps[6]()
    vec_one.wait_send()
    for copy in vec_two + vec_three:
        copy.wait_send()

    @pl.loop(0, CHUNKS)
    def _(c):
        own_mixed(c).wait()
        mixed_wait_recv(c)
        mixed_wait_send(c)
        cot_wait_send(c)
        grad_wait_send(c)
        pltpu.make_async_copy(
            normed_one.at[c].reshape(SWAP, PIECE, WIDTH), tokens_grad.at[:, c], out_sem.at[c]
        ).wait()


def finish_kernel(mixed, tokens_grad, sums_hbm, small_hbm, *refs):
    outs, (sums, small, held, sem) = refs[:10], refs[10:]
    loads = [pltpu.make_async_copy(sums_hbm.at[k], sums.at[k], sem.at[k]) for k in range(SUMS)]
    loads.append(pltpu.make_async_copy(small_hbm, small, sem.at[SUMS]))
    cells_in, cells_out = [], []
    for index, source in enumerate((mixed, tokens_grad)):
        for half in range(2):
            part = slice(4 * half, 4 * half + 4)
            place = SUMS + 1 + 2 * index + half
            cells_in.append(pltpu.make_async_copy(source.at[part], held.at[index, part], sem.at[place]))
            cells_out.append(pltpu.make_async_copy(held.at[index, part], outs[index].at[part], sem.at[place + 4]))
    for copy in cells_in + loads:
        copy.start()
    for before, after in zip(cells_in, cells_out):
        before.wait()
        after.start()
    for copy in loads:
        copy.wait()
    for grp in range(GRP):
        rows = slice(16 * grp, 16 * grp + 16)
        for part in range(4):
            cut = slice(WIDTH * part, WIDTH * part + WIDTH)
            piece = slice(16 * part, 16 * part + 16)
            outs[6][rows, cut] = sums[0, grp, piece].astype(F32)
            if part < 3:
                outs[2][1, rows, cut] = sums[2, grp, piece].astype(F32)
                outs[2][0, rows, cut] = sums[3, grp, 16 * part + 16 : 16 * part + 32].astype(F32)
        outs[8][SHARE * grp : SHARE * grp + SHARE] = sums[1, grp].astype(F32)
        outs[3][1, rows] = sums[2, grp, 48:64].astype(F32)
        outs[3][0, rows] = sums[3, grp, 0:16].astype(F32)
    outs[4][...] = small[0:3, 0:64]
    outs[5][...] = small[3:6, 0:64]
    outs[7][...] = small[6:7, 0:256]
    outs[9][...] = small[7:8, 0:64]
    for copy in cells_out:
        copy.wait()


def fused_local(
    tokens,
    sample_counts,
    feature_counts,
    attn_in,
    attn_out,
    norm_gain,
    norm_bias,
    mlp_in,
    mlp_in_bias,
    mlp_out,
    mlp_out_bias,
    cotangent,
):
    cells = (SWAP, CHUNKS, PIECE, WIDTH)
    blocks = (CHUNKS, SWAP, PIECE, WIDTH)
    rows = (CHUNKS, BLOCK, WIDTH)
    anywhere = pl.BlockSpec(memory_space=pl.ANY)
    scalar = pl.BlockSpec(memory_space=pltpu.SMEM)
    vector = pl.BlockSpec(memory_space=pltpu.VMEM)
    sem = pltpu.SemaphoreType.DMA

    def buffer(*shape, kind=BF):
        return pltpu.VMEM(shape, kind)

    def result(shape, kind=F32):
        return jax.ShapeDtypeStruct(shape, kind)

    mixed, tokens_grad, sums, small = pl.pallas_call(
        fused_kernel,
        name="layer",
        out_shape=(
            result(cells, BF),
            result(cells, BF),
            result((SUMS, GRP, SHARE, WIDTH), BF),
            result((8, 256)),
        ),
        in_specs=[anywhere, anywhere, scalar, scalar] + [anywhere] * 8,
        out_specs=(anywhere, anywhere, anywhere, vector),
        scratch_shapes=[
            buffer(2, WIDTH, 3 * WIDTH),
            buffer(2, WIDTH, WIDTH),
            buffer(3, WIDTH, kind=F32),
            buffer(3, WIDTH, kind=F32),
            buffer(WIDTH, 4 * WIDTH),
            buffer(1, 4 * WIDTH, kind=F32),
            buffer(4, 2, 2, 2, SHARE, WIDTH),
            buffer(1, WIDTH, kind=F32),
            buffer(*blocks),
            buffer(*rows),
            buffer(CHUNKS, PAIRS, BLOCK, 256),
            buffer(HEADS, CHUNKS, BLOCK, 128),
            buffer(HEADS, CHUNKS, BLOCK, 128),
            buffer(2, CHUNKS, BLOCK, 128),
            buffer(2, CHUNKS, BLOCK, 128),
            buffer(*rows),
            buffer(*blocks),
            buffer(*blocks),
            buffer(*blocks),
            buffer(*blocks),
            buffer(*rows),
            buffer(*rows),
            buffer(*rows),
            buffer(4, *rows),
            buffer(4, CHUNKS, 2, 2, SHARE, WIDTH),
            buffer(CHUNKS, BLOCK, 3 * WIDTH),
            buffer(*rows),
            buffer(PAIRS, BLOCK, 256),
            buffer(HEADS, BLOCK, 256),
            buffer(HEADS, BLOCK, 256),
            buffer(BLOCK, BLOCK, kind=F32),
            buffer(8, WIDTH, kind=F32),
            buffer(2, CHUNKS * BLOCK, 128, kind=F32),
            buffer(2, CHUNKS * BLOCK, 128, kind=F32),
            buffer(256, 128),
            buffer(16, WIDTH, kind=F32),
            buffer(16, WIDTH, kind=F32),
            buffer(GRP, 16, WIDTH, kind=F32),
            buffer(4, 16, WIDTH, kind=F32),
            buffer(3, 4, 2, 2, 2, SHARE, WIDTH),
            buffer(3, 4, 2, 2, SHARE, WIDTH),
            buffer(3, 3, 2, 2, SHARE, WIDTH),
            buffer(3, 3, SHARE, WIDTH),
            buffer(3, SHARE, WIDTH),
            sem((CHUNKS + 10,)),
        ]
        + [sem((CHUNKS, SWAP))] * 8
        + [sem((CHUNKS,))]
        + [sem((5, 12))] * 2
        + [sem((7,))] * 2,
        compiler_params=pltpu.CompilerParams(
            collective_id=0, has_side_effects=True, vmem_limit_bytes=VMEM_LIMIT
        ),
    )(
        tokens.reshape(cells),
        cotangent.reshape(cells),
        sample_counts,
        feature_counts,
        attn_in,
        attn_out,
        norm_gain,
        norm_bias,
        mlp_in,
        mlp_in_bias.reshape(1, -1),
        mlp_out.reshape(4, 2, 2, 2, SHARE, WIDTH),
        mlp_out_bias.reshape(1, -1),
    )
    shapes = (
        result(cells, BF),
        result(cells, BF),
        result((2, 64, 3 * WIDTH)),
        result((2, 64, WIDTH)),
        result((3, 64)),
        result((3, 64)),
        result((64, 4 * WIDTH)),
        result((1, 256)),
        result((256, WIDTH)),
        result((1, 64)),
    )
    outs = pl.pallas_call(
        finish_kernel,
        name="results",
        out_shape=shapes,
        in_specs=[anywhere] * 4,
        out_specs=(anywhere, anywhere) + (vector,) * 8,
        scratch_shapes=[
            buffer(SUMS, GRP, SHARE, WIDTH),
            buffer(8, 256, kind=F32),
            buffer(2, *cells),
            sem((SUMS + 9,)),
        ],
        compiler_params=pltpu.CompilerParams(vmem_limit_bytes=VMEM_LIMIT),
    )(mixed, tokens_grad, sums, small)
    return (
        outs[0].reshape(tokens.shape),
        outs[1].reshape(tokens.shape),
        *outs[2:7],
        outs[7].reshape(-1),
        outs[8],
        outs[9].reshape(-1),
    )


def solution(mesh):
    placed = (
        P("grp", None, "swap", None),
        P("grp"),
        P("grp"),
        P(),
        P(),
        P(),
        P(),
        P(),
        P(),
        P(),
        P(),
        P("grp", None, "swap", None),
    )
    def layer(*args):
        tokens, mlp_in = args[0], args[7]
        fits = (
            (mesh.shape["swap"], mesh.shape["grp"]) == (SWAP, GRP)
            and tokens.shape == (1, CHUNKS * BLOCK, 1, WIDTH)
            and mlp_in.shape == (WIDTH, 4 * WIDTH)
        )
        return fused_local(*args) if fits else local(*args)

    return jax.shard_map(
        layer,
        mesh=mesh,
        in_specs=placed,
        out_specs=(
            P("grp", None, "swap", None),
            P("grp", None, "swap", None),
            P(None, "swap", None),
            P(None, "swap", None),
            P(None, "swap"),
            P(None, "swap"),
            P("swap", None),
            P("swap"),
            P("swap", None),
            P("swap"),
        ),
        check_vma=False,
    )
```

```python
import jax
import jax.numpy as jnp
from jax import lax
from jax.experimental import pallas as pl
from jax.experimental.pallas import tpu as pltpu
from jax.sharding import PartitionSpec as P

HEADS = 8
HEAD_DIM = 64


EPSILON = 1e-05
MASKED = -1e30
SAMPLE_FORMS = ("tqfhe,tkfhe->tfhqk", "tfhqk,tkfhe->tqfhe", "tfhqk,tqfhe->tkfhe")
FEATURE_FORMS = ("tsqhe,tskhe->tshqk", "tshqk,tskhe->tsqhe", "tshqk,tsqhe->tskhe")


def layer_norm(values, factor, offset):
    centre = values - jnp.mean(values, axis=-1, keepdims=True)
    spread = jnp.mean(centre * centre, axis=-1, keepdims=True)
    return centre * lax.rsqrt(spread + EPSILON) * factor + offset


def exact_gelu(values):
    return jax.nn.gelu(values, approximate=False)


def project(left, weight):
    return jnp.dot(left, weight, preferred_element_type=jnp.float32)


def project_back(grad_rows, weight):
    return jnp.einsum("...c,dc->...d", grad_rows, weight, preferred_element_type=jnp.float32)


def weight_grad(left, grad_rows):
    return jnp.einsum(
        "nd,nc->dc",
        left.reshape(-1, left.shape[-1]),
        grad_rows.reshape(-1, grad_rows.shape[-1]),
        preferred_element_type=jnp.float32,
    )


def split_heads(packed):
    leading = packed.shape[:-1]
    model_width = packed.shape[-1] // 3
    query_rows = packed[..., :model_width].reshape(leading + (HEADS, HEAD_DIM))
    key_rows = packed[..., model_width : 2 * model_width].reshape(leading + (HEADS, HEAD_DIM))
    value_rows = packed[..., 2 * model_width :].reshape(leading + (HEADS, HEAD_DIM))
    return (query_rows, key_rows, value_rows)


def masked_scores(query_rows, key_rows, valid, forms):
    raw_scores = jnp.einsum(
        forms[0], query_rows, key_rows, preferred_element_type=jnp.float32
    ) * HEAD_DIM ** (-0.5)
    return jnp.where(valid[:, None, None, None, :], raw_scores, MASKED)


def attend(packed, valid, forms):
    leading = packed.shape[:-1]
    query_rows, key_rows, value_rows = split_heads(packed)
    scores = masked_scores(query_rows, key_rows, valid, forms)
    row_max = jnp.max(scores, axis=-1, keepdims=True)
    exponent = jnp.exp(scores - row_max)
    row_total = jnp.sum(exponent, axis=-1, keepdims=True)
    probability = (exponent / row_total).astype(jnp.bfloat16)
    mixed_rows = jnp.einsum(forms[1], probability, value_rows, preferred_element_type=jnp.float32)
    return (mixed_rows.reshape(leading + (packed.shape[-1] // 3,)), row_max + jnp.log(row_total))


def attend_back(packed, valid, log_total, grad_out, forms):
    leading = packed.shape[:-1]
    model_width = packed.shape[-1] // 3
    query_rows, key_rows, value_rows = split_heads(packed)
    grad_rows = grad_out.reshape(leading + (HEADS, HEAD_DIM))
    scores = masked_scores(query_rows, key_rows, valid, forms)
    probability = jnp.exp(scores - log_total)
    grad_values = jnp.einsum(
        forms[2], probability.astype(jnp.bfloat16), grad_rows, preferred_element_type=jnp.float32
    )
    grad_probs = jnp.einsum(forms[0], grad_rows, value_rows, preferred_element_type=jnp.float32)
    inner_sum = jnp.sum(probability * grad_probs, axis=-1, keepdims=True)
    grad_scores = (probability * (grad_probs - inner_sum)).astype(jnp.bfloat16)
    grad_query = jnp.einsum(
        forms[1], grad_scores, key_rows, preferred_element_type=jnp.float32
    ) * HEAD_DIM ** (-0.5)
    grad_keys = jnp.einsum(
        forms[2], grad_scores, query_rows, preferred_element_type=jnp.float32
    ) * HEAD_DIM ** (-0.5)
    return jnp.concatenate(
        [
            grad_query.reshape(leading + (model_width,)).astype(jnp.bfloat16),
            grad_keys.reshape(leading + (model_width,)).astype(jnp.bfloat16),
            grad_values.reshape(leading + (model_width,)).astype(jnp.bfloat16),
        ],
        axis=-1,
    )


def local(
    tokens,
    sample_counts,
    feature_counts,
    attn_in,
    attn_out,
    norm_gain,
    norm_bias,
    mlp_in,
    mlp_in_bias,
    mlp_out,
    mlp_out_bias,
    cotangent,
):
    samples = tokens.shape[1]
    sample_valid = jnp.arange(samples, dtype=jnp.int32)[None, :] < sample_counts[:, None]
    inputs = tokens.astype(jnp.float32)
    norm_one, back_one = jax.vjp(layer_norm, inputs, norm_gain[0], norm_bias[0])
    normed_one = norm_one.astype(jnp.bfloat16)
    packed_one = project(normed_one, attn_in[0]).astype(jnp.bfloat16)
    attn_one, log_total_one = attend(packed_one, sample_valid, SAMPLE_FORMS)
    attn_one = attn_one.astype(jnp.bfloat16)
    first_resid = (inputs + project(attn_one, attn_out[0])).astype(jnp.bfloat16)
    moved_rows = lax.all_to_all(first_resid, "swap", split_axis=1, concat_axis=2, tiled=True)
    features = moved_rows.shape[2]
    feature_valid = jnp.arange(features, dtype=jnp.int32)[None, :] < feature_counts[:, None]
    resid_one = moved_rows.astype(jnp.float32)
    norm_two, back_two = jax.vjp(layer_norm, resid_one, norm_gain[1], norm_bias[1])
    normed_two = norm_two.astype(jnp.bfloat16)
    packed_two = project(normed_two, attn_in[1]).astype(jnp.bfloat16)
    attn_two, log_total_two = attend(packed_two, feature_valid, FEATURE_FORMS)
    attn_two = attn_two.astype(jnp.bfloat16)
    resid_two = resid_one + project(attn_two, attn_out[1])
    norm_three, back_three = jax.vjp(layer_norm, resid_two, norm_gain[2], norm_bias[2])
    normed_three = norm_three.astype(jnp.bfloat16)
    hidden = project(normed_three, mlp_in) + mlp_in_bias
    activated, back_gelu = jax.vjp(exact_gelu, hidden)
    active_low = activated.astype(jnp.bfloat16)
    outcome = (resid_two + project(active_low, mlp_out) + mlp_out_bias).astype(jnp.bfloat16)
    mixed_out = lax.all_to_all(outcome, "swap", split_axis=2, concat_axis=1, tiled=True)
    grad_out = lax.all_to_all(cotangent, "swap", split_axis=1, concat_axis=2, tiled=True)
    grad_three = grad_out.astype(jnp.float32)
    grad_mlp_out = weight_grad(active_low, grad_out)
    grad_mlp_out_bias = jnp.sum(grad_three.reshape(-1, grad_three.shape[-1]), axis=0)
    grad_active = project_back(grad_out, mlp_out)
    grad_hidden = back_gelu(grad_active)[0].astype(jnp.bfloat16)
    grad_mlp_in = weight_grad(normed_three, grad_hidden)
    grad_mlp_in_bias = jnp.sum(
        grad_hidden.astype(jnp.float32).reshape(-1, grad_hidden.shape[-1]), axis=0
    )
    grad_resid, gain_three, offset_three = back_three(project_back(grad_hidden, mlp_in))
    grad_second = grad_three + grad_resid
    grad_second_low = grad_second.astype(jnp.bfloat16)
    grad_attn_out_two = weight_grad(attn_two, grad_second_low)
    grad_attn_two = project_back(grad_second_low, attn_out[1]).astype(jnp.bfloat16)
    grad_packed_two = attend_back(
        packed_two, feature_valid, log_total_two, grad_attn_two, FEATURE_FORMS
    )
    grad_attn_in_two = weight_grad(normed_two, grad_packed_two)
    grad_resid_two, gain_two, offset_two = back_two(project_back(grad_packed_two, attn_in[1]))
    grad_first = (grad_second + grad_resid_two).astype(jnp.bfloat16)
    grad_back = lax.all_to_all(grad_first, "swap", split_axis=2, concat_axis=1, tiled=True)
    grad_attn_out_one = weight_grad(attn_one, grad_back)
    grad_attn_one = project_back(grad_back, attn_out[0]).astype(jnp.bfloat16)
    grad_packed_one = attend_back(
        packed_one, sample_valid, log_total_one, grad_attn_one, SAMPLE_FORMS
    )
    grad_attn_in_one = weight_grad(normed_one, grad_packed_one)
    grad_input, gain_one, offset_one = back_one(project_back(grad_packed_one, attn_in[0]))
    tokens_grad = (grad_back.astype(jnp.float32) + grad_input).astype(jnp.bfloat16)
    stack_in = jnp.stack([grad_attn_in_one, grad_attn_in_two])
    stack_out = jnp.stack([grad_attn_out_one, grad_attn_out_two])
    stack_gain = jnp.stack([gain_one, gain_two, gain_three])
    stack_offset = jnp.stack([offset_one, offset_two, offset_three])
    (
        part_in,
        part_out,
        part_gain,
        part_offset,
        part_mlp_in,
        part_mlp_in_bias,
        part_mlp_out,
        part_mlp_out_bias,
    ) = (
        lax.psum_scatter(stack_in, "swap", scatter_dimension=1, tiled=True),
        lax.psum_scatter(stack_out, "swap", scatter_dimension=1, tiled=True),
        lax.psum_scatter(stack_gain, "swap", scatter_dimension=1, tiled=True),
        lax.psum_scatter(stack_offset, "swap", scatter_dimension=1, tiled=True),
        lax.psum_scatter(grad_mlp_in, "swap", scatter_dimension=0, tiled=True),
        lax.psum_scatter(grad_mlp_in_bias, "swap", scatter_dimension=0, tiled=True),
        lax.psum_scatter(grad_mlp_out, "swap", scatter_dimension=0, tiled=True),
        lax.psum_scatter(grad_mlp_out_bias, "swap", scatter_dimension=0, tiled=True),
    )
    (
        share_in,
        share_out,
        share_gain,
        share_offset,
        share_mlp_in,
        share_mlp_in_bias,
        share_mlp_out,
        share_mlp_out_bias,
    ) = (
        lax.psum(part_in.astype(jnp.bfloat16), "grp").astype(jnp.float32),
        lax.psum(part_out.astype(jnp.bfloat16), "grp").astype(jnp.float32),
        lax.psum(part_gain.astype(jnp.bfloat16), "grp").astype(jnp.float32),
        lax.psum(part_offset.astype(jnp.bfloat16), "grp").astype(jnp.float32),
        lax.psum(part_mlp_in.astype(jnp.bfloat16), "grp").astype(jnp.float32),
        lax.psum(part_mlp_in_bias.astype(jnp.bfloat16), "grp").astype(jnp.float32),
        lax.psum(part_mlp_out.astype(jnp.bfloat16), "grp").astype(jnp.float32),
        lax.psum(part_mlp_out_bias.astype(jnp.bfloat16), "grp").astype(jnp.float32),
    )
    return (
        mixed_out,
        tokens_grad,
        share_in,
        share_out,
        share_gain,
        share_offset,
        share_mlp_in,
        share_mlp_in_bias,
        share_mlp_out,
        share_mlp_out_bias,
    )


MESH = pl.DeviceIdType.MESH
VMEM_LIMIT = 60 * 1024 * 1024
SCALE = HEAD_DIM ** (-0.5)
LOG2E = 1.4426950408889634
LN2 = 0.6931471805599453
BF = jnp.bfloat16
F32 = jnp.float32
NT = (((1,), (1,)), ((), ()))
NN = (((1,), (0,)), ((), ()))
TN = (((0,), (0,)), ((), ()))
CHUNKS = 4
BLOCK = 256
SWAP = 8
GRP = 4
PIECE = BLOCK // SWAP
PAIRS = 4
WIDTH = 512
SHARE = 64
SUMS = 4


def mm(left, right, form=NN):
    return lax.dot_general(left, right, form, preferred_element_type=F32)


def norm_stats(values):
    centre = values - jnp.mean(values, axis=-1, keepdims=True)
    inverse = lax.rsqrt(jnp.mean(centre * centre, axis=-1, keepdims=True) + EPSILON)
    return centre * inverse, inverse


def norm_back(grad, vhat, inverse, gain):
    scaled = grad * gain
    mean_one = jnp.mean(scaled, axis=-1, keepdims=True)
    mean_two = jnp.mean(scaled * vhat, axis=-1, keepdims=True)
    return inverse * (scaled - mean_one - vhat * mean_two)


def lanes(rows=BLOCK):
    return lax.broadcasted_iota(jnp.int32, (rows, 128), 1)


def split_three(values):
    high = values.astype(BF).astype(F32)
    rest = values - high
    middle = rest.astype(BF).astype(F32)
    low = rest - middle
    place = lanes(values.shape[0]) & 63
    terms = jnp.where(place == 0, high, jnp.where(place == 1, middle, jnp.where(place == 2, low, 0.0)))
    return terms.astype(BF)


def attention_forward(query, key, value, bias, put):
    def score(head):
        raw = mm(query(head // 2), key(head), NT)
        return raw if bias is None else raw + bias

    current = score(0)
    for pair in range(PAIRS):
        total = None
        tops = []
        for half in range(2):
            head = 2 * pair + half
            following = score(head + 1) if head + 1 < HEADS else None
            top = jnp.max(current, axis=-1, keepdims=True)
            weight = jnp.exp2(current - top).astype(BF)
            term = mm(weight, value(head))
            total = term if total is None else total + term
            tops.append(top)
            current = following
        row_total = total[:, 128:]
        out = (total[:, :128] / row_total).astype(BF)
        top_pair = jnp.where(lanes() < 64, tops[0], tops[1])
        put(pair, out, split_three(-(top_pair + jnp.log(row_total) * LOG2E)))


def attention_back(query, grad, key, value, bias):
    left = lanes() < 64
    grad_query = grad_key = grad_value = None
    for half in range(2):
        keys = key(half)
        score = mm(query, keys, NT)
        if bias is not None:
            score = score + bias
        weight = jnp.exp2(score)
        slope = mm(grad, value(half), NT)
        grad_score = (weight * slope).astype(BF)
        weight = weight.astype(BF)
        mine = left if half == 0 else jnp.logical_not(left)
        nothing = jnp.zeros((BLOCK, 128), BF)
        terms = (
            mm(grad_score, keys[:, :128]),
            mm(grad_score, jnp.where(mine, query[:, :128], nothing), TN),
            mm(weight, jnp.where(mine, grad[:, :128], nothing), TN),
        )
        if half == 0:
            grad_query, grad_key, grad_value = terms
        else:
            grad_query, grad_key, grad_value = (
                grad_query + terms[0],
                grad_key + terms[1],
                grad_value + terms[2],
            )
    return grad_query, grad_key, grad_value


def fused_kernel(
    tokens,
    cotangent,
    sample_counts,
    feature_counts,
    attn_in_hbm,
    attn_out_hbm,
    norm_gain_hbm,
    norm_bias_hbm,
    mlp_in_hbm,
    mlp_in_bias_hbm,
    mlp_out_hbm,
    mlp_out_bias_hbm,
    mixed,
    tokens_grad,
    sums,
    small,
    attn_in,
    attn_out,
    norm_gain,
    norm_bias,
    mlp_in,
    mlp_in_bias,
    mlp_out,
    mlp_out_bias,
    x_rows,
    normed_one,
    query_one,
    key_one,
    value_one,
    ones_key,
    ones_value,
    attn_one,
    first_send,
    first_recv,
    cot_recv,
    grad_recv,
    normed_two,
    attn_two,
    normed_three,
    active,
    grad_hidden,
    grad_packed,
    grad_low,
    query_two,
    key_two,
    value_two,
    feature_bias,
    key_zero,
    grad_key,
    grad_value,
    head_sum,
    vectors,
    vec_pair,
    vec_grp,
    vec_z,
    part_sum,
    one_sum,
    two_sum,
    three_sum,
    done_sum,
    load_sem,
    first_ss,
    first_rs,
    cot_ss,
    cot_rs,
    mixed_ss,
    mixed_rs,
    grad_ss,
    grad_rs,
    own_sem,
    out_sem,
    sum_ss,
    sum_rs,
    vec_ss,
    vec_rs,
):
    grp = lax.axis_index("grp")
    me = lax.axis_index("swap")
    chip = me // 2
    core = me % 2
    col = grp % 2
    row = grp // 2
    odd = chip % 2
    upper = chip // 2
    samples = sample_counts[0]
    features = feature_counts[0]

    def swap_peer(k):
        return (me + k) % SWAP

    def grp_peer(k):
        return (grp + k) % GRP

    def z_peer(k):
        return ((chip + k) % 4) * 2 + core

    loads = [pltpu.make_async_copy(tokens.at[:, c], x_rows.at[c], load_sem.at[c]) for c in range(CHUNKS)]
    for index, (source, target) in enumerate(
        (
            (attn_in_hbm.at[0], attn_in.at[0]),
            (attn_out_hbm.at[0], attn_out.at[0]),
            (norm_gain_hbm, norm_gain),
            (norm_bias_hbm, norm_bias),
            (mlp_in_bias_hbm, mlp_in_bias),
            (mlp_out_bias_hbm, mlp_out_bias),
            (attn_in_hbm.at[1], attn_in.at[1]),
            (attn_out_hbm.at[1], attn_out.at[1]),
            (mlp_in_hbm, mlp_in),
            (mlp_out_hbm, mlp_out),
        )
    ):
        loads.append(pltpu.make_async_copy(source, target, load_sem.at[CHUNKS + index]))
    for copy in loads:
        copy.start()

    barrier = pltpu.get_barrier_semaphore()
    for k in range(1, SWAP):
        pl.semaphore_signal(barrier, inc=1, device_id={"swap": swap_peer(k)}, device_id_type=MESH)
    for k in range(1, GRP):
        pl.semaphore_signal(barrier, inc=1, device_id={"grp": grp_peer(k)}, device_id_type=MESH)
    pl.semaphore_wait(barrier, SWAP - 1 + GRP - 1)

    others = slice(0, SWAP - 1)

    def exchange(source, target, send, recv):
        def copy(c, d, come, go):
            return pltpu.make_async_remote_copy(
                src_ref=source(c, go),
                dst_ref=target(c, come),
                send_sem=send.at[c],
                recv_sem=recv.at[c],
                device_id={"swap": d},
                device_id_type=MESH,
            )

        def start(c):
            for k in range(1, SWAP):
                copy(c, swap_peer(k), me, swap_peer(k)).start()

        def wait_send(c):
            copy(c, swap_peer(1), others, others).wait_send()

        def wait_recv(c):
            copy(c, swap_peer(1), others, others).wait_recv()

        return start, wait_send, wait_recv

    first_start, first_wait_send, first_wait_recv = exchange(
        lambda c, d: first_send.at[c, d], lambda c, d: first_recv.at[c, d], first_ss, first_rs
    )
    cot_start, cot_wait_send, cot_wait_recv = exchange(
        lambda c, d: cotangent.at[d, c], lambda c, d: cot_recv.at[c, d], cot_ss, cot_rs
    )
    mixed_start, mixed_wait_send, mixed_wait_recv = exchange(
        lambda c, d: first_send.at[c, d], lambda c, d: mixed.at[d, c], mixed_ss, mixed_rs
    )
    grad_start, grad_wait_send, grad_wait_recv = exchange(
        lambda c, d: first_recv.at[c, d], lambda c, d: grad_recv.at[c, d], grad_ss, grad_rs
    )

    def own_cot(c):
        return pltpu.make_async_copy(cotangent.at[me, c], cot_recv.at[c, me], own_sem.at[0, c])

    def own_mixed(c):
        return pltpu.make_async_copy(first_send.at[c, me], mixed.at[me, c], own_sem.at[1, c])

    def cot_begin(c):
        own_cot(c).start()
        cot_start(c)

    cot_begin(0)

    vectors[...] = jnp.zeros((16, WIDTH), F32)
    low_half = lax.broadcasted_iota(jnp.int32, (CHUNKS, BLOCK, 128), 2) < 64
    ones_key[0] = jnp.where(low_half, 1.0, 0.0).astype(BF)
    ones_key[1] = jnp.where(low_half, 0.0, 1.0).astype(BF)
    head_sum[...] = jnp.where(
        ((lax.broadcasted_iota(jnp.int32, (256, 128), 0) // 64) & 1)
        == (lax.broadcasted_iota(jnp.int32, (256, 128), 1) // 64),
        1.0,
        0.0,
    ).astype(BF)
    row_cell = lax.broadcasted_iota(jnp.int32, (BLOCK, BLOCK), 0)
    col_cell = lax.broadcasted_iota(jnp.int32, (BLOCK, BLOCK), 1)
    seen = jnp.logical_and((row_cell % PIECE) == (col_cell % PIECE), (col_cell // PIECE) < features)
    feature_bias[...] = jnp.where(seen, 0.0, MASKED).astype(F32)

    def valid_rows(c):
        row = lax.broadcasted_iota(jnp.int32, (BLOCK, 1), 0)
        return (row // PIECE) * (CHUNKS * PIECE) + c * PIECE + row % PIECE < samples

    def half_of(values, half):
        mine = (lanes(values.shape[0]) < 64) == (half == 0)
        return jnp.where(mine, values, jnp.zeros_like(values))

    def add_row(row, values):
        vectors[row : row + 1, :] += jnp.sum(values, axis=0, keepdims=True)

    def block(ref, c):
        return ref[c].reshape(BLOCK, WIDTH)

    for index in (0, 2, 3):
        loads[CHUNKS + index].wait()

    @pl.loop(0, CHUNKS)
    def _(c):
        pltpu.make_async_copy(tokens.at[:, c], x_rows.at[c], load_sem.at[c]).wait()
        vhat, _ = norm_stats(block(x_rows, c).astype(F32))
        normed = (vhat * norm_gain[0:1, :] + norm_bias[0:1, :]).astype(BF)
        normed_one[c] = normed
        valid = valid_rows(c)
        queries = mm(normed, attn_in[0, :, :WIDTH]) * (SCALE * LOG2E)
        for pair in range(PAIRS):
            query_one[c, pair, :, :128] = queries[:, 128 * pair : 128 * pair + 128].astype(BF)
        keys = mm(normed, attn_in[0, :, WIDTH : 2 * WIDTH])

        @pl.when(c == 0)
        def _():
            key_zero[...] = keys[0:8, :]

        keys = jnp.where(valid, keys, key_zero[0:1, :]).astype(BF)
        values = mm(normed, attn_in[0, :, 2 * WIDTH :])
        values = jnp.where(valid, values, 0.0).astype(BF)
        for head in range(HEADS):
            pair, half = head // 2, head % 2
            cut = slice(128 * pair, 128 * pair + 128)
            key_one[head, c] = half_of(keys[:, cut], half)
            value_one[head, c] = half_of(values[:, cut], half)
        for half in range(2):
            mine = (lanes() < 64) == (half == 0)
            ones_value[half, c] = jnp.where(jnp.logical_and(mine, valid), 1.0, 0.0).astype(BF)

    cells = CHUNKS * BLOCK

    def key_all(head):
        return key_one[head].reshape(cells, 128)

    def key_wide(head):
        return jnp.concatenate([key_all(head), ones_key[head % 2].reshape(cells, 128)], axis=1)

    def value_wide(head):
        return jnp.concatenate(
            [value_one[head].reshape(cells, 128), ones_value[head % 2].reshape(cells, 128)], axis=1
        )

    loads[CHUNKS + 1].wait()

    @pl.loop(0, CHUNKS)
    def _(c):
        def put(pair, out, extra):
            attn_one[c, :, 128 * pair : 128 * pair + 128] = out
            query_one[c, pair, :, 128:] = extra

        attention_forward(
            lambda pair: query_one[c, pair, :, :128], key_all, value_wide, None, put
        )
        first = block(x_rows, c).astype(F32) + mm(attn_one[c], attn_out[0])
        first_send[c] = first.astype(BF).reshape(SWAP, PIECE, WIDTH)
        first_recv[c, me] = first_send[c, me]
        first_start(c)

        @pl.when(c == 1)
        def _():
            cot_begin(1)

    def reduction(number, part, one, two, three, done, cut):
        def remote(source, target, index, where):
            return pltpu.make_async_remote_copy(
                src_ref=source,
                dst_ref=target,
                send_sem=sum_ss.at[number, index],
                recv_sem=sum_rs.at[number, index],
                device_id=where,
                device_id_type=MESH,
            )

        beside = {"grp": grp + 1 - 2 * col}
        above = {"grp": grp + 2 - 4 * row}
        out = sums.at[min(number, SUMS - 1), grp, :, cut]
        step_one = [
            remote(part.at[:, 1 - core, :, :, :, cut], one.at[:, :, :, :, cut], 0, {"swap": me + 1 - 2 * core})
        ]
        step_two = [
            remote(one.at[0:2, :, 1 - col, :, cut], two.at[0, :, :, :, cut], 1, beside),
            remote(one.at[2:4, 1 - row, :, :, cut], two.at[1, :, :, :, cut], 2, above),
        ]
        step_three = [
            remote(one.at[0:2, 1 - row, col, :, cut], two.at[2, 0, :, :, cut], 3, above),
            remote(one.at[2:4, row, 1 - col, :, cut], two.at[2, 1, :, :, cut], 4, beside),
        ]
        step_four = [
            remote(one.at[2 * k + 1 - odd, row, col, :, cut], three.at[k, :, cut], 5 + k, {"swap": me + 2 - 4 * odd})
            for k in range(2)
        ]
        step_five = [
            remote(
                one.at[2 - 2 * upper + odd, row, col, :, cut], three.at[2, :, cut], 7, {"swap": me + 4 - 8 * upper}
            )
        ]
        step_six = [remote(done.at[:, cut], out, 7 + k, {"grp": grp_peer(k)}) for k in range(1, GRP)]
        own = pltpu.make_async_copy(done.at[:, cut], out, sum_rs.at[number, 11])

        def begin():
            for copy in step_one:
                copy.start()

        def after_one():
            for copy in step_one:
                copy.wait_recv()

            @pl.loop(0, 4)
            def _(a):
                total = one[a, :, :, :, cut].astype(F32) + part[a, core, :, :, :, cut].astype(F32)
                one[a, :, :, :, cut] = total.astype(BF)

            for copy in step_two:
                copy.start()

        def after_two():
            for copy in step_two:
                copy.wait_recv()
            for a in range(2):
                total = one[a, :, col, :, cut].astype(F32) + two[0, a, :, :, cut].astype(F32)
                one[a, :, col, :, cut] = total.astype(BF)
                total = one[2 + a, row, :, :, cut].astype(F32) + two[1, a, :, :, cut].astype(F32)
                one[2 + a, row, :, :, cut] = total.astype(BF)
            for copy in step_three:
                copy.start()

        def after_three():
            for copy in step_three:
                copy.wait_recv()
            for a in range(4):
                total = one[a, row, col, :, cut].astype(F32) + two[2, a // 2, a % 2, :, cut].astype(F32)
                one[a, row, col, :, cut] = total.astype(BF)
            for copy in step_four:
                copy.start()

        def after_four():
            for copy in step_four:
                copy.wait_recv()
            for k in range(2):
                total = one[2 * k + odd, row, col, :, cut].astype(F32) + three[k, :, cut].astype(F32)
                one[2 * k + odd, row, col, :, cut] = total.astype(BF)
            for copy in step_five:
                copy.start()

        def after_five():
            for copy in step_five:
                copy.wait_recv()
            total = one[chip, row, col, :, cut].astype(F32) + three[2, :, cut].astype(F32)
            done[:, cut] = total.astype(BF)
            own.start()
            for copy in step_six:
                copy.start()

        def finish():
            own.wait()
            for copy in step_six:
                copy.wait_recv()
            for copy in step_one + step_two + step_three + step_four + step_five + step_six:
                copy.wait_send()

        return [begin, after_one, after_two, after_three, after_four, after_five, finish]

    every = slice(0, WIDTH)
    mid = [
        reduction(
            number,
            part_sum.at[number],
            one_sum.at[number],
            two_sum.at[number],
            three_sum.at[number],
            done_sum.at[number],
            every,
        )
        for number in range(3)
    ]
    end = [
        reduction(
            3 + half,
            mlp_out,
            grad_hidden.at[0],
            grad_hidden.at[1, 0:3],
            grad_hidden.at[2, 0:3, 0, 0],
            grad_hidden.at[3, 0, 0, 0],
            slice(256 * half, 256 * half + 256),
        )
        for half in range(2)
    ]

    def rows_of(ref):
        return ref[...].reshape(cells, WIDTH)

    def shares(values):
        return values.astype(BF).reshape(4, 2, 2, 2, 16, values.shape[1])

    def put_shares(number, piece, tile):
        part_sum[number, :, :, :, :, 16 * piece : 16 * piece + 16, :] = shares(tile)

    def grads_in(part):
        put_shares(0, part, mm(rows_of(normed_three), grad_hidden[part].reshape(cells, WIDTH), TN))

    def grads_out(part):
        tile = mm(active[part].reshape(cells, WIDTH), rows_of(cot_recv), TN)
        part_sum[1, part] = tile.astype(BF).reshape(2, 2, 2, SHARE, WIDTH)

    def wide_grads(part):
        cut = slice(WIDTH * part, WIDTH * part + WIDTH)
        put_shares(2, part, mm(rows_of(normed_two), grad_packed[:, :, cut].reshape(cells, WIDTH), TN))
        if part == 2:
            put_shares(2, 3, mm(rows_of(attn_two), rows_of(grad_low), TN))

    for index in range(4, 10):
        loads[CHUNKS + index].wait()

    def delta_of(grad, out):
        product = grad.astype(F32) * out.astype(F32)
        high = product.astype(BF)
        low = (product - high.astype(F32)).astype(BF)
        return split_three(-mm(jnp.concatenate([high, low], axis=1), head_sum[...]))

    @pl.loop(0, CHUNKS)
    def _(c):
        @pl.when(c == 0)
        def _():
            cot_begin(2)

        @pl.when(c == 1)
        def _():
            cot_begin(3)

        first_wait_recv(c)

        @pl.when(c == 3)
        def _():
            grad_start(1)

        resid_one = block(first_recv, c).astype(F32)
        vhat_two, inverse_two = norm_stats(resid_one)
        normed = (vhat_two * norm_gain[1:2, :] + norm_bias[1:2, :]).astype(BF)
        normed_two[c] = normed
        queries = mm(normed, attn_in[1, :, :WIDTH]) * (SCALE * LOG2E)
        keys = mm(normed, attn_in[1, :, WIDTH : 2 * WIDTH]).astype(BF)
        values = mm(normed, attn_in[1, :, 2 * WIDTH :]).astype(BF)
        for pair in range(PAIRS):
            cut = slice(128 * pair, 128 * pair + 128)
            query_two[pair, :, :128] = queries[:, cut].astype(BF)
            for half in range(2):
                key_two[2 * pair + half, :, :128] = half_of(keys[:, cut], half)
                key_two[2 * pair + half, :, 128:] = ones_key[half, 0]
                value_two[2 * pair + half, :, :128] = half_of(values[:, cut], half)
                value_two[2 * pair + half, :, 128:] = ones_key[half, 0]

        def put(pair, out, extra):
            attn_two[c, :, 128 * pair : 128 * pair + 128] = out
            query_two[pair, :, 128:] = extra

        attention_forward(
            lambda pair: query_two[pair, :, :128],
            lambda head: key_two[head, :, :128],
            lambda head: value_two[head],
            feature_bias[...],
            put,
        )
        second = resid_one + mm(attn_two[c], attn_out[1])
        vhat_three, inverse_three = norm_stats(second)
        normed = (vhat_three * norm_gain[2:3, :] + norm_bias[2:3, :]).astype(BF)
        normed_three[c] = normed
        own_cot(c).wait()
        cot_wait_recv(c)
        cot_low = block(cot_recv, c)
        cot = cot_low.astype(F32)
        add_row(10, cot)

        @pl.when(c == 2)
        def _():
            grad_start(0)


        @pl.when(c == 3)
        def _():
            grad_start(2)

        outcome = second + mlp_out_bias[...]
        grad_normed = jnp.zeros((BLOCK, WIDTH), F32)
        for part in range(4):
            cut = slice(WIDTH * part, WIDTH * part + WIDTH)
            hidden = mm(normed, mlp_in[:, cut]) + mlp_in_bias[:, cut]
            weight_out = mlp_out[part].reshape(WIDTH, WIDTH)
            grad_active = mm(cot_low, weight_out, NT)
            below = 0.5 + 0.5 * lax.erf(hidden * 0.7071067811865476)
            act = (hidden * below).astype(BF)
            density = jnp.exp2(hidden * hidden * (-0.5 * LOG2E)) * 0.3989422804014327
            grad_hid = ((below + hidden * density) * grad_active).astype(BF)
            active[part, c] = act
            grad_hidden[part, c] = grad_hid.reshape(2, 2, SHARE, WIDTH)
            add_row(6 + part, grad_hid.astype(F32))
            outcome = outcome + mm(act, weight_out)
            grad_normed = grad_normed + mm(grad_hid, mlp_in[:, cut], NT)

        @pl.when(c == CHUNKS - 1)
        def _():
            for part in range(4):
                grads_in(part)
            mid[0][0]()
            for part in range(4):
                grads_out(part)
            mid[1][0]()

        first_wait_send(c)
        first_send[c] = outcome.astype(BF).reshape(SWAP, PIECE, WIDTH)
        add_row(2, grad_normed * vhat_three)
        add_row(5, grad_normed)
        grad_second = cot + norm_back(grad_normed, vhat_three, inverse_three, norm_gain[2:3, :])
        grad_second_low = grad_second.astype(BF)
        grad_low[c] = grad_second_low
        grad_attn = mm(grad_second_low, attn_out[1], NT).astype(BF)
        for pair in range(PAIRS):
            cut = slice(128 * pair, 128 * pair + 128)
            piece = grad_attn[:, cut]
            wide = jnp.concatenate([piece, delta_of(piece, attn_two[c, :, cut])], axis=1)
            grad_q, grad_k, grad_v = attention_back(
                query_two[pair],
                wide,
                lambda half: key_two[2 * pair + half],
                lambda half: value_two[2 * pair + half],
                feature_bias[...],
            )
            grad_packed[c, :, 128 * pair : 128 * pair + 128] = (grad_q * SCALE).astype(BF)
            grad_packed[c, :, WIDTH + 128 * pair : WIDTH + 128 * pair + 128] = (grad_k * LN2).astype(BF)
            grad_packed[c, :, 2 * WIDTH + 128 * pair : 2 * WIDTH + 128 * pair + 128] = grad_v.astype(BF)
        grad_normed = mm(grad_packed[c], attn_in[1], NT)
        add_row(1, grad_normed * vhat_two)
        add_row(4, grad_normed)
        grad_first = grad_second + norm_back(grad_normed, vhat_two, inverse_two, norm_gain[1:2, :])
        first_recv[c] = grad_first.astype(BF).reshape(SWAP, PIECE, WIDTH)
        grad_recv[c, me] = first_recv[c, me]
        own_mixed(c).start()

        @pl.when(c == CHUNKS - 1)
        def _():
            grad_start(c)

    mid[0][1]()

    for part in range(3):
        wide_grads(part)
    mid[2][0]()
    mid[1][1]()

    def run(hooks, c):
        for when, call in hooks:

            @pl.when(c == when)
            def _():
                call()

    hooks = (
        (),
        ((0, mid[2][1]), (2, mid[0][2]), (3, mid[1][2]), ),
        (),
        ((0, mid[2][2]), (1, mid[0][3]), (1, end[0][1]), (2, mid[1][3]), (3, mid[0][4]), (3, mid[2][3]), (3, end[0][2]), ),
        ((0, mid[1][4]), (0, end[1][1]), (1, mid[0][5]), (1, mid[2][4]), (2, end[0][3]), (2, end[1][2]), (3, mid[1][5]), ),
    )
    for half in range(2):
        pairs = (2 * half, 2 * half + 1)
        grad_key[...] = jnp.zeros((2, cells, 128), F32)
        grad_value[...] = jnp.zeros((2, cells, 128), F32)

        @pl.loop(0, CHUNKS)
        def _(c):
            if half == 0:
                grad_wait_recv(c)
                mixed_start(c)
                grad_attn = mm(block(grad_recv, c), attn_out[0], NT).astype(BF)
                for pair in range(PAIRS):
                    cut = slice(128 * pair, 128 * pair + 128)
                    piece = grad_attn[:, cut]
                    active[pair, c, :, :128] = piece
                    active[pair, c, :, 128:256] = delta_of(piece, attn_one[c, :, cut])
            for pair in pairs:
                grad_q, grad_k, grad_v = attention_back(
                    query_one[c, pair],
                    active[pair, c, :, :256],
                    lambda side: key_wide(2 * pair + side),
                    lambda side: value_wide(2 * pair + side),
                    None,
                )
                grad_packed[c, :, 128 * pair : 128 * pair + 128] = (grad_q * SCALE).astype(BF)
                grad_key[pair % 2] += grad_k
                grad_value[pair % 2] += grad_v
                run(hooks[pair], c)

        for pair in pairs:
            for c in range(CHUNKS):
                rows = slice(BLOCK * c, BLOCK * c + BLOCK)
                grad_packed[c, :, WIDTH + 128 * pair : WIDTH + 128 * pair + 128] = (
                    grad_key[pair % 2, rows, :] * LN2
                ).astype(BF)
                grad_packed[c, :, 2 * WIDTH + 128 * pair : 2 * WIDTH + 128 * pair + 128] = jnp.where(
                    valid_rows(c), grad_value[pair % 2, rows, :], 0.0
                ).astype(BF)
        if half == 0:
            grad_rows = grad_recv[...].reshape(cells, WIDTH)
            mlp_out[:, :, :, :, 0:16, :] = shares(mm(rows_of(attn_one), grad_rows, TN))
        for part in range(3):
            cut = slice(WIDTH * part + 256 * half, WIDTH * part + 256 * half + 256)
            tile = mm(rows_of(normed_one), grad_packed[:, :, cut].reshape(cells, 256), TN)
            mlp_out[:, :, :, :, 16 + 16 * part : 32 + 16 * part, 256 * half : 256 * half + 256] = shares(tile)
        end[half][0]()

    @pl.loop(0, CHUNKS)
    def _(c):
        grad_normed = mm(grad_packed[c], attn_in[0], NT)
        vhat, inverse = norm_stats(block(x_rows, c).astype(F32))
        add_row(0, grad_normed * vhat)
        add_row(3, grad_normed)
        result = block(grad_recv, c).astype(F32) + norm_back(grad_normed, vhat, inverse, norm_gain[0:1, :])
        normed_one[c] = result.astype(BF)
        pltpu.make_async_copy(
            normed_one.at[c].reshape(SWAP, PIECE, WIDTH), tokens_grad.at[:, c], out_sem.at[c]
        ).start()
        run(hooks[4], c)

    def vec_copy(source, target, index, where):
        return pltpu.make_async_remote_copy(
            src_ref=source,
            dst_ref=target,
            send_sem=vec_ss.at[index],
            recv_sem=vec_rs.at[index],
            device_id=where,
            device_id_type=MESH,
        )

    vec_one = vec_copy(vectors, vec_pair, 0, {"swap": me + 1 - 2 * core})
    vec_two = [vec_copy(vec_grp.at[grp], vec_grp.at[grp], k, {"grp": grp_peer(k)}) for k in range(1, GRP)]
    vec_two_in = [
        vec_copy(vec_grp.at[grp_peer(-k)], vec_grp.at[grp_peer(-k)], k, {"grp": grp_peer(-k)}) for k in range(1, GRP)
    ]
    vec_three = [vec_copy(vec_z.at[chip], vec_z.at[chip], 3 + k, {"swap": z_peer(k)}) for k in range(1, 4)]
    vec_three_in = [
        vec_copy(vec_z.at[(chip - k) % 4], vec_z.at[(chip - k) % 4], 3 + k, {"swap": z_peer(-k)}) for k in range(1, 4)
    ]
    vec_one.start()
    mid[2][5]()
    end[0][4]()
    end[1][3]()
    vec_one.wait_recv()
    vec_grp[grp] = vectors[...] + vec_pair[...]
    for copy in vec_two:
        copy.start()
    end[0][5]()
    end[1][4]()
    for copy in vec_two_in:
        copy.wait_recv()
    vec_z[chip] = (vec_grp[0] + vec_grp[1]) + (vec_grp[2] + vec_grp[3])
    for copy in vec_three:
        copy.start()
    end[1][5]()
    for copy in vec_three_in:
        copy.wait_recv()
    whole = (vec_z[0] + vec_z[1]) + (vec_z[2] + vec_z[3])

    def share(rows, width, step):
        result = None
        for index in range(WIDTH // width):
            piece = whole[rows, index * width : index * width + width]
            mine = step == index
            result = jnp.where(mine, piece, 0.0 if result is None else result)
        return result

    small[0:3, 0:64] = share(slice(0, 3), 64, me)
    small[3:6, 0:64] = share(slice(3, 6), 64, me)
    bias_row = None
    for index in range(4):
        piece = share(slice(6 + index, 7 + index), 256, core)
        bias_row = jnp.where(chip == index, piece, 0.0 if bias_row is None else bias_row)
    small[6:7, :] = bias_row
    small[7:8, 0:64] = share(slice(10, 11), 64, me)

    for steps in mid + end:
        steps[6]()
    vec_one.wait_send()
    for copy in vec_two + vec_three:
        copy.wait_send()

    @pl.loop(0, CHUNKS)
    def _(c):
        own_mixed(c).wait()
        mixed_wait_recv(c)
        mixed_wait_send(c)
        cot_wait_send(c)
        grad_wait_send(c)
        pltpu.make_async_copy(
            normed_one.at[c].reshape(SWAP, PIECE, WIDTH), tokens_grad.at[:, c], out_sem.at[c]
        ).wait()


def finish_kernel(mixed, tokens_grad, sums_hbm, small_hbm, *refs):
    outs, (sums, small, held, sem) = refs[:10], refs[10:]
    loads = [pltpu.make_async_copy(sums_hbm.at[k], sums.at[k], sem.at[k]) for k in range(SUMS)]
    loads.append(pltpu.make_async_copy(small_hbm, small, sem.at[SUMS]))
    cells_in, cells_out = [], []
    for index, source in enumerate((mixed, tokens_grad)):
        for half in range(2):
            part = slice(4 * half, 4 * half + 4)
            place = SUMS + 1 + 2 * index + half
            cells_in.append(pltpu.make_async_copy(source.at[part], held.at[index, part], sem.at[place]))
            cells_out.append(pltpu.make_async_copy(held.at[index, part], outs[index].at[part], sem.at[place + 4]))
    for copy in cells_in + loads:
        copy.start()
    for before, after in zip(cells_in, cells_out):
        before.wait()
        after.start()
    for copy in loads:
        copy.wait()
    for grp in range(GRP):
        rows = slice(16 * grp, 16 * grp + 16)
        for part in range(4):
            cut = slice(WIDTH * part, WIDTH * part + WIDTH)
            piece = slice(16 * part, 16 * part + 16)
            outs[6][rows, cut] = sums[0, grp, piece].astype(F32)
            if part < 3:
                outs[2][1, rows, cut] = sums[2, grp, piece].astype(F32)
                outs[2][0, rows, cut] = sums[3, grp, 16 * part + 16 : 16 * part + 32].astype(F32)
        outs[8][SHARE * grp : SHARE * grp + SHARE] = sums[1, grp].astype(F32)
        outs[3][1, rows] = sums[2, grp, 48:64].astype(F32)
        outs[3][0, rows] = sums[3, grp, 0:16].astype(F32)
    outs[4][...] = small[0:3, 0:64]
    outs[5][...] = small[3:6, 0:64]
    outs[7][...] = small[6:7, 0:256]
    outs[9][...] = small[7:8, 0:64]
    for copy in cells_out:
        copy.wait()


def fused_local(
    tokens,
    sample_counts,
    feature_counts,
    attn_in,
    attn_out,
    norm_gain,
    norm_bias,
    mlp_in,
    mlp_in_bias,
    mlp_out,
    mlp_out_bias,
    cotangent,
):
    cells = (SWAP, CHUNKS, PIECE, WIDTH)
    blocks = (CHUNKS, SWAP, PIECE, WIDTH)
    rows = (CHUNKS, BLOCK, WIDTH)
    anywhere = pl.BlockSpec(memory_space=pl.ANY)
    scalar = pl.BlockSpec(memory_space=pltpu.SMEM)
    vector = pl.BlockSpec(memory_space=pltpu.VMEM)
    sem = pltpu.SemaphoreType.DMA

    def buffer(*shape, kind=BF):
        return pltpu.VMEM(shape, kind)

    def result(shape, kind=F32):
        return jax.ShapeDtypeStruct(shape, kind)

    mixed, tokens_grad, sums, small = pl.pallas_call(
        fused_kernel,
        name="layer",
        out_shape=(
            result(cells, BF),
            result(cells, BF),
            result((SUMS, GRP, SHARE, WIDTH), BF),
            result((8, 256)),
        ),
        in_specs=[anywhere, anywhere, scalar, scalar] + [anywhere] * 8,
        out_specs=(anywhere, anywhere, anywhere, vector),
        scratch_shapes=[
            buffer(2, WIDTH, 3 * WIDTH),
            buffer(2, WIDTH, WIDTH),
            buffer(3, WIDTH, kind=F32),
            buffer(3, WIDTH, kind=F32),
            buffer(WIDTH, 4 * WIDTH),
            buffer(1, 4 * WIDTH, kind=F32),
            buffer(4, 2, 2, 2, SHARE, WIDTH),
            buffer(1, WIDTH, kind=F32),
            buffer(*blocks),
            buffer(*rows),
            buffer(CHUNKS, PAIRS, BLOCK, 256),
            buffer(HEADS, CHUNKS, BLOCK, 128),
            buffer(HEADS, CHUNKS, BLOCK, 128),
            buffer(2, CHUNKS, BLOCK, 128),
            buffer(2, CHUNKS, BLOCK, 128),
            buffer(*rows),
            buffer(*blocks),
            buffer(*blocks),
            buffer(*blocks),
            buffer(*blocks),
            buffer(*rows),
            buffer(*rows),
            buffer(*rows),
            buffer(4, *rows),
            buffer(4, CHUNKS, 2, 2, SHARE, WIDTH),
            buffer(CHUNKS, BLOCK, 3 * WIDTH),
            buffer(*rows),
            buffer(PAIRS, BLOCK, 256),
            buffer(HEADS, BLOCK, 256),
            buffer(HEADS, BLOCK, 256),
            buffer(BLOCK, BLOCK, kind=F32),
            buffer(8, WIDTH, kind=F32),
            buffer(2, CHUNKS * BLOCK, 128, kind=F32),
            buffer(2, CHUNKS * BLOCK, 128, kind=F32),
            buffer(256, 128),
            buffer(16, WIDTH, kind=F32),
            buffer(16, WIDTH, kind=F32),
            buffer(GRP, 16, WIDTH, kind=F32),
            buffer(4, 16, WIDTH, kind=F32),
            buffer(3, 4, 2, 2, 2, SHARE, WIDTH),
            buffer(3, 4, 2, 2, SHARE, WIDTH),
            buffer(3, 3, 2, 2, SHARE, WIDTH),
            buffer(3, 3, SHARE, WIDTH),
            buffer(3, SHARE, WIDTH),
            sem((CHUNKS + 10,)),
        ]
        + [sem((CHUNKS,))] * 8
        + [sem((2, CHUNKS)), sem((CHUNKS,))]
        + [sem((5, 12))] * 2
        + [sem((7,))] * 2,
        compiler_params=pltpu.CompilerParams(
            collective_id=0, has_side_effects=True, vmem_limit_bytes=VMEM_LIMIT
        ),
    )(
        tokens.reshape(cells),
        cotangent.reshape(cells),
        sample_counts,
        feature_counts,
        attn_in,
        attn_out,
        norm_gain,
        norm_bias,
        mlp_in,
        mlp_in_bias.reshape(1, -1),
        mlp_out.reshape(4, 2, 2, 2, SHARE, WIDTH),
        mlp_out_bias.reshape(1, -1),
    )
    shapes = (
        result(cells, BF),
        result(cells, BF),
        result((2, 64, 3 * WIDTH)),
        result((2, 64, WIDTH)),
        result((3, 64)),
        result((3, 64)),
        result((64, 4 * WIDTH)),
        result((1, 256)),
        result((256, WIDTH)),
        result((1, 64)),
    )
    outs = pl.pallas_call(
        finish_kernel,
        name="results",
        out_shape=shapes,
        in_specs=[anywhere] * 4,
        out_specs=(anywhere, anywhere) + (vector,) * 8,
        scratch_shapes=[
            buffer(SUMS, GRP, SHARE, WIDTH),
            buffer(8, 256, kind=F32),
            buffer(2, *cells),
            sem((SUMS + 9,)),
        ],
        compiler_params=pltpu.CompilerParams(vmem_limit_bytes=VMEM_LIMIT),
    )(mixed, tokens_grad, sums, small)
    return (
        outs[0].reshape(tokens.shape),
        outs[1].reshape(tokens.shape),
        *outs[2:7],
        outs[7].reshape(-1),
        outs[8],
        outs[9].reshape(-1),
    )


def solution(mesh):
    placed = (
        P("grp", None, "swap", None),
        P("grp"),
        P("grp"),
        P(),
        P(),
        P(),
        P(),
        P(),
        P(),
        P(),
        P(),
        P("grp", None, "swap", None),
    )
    def layer(*args):
        tokens, mlp_in = args[0], args[7]
        fits = (
            (mesh.shape["swap"], mesh.shape["grp"]) == (SWAP, GRP)
            and tokens.shape == (1, CHUNKS * BLOCK, 1, WIDTH)
            and mlp_in.shape == (WIDTH, 4 * WIDTH)
        )
        return fused_local(*args) if fits else local(*args)

    return jax.shard_map(
        layer,
        mesh=mesh,
        in_specs=placed,
        out_specs=(
            P("grp", None, "swap", None),
            P("grp", None, "swap", None),
            P(None, "swap", None),
            P(None, "swap", None),
            P(None, "swap"),
            P(None, "swap"),
            P("swap", None),
            P("swap"),
            P("swap", None),
            P("swap"),
        ),
        check_vma=False,
    )
```

```python
import jax
import jax.numpy as jnp
from jax import lax
from jax.experimental import pallas as pl
from jax.experimental.pallas import tpu as pltpu
from jax.sharding import PartitionSpec as P

HEADS = 8
HEAD_DIM = 64


EPSILON = 1e-05
MASKED = -1e30
SAMPLE_FORMS = ("tqfhe,tkfhe->tfhqk", "tfhqk,tkfhe->tqfhe", "tfhqk,tqfhe->tkfhe")
FEATURE_FORMS = ("tsqhe,tskhe->tshqk", "tshqk,tskhe->tsqhe", "tshqk,tsqhe->tskhe")


def layer_norm(values, factor, offset):
    centre = values - jnp.mean(values, axis=-1, keepdims=True)
    spread = jnp.mean(centre * centre, axis=-1, keepdims=True)
    return centre * lax.rsqrt(spread + EPSILON) * factor + offset


def exact_gelu(values):
    return jax.nn.gelu(values, approximate=False)


def project(left, weight):
    return jnp.dot(left, weight, preferred_element_type=jnp.float32)


def project_back(grad_rows, weight):
    return jnp.einsum("...c,dc->...d", grad_rows, weight, preferred_element_type=jnp.float32)


def weight_grad(left, grad_rows):
    return jnp.einsum(
        "nd,nc->dc",
        left.reshape(-1, left.shape[-1]),
        grad_rows.reshape(-1, grad_rows.shape[-1]),
        preferred_element_type=jnp.float32,
    )


def split_heads(packed):
    leading = packed.shape[:-1]
    model_width = packed.shape[-1] // 3
    query_rows = packed[..., :model_width].reshape(leading + (HEADS, HEAD_DIM))
    key_rows = packed[..., model_width : 2 * model_width].reshape(leading + (HEADS, HEAD_DIM))
    value_rows = packed[..., 2 * model_width :].reshape(leading + (HEADS, HEAD_DIM))
    return (query_rows, key_rows, value_rows)


def masked_scores(query_rows, key_rows, valid, forms):
    raw_scores = jnp.einsum(
        forms[0], query_rows, key_rows, preferred_element_type=jnp.float32
    ) * HEAD_DIM ** (-0.5)
    return jnp.where(valid[:, None, None, None, :], raw_scores, MASKED)


def attend(packed, valid, forms):
    leading = packed.shape[:-1]
    query_rows, key_rows, value_rows = split_heads(packed)
    scores = masked_scores(query_rows, key_rows, valid, forms)
    row_max = jnp.max(scores, axis=-1, keepdims=True)
    exponent = jnp.exp(scores - row_max)
    row_total = jnp.sum(exponent, axis=-1, keepdims=True)
    probability = (exponent / row_total).astype(jnp.bfloat16)
    mixed_rows = jnp.einsum(forms[1], probability, value_rows, preferred_element_type=jnp.float32)
    return (mixed_rows.reshape(leading + (packed.shape[-1] // 3,)), row_max + jnp.log(row_total))


def attend_back(packed, valid, log_total, grad_out, forms):
    leading = packed.shape[:-1]
    model_width = packed.shape[-1] // 3
    query_rows, key_rows, value_rows = split_heads(packed)
    grad_rows = grad_out.reshape(leading + (HEADS, HEAD_DIM))
    scores = masked_scores(query_rows, key_rows, valid, forms)
    probability = jnp.exp(scores - log_total)
    grad_values = jnp.einsum(
        forms[2], probability.astype(jnp.bfloat16), grad_rows, preferred_element_type=jnp.float32
    )
    grad_probs = jnp.einsum(forms[0], grad_rows, value_rows, preferred_element_type=jnp.float32)
    inner_sum = jnp.sum(probability * grad_probs, axis=-1, keepdims=True)
    grad_scores = (probability * (grad_probs - inner_sum)).astype(jnp.bfloat16)
    grad_query = jnp.einsum(
        forms[1], grad_scores, key_rows, preferred_element_type=jnp.float32
    ) * HEAD_DIM ** (-0.5)
    grad_keys = jnp.einsum(
        forms[2], grad_scores, query_rows, preferred_element_type=jnp.float32
    ) * HEAD_DIM ** (-0.5)
    return jnp.concatenate(
        [
            grad_query.reshape(leading + (model_width,)).astype(jnp.bfloat16),
            grad_keys.reshape(leading + (model_width,)).astype(jnp.bfloat16),
            grad_values.reshape(leading + (model_width,)).astype(jnp.bfloat16),
        ],
        axis=-1,
    )


def local(
    tokens,
    sample_counts,
    feature_counts,
    attn_in,
    attn_out,
    norm_gain,
    norm_bias,
    mlp_in,
    mlp_in_bias,
    mlp_out,
    mlp_out_bias,
    cotangent,
):
    samples = tokens.shape[1]
    sample_valid = jnp.arange(samples, dtype=jnp.int32)[None, :] < sample_counts[:, None]
    inputs = tokens.astype(jnp.float32)
    norm_one, back_one = jax.vjp(layer_norm, inputs, norm_gain[0], norm_bias[0])
    normed_one = norm_one.astype(jnp.bfloat16)
    packed_one = project(normed_one, attn_in[0]).astype(jnp.bfloat16)
    attn_one, log_total_one = attend(packed_one, sample_valid, SAMPLE_FORMS)
    attn_one = attn_one.astype(jnp.bfloat16)
    first_resid = (inputs + project(attn_one, attn_out[0])).astype(jnp.bfloat16)
    moved_rows = lax.all_to_all(first_resid, "swap", split_axis=1, concat_axis=2, tiled=True)
    features = moved_rows.shape[2]
    feature_valid = jnp.arange(features, dtype=jnp.int32)[None, :] < feature_counts[:, None]
    resid_one = moved_rows.astype(jnp.float32)
    norm_two, back_two = jax.vjp(layer_norm, resid_one, norm_gain[1], norm_bias[1])
    normed_two = norm_two.astype(jnp.bfloat16)
    packed_two = project(normed_two, attn_in[1]).astype(jnp.bfloat16)
    attn_two, log_total_two = attend(packed_two, feature_valid, FEATURE_FORMS)
    attn_two = attn_two.astype(jnp.bfloat16)
    resid_two = resid_one + project(attn_two, attn_out[1])
    norm_three, back_three = jax.vjp(layer_norm, resid_two, norm_gain[2], norm_bias[2])
    normed_three = norm_three.astype(jnp.bfloat16)
    hidden = project(normed_three, mlp_in) + mlp_in_bias
    activated, back_gelu = jax.vjp(exact_gelu, hidden)
    active_low = activated.astype(jnp.bfloat16)
    outcome = (resid_two + project(active_low, mlp_out) + mlp_out_bias).astype(jnp.bfloat16)
    mixed_out = lax.all_to_all(outcome, "swap", split_axis=2, concat_axis=1, tiled=True)
    grad_out = lax.all_to_all(cotangent, "swap", split_axis=1, concat_axis=2, tiled=True)
    grad_three = grad_out.astype(jnp.float32)
    grad_mlp_out = weight_grad(active_low, grad_out)
    grad_mlp_out_bias = jnp.sum(grad_three.reshape(-1, grad_three.shape[-1]), axis=0)
    grad_active = project_back(grad_out, mlp_out)
    grad_hidden = back_gelu(grad_active)[0].astype(jnp.bfloat16)
    grad_mlp_in = weight_grad(normed_three, grad_hidden)
    grad_mlp_in_bias = jnp.sum(
        grad_hidden.astype(jnp.float32).reshape(-1, grad_hidden.shape[-1]), axis=0
    )
    grad_resid, gain_three, offset_three = back_three(project_back(grad_hidden, mlp_in))
    grad_second = grad_three + grad_resid
    grad_second_low = grad_second.astype(jnp.bfloat16)
    grad_attn_out_two = weight_grad(attn_two, grad_second_low)
    grad_attn_two = project_back(grad_second_low, attn_out[1]).astype(jnp.bfloat16)
    grad_packed_two = attend_back(
        packed_two, feature_valid, log_total_two, grad_attn_two, FEATURE_FORMS
    )
    grad_attn_in_two = weight_grad(normed_two, grad_packed_two)
    grad_resid_two, gain_two, offset_two = back_two(project_back(grad_packed_two, attn_in[1]))
    grad_first = (grad_second + grad_resid_two).astype(jnp.bfloat16)
    grad_back = lax.all_to_all(grad_first, "swap", split_axis=2, concat_axis=1, tiled=True)
    grad_attn_out_one = weight_grad(attn_one, grad_back)
    grad_attn_one = project_back(grad_back, attn_out[0]).astype(jnp.bfloat16)
    grad_packed_one = attend_back(
        packed_one, sample_valid, log_total_one, grad_attn_one, SAMPLE_FORMS
    )
    grad_attn_in_one = weight_grad(normed_one, grad_packed_one)
    grad_input, gain_one, offset_one = back_one(project_back(grad_packed_one, attn_in[0]))
    tokens_grad = (grad_back.astype(jnp.float32) + grad_input).astype(jnp.bfloat16)
    stack_in = jnp.stack([grad_attn_in_one, grad_attn_in_two])
    stack_out = jnp.stack([grad_attn_out_one, grad_attn_out_two])
    stack_gain = jnp.stack([gain_one, gain_two, gain_three])
    stack_offset = jnp.stack([offset_one, offset_two, offset_three])
    (
        part_in,
        part_out,
        part_gain,
        part_offset,
        part_mlp_in,
        part_mlp_in_bias,
        part_mlp_out,
        part_mlp_out_bias,
    ) = (
        lax.psum_scatter(stack_in, "swap", scatter_dimension=1, tiled=True),
        lax.psum_scatter(stack_out, "swap", scatter_dimension=1, tiled=True),
        lax.psum_scatter(stack_gain, "swap", scatter_dimension=1, tiled=True),
        lax.psum_scatter(stack_offset, "swap", scatter_dimension=1, tiled=True),
        lax.psum_scatter(grad_mlp_in, "swap", scatter_dimension=0, tiled=True),
        lax.psum_scatter(grad_mlp_in_bias, "swap", scatter_dimension=0, tiled=True),
        lax.psum_scatter(grad_mlp_out, "swap", scatter_dimension=0, tiled=True),
        lax.psum_scatter(grad_mlp_out_bias, "swap", scatter_dimension=0, tiled=True),
    )
    (
        share_in,
        share_out,
        share_gain,
        share_offset,
        share_mlp_in,
        share_mlp_in_bias,
        share_mlp_out,
        share_mlp_out_bias,
    ) = (
        lax.psum(part_in.astype(jnp.bfloat16), "grp").astype(jnp.float32),
        lax.psum(part_out.astype(jnp.bfloat16), "grp").astype(jnp.float32),
        lax.psum(part_gain.astype(jnp.bfloat16), "grp").astype(jnp.float32),
        lax.psum(part_offset.astype(jnp.bfloat16), "grp").astype(jnp.float32),
        lax.psum(part_mlp_in.astype(jnp.bfloat16), "grp").astype(jnp.float32),
        lax.psum(part_mlp_in_bias.astype(jnp.bfloat16), "grp").astype(jnp.float32),
        lax.psum(part_mlp_out.astype(jnp.bfloat16), "grp").astype(jnp.float32),
        lax.psum(part_mlp_out_bias.astype(jnp.bfloat16), "grp").astype(jnp.float32),
    )
    return (
        mixed_out,
        tokens_grad,
        share_in,
        share_out,
        share_gain,
        share_offset,
        share_mlp_in,
        share_mlp_in_bias,
        share_mlp_out,
        share_mlp_out_bias,
    )


MESH = pl.DeviceIdType.MESH
VMEM_LIMIT = 60 * 1024 * 1024
SCALE = HEAD_DIM ** (-0.5)
LOG2E = 1.4426950408889634
LN2 = 0.6931471805599453
BF = jnp.bfloat16
F32 = jnp.float32
NT = (((1,), (1,)), ((), ()))
NN = (((1,), (0,)), ((), ()))
TN = (((0,), (0,)), ((), ()))
CHUNKS = 4
BLOCK = 256
SWAP = 8
GRP = 4
PIECE = BLOCK // SWAP
PAIRS = 4
WIDTH = 512
SHARE = 64
SUMS = 4


def mm(left, right, form=NN):
    return lax.dot_general(left, right, form, preferred_element_type=F32)


def norm_stats(values):
    centre = values - jnp.mean(values, axis=-1, keepdims=True)
    inverse = lax.rsqrt(jnp.mean(centre * centre, axis=-1, keepdims=True) + EPSILON)
    return centre * inverse, inverse


def norm_back(grad, vhat, inverse, gain):
    scaled = grad * gain
    mean_one = jnp.mean(scaled, axis=-1, keepdims=True)
    mean_two = jnp.mean(scaled * vhat, axis=-1, keepdims=True)
    return inverse * (scaled - mean_one - vhat * mean_two)


def lanes(rows=BLOCK):
    return lax.broadcasted_iota(jnp.int32, (rows, 128), 1)


def split_three(values):
    high = values.astype(BF).astype(F32)
    rest = values - high
    middle = rest.astype(BF).astype(F32)
    low = rest - middle
    place = lanes(values.shape[0]) & 63
    terms = jnp.where(place == 0, high, jnp.where(place == 1, middle, jnp.where(place == 2, low, 0.0)))
    return terms.astype(BF)


def attention_forward(query, key, value, bias, put):
    def score(head):
        raw = mm(query(head // 2), key(head), NT)
        return raw if bias is None else raw + bias

    current = score(0)
    for pair in range(PAIRS):
        total = None
        tops = []
        for half in range(2):
            head = 2 * pair + half
            following = score(head + 1) if head + 1 < HEADS else None
            top = jnp.max(current, axis=-1, keepdims=True)
            weight = jnp.exp2(current - top).astype(BF)
            term = mm(weight, value(head))
            total = term if total is None else total + term
            tops.append(top)
            current = following
        row_total = total[:, 128:]
        out = (total[:, :128] / row_total).astype(BF)
        top_pair = jnp.where(lanes() < 64, tops[0], tops[1])
        put(pair, out, split_three(-(top_pair + jnp.log(row_total) * LOG2E)))


def attention_back(query, grad, key, value, bias):
    left = lanes() < 64
    grad_query = grad_key = grad_value = None
    for half in range(2):
        keys = key(half)
        score = mm(query, keys, NT)
        if bias is not None:
            score = score + bias
        weight = jnp.exp2(score)
        slope = mm(grad, value(half), NT)
        grad_score = (weight * slope).astype(BF)
        weight = weight.astype(BF)
        mine = left if half == 0 else jnp.logical_not(left)
        nothing = jnp.zeros((BLOCK, 128), BF)
        terms = (
            mm(grad_score, keys[:, :128]),
            mm(grad_score, jnp.where(mine, query[:, :128], nothing), TN),
            mm(weight, jnp.where(mine, grad[:, :128], nothing), TN),
        )
        if half == 0:
            grad_query, grad_key, grad_value = terms
        else:
            grad_query, grad_key, grad_value = (
                grad_query + terms[0],
                grad_key + terms[1],
                grad_value + terms[2],
            )
    return grad_query, grad_key, grad_value


def fused_kernel(
    tokens,
    cotangent,
    sample_counts,
    feature_counts,
    attn_in_hbm,
    attn_out_hbm,
    norm_gain_hbm,
    norm_bias_hbm,
    mlp_in_hbm,
    mlp_in_bias_hbm,
    mlp_out_hbm,
    mlp_out_bias_hbm,
    mixed,
    tokens_grad,
    sums,
    small,
    attn_in,
    attn_out,
    norm_gain,
    norm_bias,
    mlp_in,
    mlp_in_bias,
    mlp_out,
    mlp_out_bias,
    x_rows,
    normed_one,
    query_one,
    key_one,
    value_one,
    ones_key,
    ones_value,
    attn_one,
    first_send,
    first_recv,
    cot_recv,
    grad_recv,
    normed_two,
    attn_two,
    normed_three,
    active,
    grad_hidden,
    grad_packed,
    grad_low,
    query_two,
    key_two,
    value_two,
    feature_bias,
    key_zero,
    grad_key,
    grad_value,
    head_sum,
    vectors,
    vec_pair,
    vec_grp,
    vec_z,
    part_sum,
    one_sum,
    two_sum,
    three_sum,
    done_sum,
    load_sem,
    first_ss,
    first_rs,
    cot_ss,
    cot_rs,
    mixed_ss,
    mixed_rs,
    grad_ss,
    grad_rs,
    own_sem,
    out_sem,
    sum_ss,
    sum_rs,
    vec_ss,
    vec_rs,
):
    grp = lax.axis_index("grp")
    me = lax.axis_index("swap")
    chip = me // 2
    core = me % 2
    col = grp % 2
    row = grp // 2
    odd = chip % 2
    upper = chip // 2
    samples = sample_counts[0]
    features = feature_counts[0]

    def swap_peer(k):
        return (me + k) % SWAP

    def grp_peer(k):
        return (grp + k) % GRP

    def z_peer(k):
        return ((chip + k) % 4) * 2 + core

    loads = [pltpu.make_async_copy(tokens.at[:, c], x_rows.at[c], load_sem.at[c]) for c in range(CHUNKS)]
    for index, (source, target) in enumerate(
        (
            (attn_in_hbm.at[0], attn_in.at[0]),
            (attn_out_hbm.at[0], attn_out.at[0]),
            (norm_gain_hbm, norm_gain),
            (norm_bias_hbm, norm_bias),
            (mlp_in_bias_hbm, mlp_in_bias),
            (mlp_out_bias_hbm, mlp_out_bias),
            (attn_in_hbm.at[1], attn_in.at[1]),
            (attn_out_hbm.at[1], attn_out.at[1]),
            (mlp_in_hbm, mlp_in),
            (mlp_out_hbm, mlp_out),
        )
    ):
        loads.append(pltpu.make_async_copy(source, target, load_sem.at[CHUNKS + index]))
    for copy in loads:
        copy.start()

    barrier = pltpu.get_barrier_semaphore()
    for k in range(1, SWAP):
        pl.semaphore_signal(barrier, inc=1, device_id={"swap": swap_peer(k)}, device_id_type=MESH)
    for k in range(1, GRP):
        pl.semaphore_signal(barrier, inc=1, device_id={"grp": grp_peer(k)}, device_id_type=MESH)
    pl.semaphore_wait(barrier, SWAP - 1 + GRP - 1)

    others = slice(0, SWAP - 1)

    def exchange(source, target, send, recv):
        def copy(c, d, come, go):
            return pltpu.make_async_remote_copy(
                src_ref=source(c, go),
                dst_ref=target(c, come),
                send_sem=send.at[c],
                recv_sem=recv.at[c],
                device_id={"swap": d},
                device_id_type=MESH,
            )

        def start(c):
            for k in range(1, SWAP):
                copy(c, swap_peer(k), me, swap_peer(k)).start()

        def wait_send(c):
            copy(c, swap_peer(1), others, others).wait_send()

        def wait_recv(c):
            copy(c, swap_peer(1), others, others).wait_recv()

        return start, wait_send, wait_recv

    first_start, first_wait_send, first_wait_recv = exchange(
        lambda c, d: first_send.at[c, d], lambda c, d: first_recv.at[c, d], first_ss, first_rs
    )
    cot_start, cot_wait_send, cot_wait_recv = exchange(
        lambda c, d: cotangent.at[d, c], lambda c, d: cot_recv.at[c, d], cot_ss, cot_rs
    )
    mixed_start, mixed_wait_send, mixed_wait_recv = exchange(
        lambda c, d: first_send.at[c, d], lambda c, d: mixed.at[d, c], mixed_ss, mixed_rs
    )
    grad_start, grad_wait_send, grad_wait_recv = exchange(
        lambda c, d: first_recv.at[c, d], lambda c, d: grad_recv.at[c, d], grad_ss, grad_rs
    )

    def own_cot(c):
        return pltpu.make_async_copy(cotangent.at[me, c], cot_recv.at[c, me], own_sem.at[0, c])

    def own_mixed(c):
        return pltpu.make_async_copy(first_send.at[c, me], mixed.at[me, c], own_sem.at[1, c])

    def cot_begin(c):
        own_cot(c).start()
        cot_start(c)

    cot_begin(0)

    vectors[...] = jnp.zeros((16, WIDTH), F32)
    low_half = lax.broadcasted_iota(jnp.int32, (CHUNKS, BLOCK, 128), 2) < 64
    ones_key[0] = jnp.where(low_half, 1.0, 0.0).astype(BF)
    ones_key[1] = jnp.where(low_half, 0.0, 1.0).astype(BF)
    head_sum[...] = jnp.where(
        ((lax.broadcasted_iota(jnp.int32, (256, 128), 0) // 64) & 1)
        == (lax.broadcasted_iota(jnp.int32, (256, 128), 1) // 64),
        1.0,
        0.0,
    ).astype(BF)
    row_cell = lax.broadcasted_iota(jnp.int32, (BLOCK, BLOCK), 0)
    col_cell = lax.broadcasted_iota(jnp.int32, (BLOCK, BLOCK), 1)
    seen = jnp.logical_and((row_cell % PIECE) == (col_cell % PIECE), (col_cell // PIECE) < features)
    feature_bias[...] = jnp.where(seen, 0.0, MASKED).astype(F32)

    def valid_rows(c):
        row = lax.broadcasted_iota(jnp.int32, (BLOCK, 1), 0)
        return (row // PIECE) * (CHUNKS * PIECE) + c * PIECE + row % PIECE < samples

    def half_of(values, half):
        mine = (lanes(values.shape[0]) < 64) == (half == 0)
        return jnp.where(mine, values, jnp.zeros_like(values))

    def add_row(row, values):
        vectors[row : row + 1, :] += jnp.sum(values, axis=0, keepdims=True)

    def block(ref, c):
        return ref[c].reshape(BLOCK, WIDTH)

    for index in (0, 2, 3):
        loads[CHUNKS + index].wait()

    @pl.loop(0, CHUNKS)
    def _(c):
        pltpu.make_async_copy(tokens.at[:, c], x_rows.at[c], load_sem.at[c]).wait()
        vhat, _ = norm_stats(block(x_rows, c).astype(F32))
        normed = (vhat * norm_gain[0:1, :] + norm_bias[0:1, :]).astype(BF)
        normed_one[c] = normed
        valid = valid_rows(c)
        queries = mm(normed, attn_in[0, :, :WIDTH]) * (SCALE * LOG2E)
        for pair in range(PAIRS):
            query_one[c, pair, :, :128] = queries[:, 128 * pair : 128 * pair + 128].astype(BF)
        keys = mm(normed, attn_in[0, :, WIDTH : 2 * WIDTH])

        @pl.when(c == 0)
        def _():
            key_zero[...] = keys[0:8, :]

        keys = jnp.where(valid, keys, key_zero[0:1, :]).astype(BF)
        values = mm(normed, attn_in[0, :, 2 * WIDTH :])
        values = jnp.where(valid, values, 0.0).astype(BF)
        for head in range(HEADS):
            pair, half = head // 2, head % 2
            cut = slice(128 * pair, 128 * pair + 128)
            key_one[head, c] = half_of(keys[:, cut], half)
            value_one[head, c] = half_of(values[:, cut], half)
        for half in range(2):
            mine = (lanes() < 64) == (half == 0)
            ones_value[half, c] = jnp.where(jnp.logical_and(mine, valid), 1.0, 0.0).astype(BF)

    cells = CHUNKS * BLOCK

    def key_all(head):
        return key_one[head].reshape(cells, 128)

    def key_wide(head):
        return jnp.concatenate([key_all(head), ones_key[head % 2].reshape(cells, 128)], axis=1)

    def value_wide(head):
        return jnp.concatenate(
            [value_one[head].reshape(cells, 128), ones_value[head % 2].reshape(cells, 128)], axis=1
        )

    loads[CHUNKS + 1].wait()

    @pl.loop(0, CHUNKS)
    def _(c):
        def put(pair, out, extra):
            attn_one[c, :, 128 * pair : 128 * pair + 128] = out
            query_one[c, pair, :, 128:] = extra

        attention_forward(
            lambda pair: query_one[c, pair, :, :128], key_all, value_wide, None, put
        )
        first = block(x_rows, c).astype(F32) + mm(attn_one[c], attn_out[0])
        first_send[c] = first.astype(BF).reshape(SWAP, PIECE, WIDTH)
        first_recv[c, me] = first_send[c, me]
        first_start(c)

        @pl.when(c == 1)
        def _():
            cot_begin(1)

    def reduction(number, part, one, two, three, done, cut):
        def remote(source, target, index, where):
            return pltpu.make_async_remote_copy(
                src_ref=source,
                dst_ref=target,
                send_sem=sum_ss.at[number, index],
                recv_sem=sum_rs.at[number, index],
                device_id=where,
                device_id_type=MESH,
            )

        beside = {"grp": grp + 1 - 2 * col}
        above = {"grp": grp + 2 - 4 * row}
        out = sums.at[min(number, SUMS - 1), grp, :, cut]
        step_one = [
            remote(part.at[:, 1 - core, :, :, :, cut], one.at[:, :, :, :, cut], 0, {"swap": me + 1 - 2 * core})
        ]
        step_two = [
            remote(one.at[0:2, :, 1 - col, :, cut], two.at[0, :, :, :, cut], 1, beside),
            remote(one.at[2:4, 1 - row, :, :, cut], two.at[1, :, :, :, cut], 2, above),
        ]
        step_three = [
            remote(one.at[0:2, 1 - row, col, :, cut], two.at[2, 0, :, :, cut], 3, above),
            remote(one.at[2:4, row, 1 - col, :, cut], two.at[2, 1, :, :, cut], 4, beside),
        ]
        step_four = [
            remote(one.at[2 * k + 1 - odd, row, col, :, cut], three.at[k, :, cut], 5 + k, {"swap": me + 2 - 4 * odd})
            for k in range(2)
        ]
        step_five = [
            remote(
                one.at[2 - 2 * upper + odd, row, col, :, cut], three.at[2, :, cut], 7, {"swap": me + 4 - 8 * upper}
            )
        ]
        step_six = [remote(done.at[:, cut], out, 7 + k, {"grp": grp_peer(k)}) for k in range(1, GRP)]
        own = pltpu.make_async_copy(done.at[:, cut], out, sum_rs.at[number, 11])

        def begin():
            for copy in step_one:
                copy.start()

        def after_one():
            for copy in step_one:
                copy.wait_recv()

            @pl.loop(0, 4)
            def _(a):
                total = one[a, :, :, :, cut].astype(F32) + part[a, core, :, :, :, cut].astype(F32)
                one[a, :, :, :, cut] = total.astype(BF)

            for copy in step_two:
                copy.start()

        def after_two():
            for copy in step_two:
                copy.wait_recv()
            for a in range(2):
                total = one[a, :, col, :, cut].astype(F32) + two[0, a, :, :, cut].astype(F32)
                one[a, :, col, :, cut] = total.astype(BF)
                total = one[2 + a, row, :, :, cut].astype(F32) + two[1, a, :, :, cut].astype(F32)
                one[2 + a, row, :, :, cut] = total.astype(BF)
            for copy in step_three:
                copy.start()

        def after_three():
            for copy in step_three:
                copy.wait_recv()
            for a in range(4):
                total = one[a, row, col, :, cut].astype(F32) + two[2, a // 2, a % 2, :, cut].astype(F32)
                one[a, row, col, :, cut] = total.astype(BF)
            for copy in step_four:
                copy.start()

        def after_four():
            for copy in step_four:
                copy.wait_recv()
            for k in range(2):
                total = one[2 * k + odd, row, col, :, cut].astype(F32) + three[k, :, cut].astype(F32)
                one[2 * k + odd, row, col, :, cut] = total.astype(BF)
            for copy in step_five:
                copy.start()

        def after_five():
            for copy in step_five:
                copy.wait_recv()
            total = one[chip, row, col, :, cut].astype(F32) + three[2, :, cut].astype(F32)
            done[:, cut] = total.astype(BF)
            own.start()
            for copy in step_six:
                copy.start()

        def finish():
            own.wait()
            for copy in step_six:
                copy.wait_recv()
            for copy in step_one + step_two + step_three + step_four + step_five + step_six:
                copy.wait_send()

        return [begin, after_one, after_two, after_three, after_four, after_five, finish]

    every = slice(0, WIDTH)
    mid = [
        reduction(
            number,
            part_sum.at[number],
            one_sum.at[number],
            two_sum.at[number],
            three_sum.at[number],
            done_sum.at[number],
            every,
        )
        for number in range(3)
    ]
    end = [
        reduction(
            3 + half,
            mlp_out,
            grad_hidden.at[0],
            grad_hidden.at[1, 0:3],
            grad_hidden.at[2, 0:3, 0, 0],
            grad_hidden.at[3, 0, 0, 0],
            slice(256 * half, 256 * half + 256),
        )
        for half in range(2)
    ]

    def rows_of(ref):
        return ref[...].reshape(cells, WIDTH)

    def shares(values):
        return values.astype(BF).reshape(4, 2, 2, 2, 16, values.shape[1])

    def put_shares(number, piece, tile):
        part_sum[number, :, :, :, :, 16 * piece : 16 * piece + 16, :] = shares(tile)

    def grads_in(part):
        put_shares(0, part, mm(rows_of(normed_three), grad_hidden[part].reshape(cells, WIDTH), TN))

    def grads_out(part):
        tile = mm(active[part].reshape(cells, WIDTH), rows_of(cot_recv), TN)
        part_sum[1, part] = tile.astype(BF).reshape(2, 2, 2, SHARE, WIDTH)

    def wide_grads(part):
        cut = slice(WIDTH * part, WIDTH * part + WIDTH)
        put_shares(2, part, mm(rows_of(normed_two), grad_packed[:, :, cut].reshape(cells, WIDTH), TN))
        if part == 2:
            put_shares(2, 3, mm(rows_of(attn_two), rows_of(grad_low), TN))

    for index in range(4, 10):
        loads[CHUNKS + index].wait()

    def delta_of(grad, out):
        product = grad.astype(F32) * out.astype(F32)
        high = product.astype(BF)
        low = (product - high.astype(F32)).astype(BF)
        return split_three(-mm(jnp.concatenate([high, low], axis=1), head_sum[...]))

    @pl.loop(0, CHUNKS)
    def _(c):
        @pl.when(c == 0)
        def _():
            cot_begin(2)

        @pl.when(c == 1)
        def _():
            cot_begin(3)

        first_wait_recv(c)

        @pl.when(c == 3)
        def _():
            grad_start(1)

        resid_one = block(first_recv, c).astype(F32)
        vhat_two, inverse_two = norm_stats(resid_one)
        normed = (vhat_two * norm_gain[1:2, :] + norm_bias[1:2, :]).astype(BF)
        normed_two[c] = normed
        queries = mm(normed, attn_in[1, :, :WIDTH]) * (SCALE * LOG2E)
        keys = mm(normed, attn_in[1, :, WIDTH : 2 * WIDTH]).astype(BF)
        values = mm(normed, attn_in[1, :, 2 * WIDTH :]).astype(BF)
        for pair in range(PAIRS):
            cut = slice(128 * pair, 128 * pair + 128)
            query_two[pair, :, :128] = queries[:, cut].astype(BF)
            for half in range(2):
                key_two[2 * pair + half, :, :128] = half_of(keys[:, cut], half)
                key_two[2 * pair + half, :, 128:] = ones_key[half, 0]
                value_two[2 * pair + half, :, :128] = half_of(values[:, cut], half)
                value_two[2 * pair + half, :, 128:] = ones_key[half, 0]

        def put(pair, out, extra):
            attn_two[c, :, 128 * pair : 128 * pair + 128] = out
            query_two[pair, :, 128:] = extra

        attention_forward(
            lambda pair: query_two[pair, :, :128],
            lambda head: key_two[head, :, :128],
            lambda head: value_two[head],
            feature_bias[...],
            put,
        )
        second = resid_one + mm(attn_two[c], attn_out[1])
        vhat_three, inverse_three = norm_stats(second)
        normed = (vhat_three * norm_gain[2:3, :] + norm_bias[2:3, :]).astype(BF)
        normed_three[c] = normed
        own_cot(c).wait()
        cot_wait_recv(c)
        cot_low = block(cot_recv, c)
        cot = cot_low.astype(F32)
        add_row(10, cot)

        @pl.when(c == 2)
        def _():
            grad_start(0)


        @pl.when(c == 3)
        def _():
            grad_start(2)

        outcome = second + mlp_out_bias[...]
        grad_normed = jnp.zeros((BLOCK, WIDTH), F32)
        for part in range(4):
            cut = slice(WIDTH * part, WIDTH * part + WIDTH)
            hidden = mm(normed, mlp_in[:, cut]) + mlp_in_bias[:, cut]
            weight_out = mlp_out[part].reshape(WIDTH, WIDTH)
            grad_active = mm(cot_low, weight_out, NT)
            below = 0.5 + 0.5 * lax.erf(hidden * 0.7071067811865476)
            act = (hidden * below).astype(BF)
            density = jnp.exp2(hidden * hidden * (-0.5 * LOG2E)) * 0.3989422804014327
            grad_hid = ((below + hidden * density) * grad_active).astype(BF)
            active[part, c] = act
            grad_hidden[part, c] = grad_hid.reshape(2, 2, SHARE, WIDTH)
            add_row(6 + part, grad_hid.astype(F32))
            outcome = outcome + mm(act, weight_out)
            grad_normed = grad_normed + mm(grad_hid, mlp_in[:, cut], NT)

        @pl.when(c == CHUNKS - 1)
        def _():
            for part in range(4):
                grads_in(part)
            mid[0][0]()
            for part in range(4):
                grads_out(part)
            mid[1][0]()

        first_wait_send(c)
        first_send[c] = outcome.astype(BF).reshape(SWAP, PIECE, WIDTH)
        add_row(2, grad_normed * vhat_three)
        add_row(5, grad_normed)
        grad_second = cot + norm_back(grad_normed, vhat_three, inverse_three, norm_gain[2:3, :])
        grad_second_low = grad_second.astype(BF)
        grad_low[c] = grad_second_low
        grad_attn = mm(grad_second_low, attn_out[1], NT).astype(BF)
        for pair in range(PAIRS):
            cut = slice(128 * pair, 128 * pair + 128)
            piece = grad_attn[:, cut]
            wide = jnp.concatenate([piece, delta_of(piece, attn_two[c, :, cut])], axis=1)
            grad_q, grad_k, grad_v = attention_back(
                query_two[pair],
                wide,
                lambda half: key_two[2 * pair + half],
                lambda half: value_two[2 * pair + half],
                feature_bias[...],
            )
            grad_packed[c, :, 128 * pair : 128 * pair + 128] = (grad_q * SCALE).astype(BF)
            grad_packed[c, :, WIDTH + 128 * pair : WIDTH + 128 * pair + 128] = (grad_k * LN2).astype(BF)
            grad_packed[c, :, 2 * WIDTH + 128 * pair : 2 * WIDTH + 128 * pair + 128] = grad_v.astype(BF)
        grad_normed = mm(grad_packed[c], attn_in[1], NT)
        add_row(1, grad_normed * vhat_two)
        add_row(4, grad_normed)
        grad_first = grad_second + norm_back(grad_normed, vhat_two, inverse_two, norm_gain[1:2, :])
        first_recv[c] = grad_first.astype(BF).reshape(SWAP, PIECE, WIDTH)
        grad_recv[c, me] = first_recv[c, me]
        own_mixed(c).start()

        @pl.when(c == CHUNKS - 1)
        def _():
            grad_start(c)

    mid[0][1]()

    for part in range(3):
        wide_grads(part)
    mid[2][0]()
    mid[1][1]()

    def run(hooks, c):
        for when, call in hooks:

            @pl.when(c == when)
            def _():
                call()

    hooks = (
        (),
        ((0, mid[2][1]), (2, mid[0][2]), (3, mid[1][2]), ),
        (),
        ((0, mid[2][2]), (1, mid[0][3]), (1, end[0][1]), (2, mid[1][3]), (3, mid[0][4]), (3, mid[2][3]), (3, end[0][2]), ),
        ((0, mid[1][4]), (0, end[1][1]), (1, mid[0][5]), (1, mid[2][4]), (2, end[0][3]), (2, end[1][2]), (3, mid[1][5]), ),
    )
    for half in range(2):
        pairs = (2 * half, 2 * half + 1)
        grad_key[...] = jnp.zeros((2, cells, 128), F32)
        grad_value[...] = jnp.zeros((2, cells, 128), F32)

        @pl.loop(0, CHUNKS)
        def _(c):
            if half == 0:
                grad_wait_recv(c)
                mixed_start(c)
                grad_attn = mm(block(grad_recv, c), attn_out[0], NT).astype(BF)
                for pair in range(PAIRS):
                    cut = slice(128 * pair, 128 * pair + 128)
                    piece = grad_attn[:, cut]
                    active[pair, c, :, :128] = piece
                    active[pair, c, :, 128:256] = delta_of(piece, attn_one[c, :, cut])
            for pair in pairs:
                grad_q, grad_k, grad_v = attention_back(
                    query_one[c, pair],
                    active[pair, c, :, :256],
                    lambda side: key_wide(2 * pair + side),
                    lambda side: value_wide(2 * pair + side),
                    None,
                )
                grad_packed[c, :, 128 * pair : 128 * pair + 128] = (grad_q * SCALE).astype(BF)
                grad_key[pair % 2] += grad_k
                grad_value[pair % 2] += grad_v
                run(hooks[pair], c)

        for pair in pairs:
            for c in range(CHUNKS):
                rows = slice(BLOCK * c, BLOCK * c + BLOCK)
                grad_packed[c, :, WIDTH + 128 * pair : WIDTH + 128 * pair + 128] = (
                    grad_key[pair % 2, rows, :] * LN2
                ).astype(BF)
                grad_packed[c, :, 2 * WIDTH + 128 * pair : 2 * WIDTH + 128 * pair + 128] = jnp.where(
                    valid_rows(c), grad_value[pair % 2, rows, :], 0.0
                ).astype(BF)
        if half == 0:
            grad_rows = grad_recv[...].reshape(cells, WIDTH)
            mlp_out[:, :, :, :, 0:16, :] = shares(mm(rows_of(attn_one), grad_rows, TN))
        for part in range(3):
            cut = slice(WIDTH * part + 256 * half, WIDTH * part + 256 * half + 256)
            tile = mm(rows_of(normed_one), grad_packed[:, :, cut].reshape(cells, 256), TN)
            mlp_out[:, :, :, :, 16 + 16 * part : 32 + 16 * part, 256 * half : 256 * half + 256] = shares(tile)
        end[half][0]()

    @pl.loop(0, CHUNKS)
    def _(c):
        grad_normed = mm(grad_packed[c], attn_in[0], NT)
        vhat, inverse = norm_stats(block(x_rows, c).astype(F32))
        add_row(0, grad_normed * vhat)
        add_row(3, grad_normed)
        result = block(grad_recv, c).astype(F32) + norm_back(grad_normed, vhat, inverse, norm_gain[0:1, :])
        normed_one[c] = result.astype(BF)
        pltpu.make_async_copy(
            normed_one.at[c].reshape(SWAP, PIECE, WIDTH), tokens_grad.at[:, c], out_sem.at[c]
        ).start()
        run(hooks[4], c)

    def vec_copy(source, target, index, where):
        return pltpu.make_async_remote_copy(
            src_ref=source,
            dst_ref=target,
            send_sem=vec_ss.at[index],
            recv_sem=vec_rs.at[index],
            device_id=where,
            device_id_type=MESH,
        )

    vec_one = vec_copy(vectors, vec_pair, 0, {"swap": me + 1 - 2 * core})
    vec_two = [vec_copy(vec_grp.at[grp], vec_grp.at[grp], k, {"grp": grp_peer(k)}) for k in range(1, GRP)]
    vec_two_in = [
        vec_copy(vec_grp.at[grp_peer(-k)], vec_grp.at[grp_peer(-k)], k, {"grp": grp_peer(-k)}) for k in range(1, GRP)
    ]
    vec_three = [vec_copy(vec_z.at[chip], vec_z.at[chip], 3 + k, {"swap": z_peer(k)}) for k in range(1, 4)]
    vec_three_in = [
        vec_copy(vec_z.at[(chip - k) % 4], vec_z.at[(chip - k) % 4], 3 + k, {"swap": z_peer(-k)}) for k in range(1, 4)
    ]
    vec_one.start()
    mid[2][5]()
    end[0][4]()
    end[1][3]()
    vec_one.wait_recv()
    vec_grp[grp] = vectors[...] + vec_pair[...]
    for copy in vec_two:
        copy.start()
    end[0][5]()
    end[1][4]()
    for copy in vec_two_in:
        copy.wait_recv()
    vec_z[chip] = (vec_grp[0] + vec_grp[1]) + (vec_grp[2] + vec_grp[3])
    for copy in vec_three:
        copy.start()
    end[1][5]()
    for copy in vec_three_in:
        copy.wait_recv()
    whole = (vec_z[0] + vec_z[1]) + (vec_z[2] + vec_z[3])

    def share(rows, width, step):
        result = None
        for index in range(WIDTH // width):
            piece = whole[rows, index * width : index * width + width]
            mine = step == index
            result = jnp.where(mine, piece, 0.0 if result is None else result)
        return result

    small[0:3, 0:64] = share(slice(0, 3), 64, me)
    small[3:6, 0:64] = share(slice(3, 6), 64, me)
    bias_row = None
    for index in range(4):
        piece = share(slice(6 + index, 7 + index), 256, core)
        bias_row = jnp.where(chip == index, piece, 0.0 if bias_row is None else bias_row)
    small[6:7, :] = bias_row
    small[7:8, 0:64] = share(slice(10, 11), 64, me)

    for steps in mid + end:
        steps[6]()
    vec_one.wait_send()
    for copy in vec_two + vec_three:
        copy.wait_send()

    @pl.loop(0, CHUNKS)
    def _(c):
        own_mixed(c).wait()
        mixed_wait_recv(c)
        mixed_wait_send(c)
        cot_wait_send(c)
        grad_wait_send(c)
        pltpu.make_async_copy(
            normed_one.at[c].reshape(SWAP, PIECE, WIDTH), tokens_grad.at[:, c], out_sem.at[c]
        ).wait()


def finish_kernel(mixed, tokens_grad, sums_hbm, small_hbm, *refs):
    results, (sums, small, held, in_two, out_two, in_mlp, out_mlp, sem) = refs[:10], refs[10:]
    outs = [*results[:2], in_two, out_two, *results[4:6], in_mlp, results[7], out_mlp, results[9]]
    stores = [
        pltpu.make_async_copy(outs[k], results[k], sem.at[SUMS + 9 + n]) for n, k in enumerate((8, 6, 2, 3))
    ]
    loads = [pltpu.make_async_copy(sums_hbm.at[k], sums.at[k], sem.at[k]) for k in range(SUMS)]
    loads.append(pltpu.make_async_copy(small_hbm, small, sem.at[SUMS]))
    cells_in, cells_out = [], []
    for index, source in enumerate((mixed, tokens_grad)):
        for half in range(2):
            part = slice(4 * half, 4 * half + 4)
            place = SUMS + 1 + 2 * index + half
            cells_in.append(pltpu.make_async_copy(source.at[part], held.at[index, part], sem.at[place]))
            cells_out.append(pltpu.make_async_copy(held.at[index, part], outs[index].at[part], sem.at[place + 4]))
    for copy in cells_in + loads:
        copy.start()
    for before, after in zip(cells_in, cells_out):
        before.wait()
        after.start()
    for copy in loads:
        copy.wait()
    for grp in range(GRP):
        outs[8][SHARE * grp : SHARE * grp + SHARE] = sums[1, grp].astype(F32)
    stores[0].start()
    for grp in range(GRP):
        rows = slice(16 * grp, 16 * grp + 16)
        for part in range(4):
            cut = slice(WIDTH * part, WIDTH * part + WIDTH)
            outs[6][rows, cut] = sums[0, grp, 16 * part : 16 * part + 16].astype(F32)
    stores[1].start()
    for grp in range(GRP):
        rows = slice(16 * grp, 16 * grp + 16)
        for part in range(3):
            cut = slice(WIDTH * part, WIDTH * part + WIDTH)
            outs[2][1, rows, cut] = sums[2, grp, 16 * part : 16 * part + 16].astype(F32)
            outs[2][0, rows, cut] = sums[3, grp, 16 * part + 16 : 16 * part + 32].astype(F32)
        outs[3][1, rows] = sums[2, grp, 48:64].astype(F32)
        outs[3][0, rows] = sums[3, grp, 0:16].astype(F32)
    stores[2].start()
    stores[3].start()
    outs[4][...] = small[0:3, 0:64]
    outs[5][...] = small[3:6, 0:64]
    outs[7][...] = small[6:7, 0:256]
    outs[9][...] = small[7:8, 0:64]
    for copy in cells_out + stores:
        copy.wait()


def fused_local(
    tokens,
    sample_counts,
    feature_counts,
    attn_in,
    attn_out,
    norm_gain,
    norm_bias,
    mlp_in,
    mlp_in_bias,
    mlp_out,
    mlp_out_bias,
    cotangent,
):
    cells = (SWAP, CHUNKS, PIECE, WIDTH)
    blocks = (CHUNKS, SWAP, PIECE, WIDTH)
    rows = (CHUNKS, BLOCK, WIDTH)
    anywhere = pl.BlockSpec(memory_space=pl.ANY)
    scalar = pl.BlockSpec(memory_space=pltpu.SMEM)
    vector = pl.BlockSpec(memory_space=pltpu.VMEM)
    sem = pltpu.SemaphoreType.DMA

    def buffer(*shape, kind=BF):
        return pltpu.VMEM(shape, kind)

    def result(shape, kind=F32):
        return jax.ShapeDtypeStruct(shape, kind)

    mixed, tokens_grad, sums, small = pl.pallas_call(
        fused_kernel,
        name="layer",
        out_shape=(
            result(cells, BF),
            result(cells, BF),
            result((SUMS, GRP, SHARE, WIDTH), BF),
            result((8, 256)),
        ),
        in_specs=[anywhere, anywhere, scalar, scalar] + [anywhere] * 8,
        out_specs=(anywhere, anywhere, anywhere, vector),
        scratch_shapes=[
            buffer(2, WIDTH, 3 * WIDTH),
            buffer(2, WIDTH, WIDTH),
            buffer(3, WIDTH, kind=F32),
            buffer(3, WIDTH, kind=F32),
            buffer(WIDTH, 4 * WIDTH),
            buffer(1, 4 * WIDTH, kind=F32),
            buffer(4, 2, 2, 2, SHARE, WIDTH),
            buffer(1, WIDTH, kind=F32),
            buffer(*blocks),
            buffer(*rows),
            buffer(CHUNKS, PAIRS, BLOCK, 256),
            buffer(HEADS, CHUNKS, BLOCK, 128),
            buffer(HEADS, CHUNKS, BLOCK, 128),
            buffer(2, CHUNKS, BLOCK, 128),
            buffer(2, CHUNKS, BLOCK, 128),
            buffer(*rows),
            buffer(*blocks),
            buffer(*blocks),
            buffer(*blocks),
            buffer(*blocks),
            buffer(*rows),
            buffer(*rows),
            buffer(*rows),
            buffer(4, *rows),
            buffer(4, CHUNKS, 2, 2, SHARE, WIDTH),
            buffer(CHUNKS, BLOCK, 3 * WIDTH),
            buffer(*rows),
            buffer(PAIRS, BLOCK, 256),
            buffer(HEADS, BLOCK, 256),
            buffer(HEADS, BLOCK, 256),
            buffer(BLOCK, BLOCK, kind=F32),
            buffer(8, WIDTH, kind=F32),
            buffer(2, CHUNKS * BLOCK, 128, kind=F32),
            buffer(2, CHUNKS * BLOCK, 128, kind=F32),
            buffer(256, 128),
            buffer(16, WIDTH, kind=F32),
            buffer(16, WIDTH, kind=F32),
            buffer(GRP, 16, WIDTH, kind=F32),
            buffer(4, 16, WIDTH, kind=F32),
            buffer(3, 4, 2, 2, 2, SHARE, WIDTH),
            buffer(3, 4, 2, 2, SHARE, WIDTH),
            buffer(3, 3, 2, 2, SHARE, WIDTH),
            buffer(3, 3, SHARE, WIDTH),
            buffer(3, SHARE, WIDTH),
            sem((CHUNKS + 10,)),
        ]
        + [sem((CHUNKS,))] * 8
        + [sem((2, CHUNKS)), sem((CHUNKS,))]
        + [sem((5, 12))] * 2
        + [sem((7,))] * 2,
        compiler_params=pltpu.CompilerParams(
            collective_id=0, has_side_effects=True, vmem_limit_bytes=VMEM_LIMIT
        ),
    )(
        tokens.reshape(cells),
        cotangent.reshape(cells),
        sample_counts,
        feature_counts,
        attn_in,
        attn_out,
        norm_gain,
        norm_bias,
        mlp_in,
        mlp_in_bias.reshape(1, -1),
        mlp_out.reshape(4, 2, 2, 2, SHARE, WIDTH),
        mlp_out_bias.reshape(1, -1),
    )
    shapes = (
        result(cells, BF),
        result(cells, BF),
        result((2, 64, 3 * WIDTH)),
        result((2, 64, WIDTH)),
        result((3, 64)),
        result((3, 64)),
        result((64, 4 * WIDTH)),
        result((1, 256)),
        result((256, WIDTH)),
        result((1, 64)),
    )
    outs = pl.pallas_call(
        finish_kernel,
        name="results",
        out_shape=shapes,
        in_specs=[anywhere] * 4,
        out_specs=(anywhere,) * 4 + (vector,) * 2 + (anywhere, vector, anywhere, vector),
        scratch_shapes=[
            buffer(SUMS, GRP, SHARE, WIDTH),
            buffer(8, 256, kind=F32),
            buffer(2, *cells),
            buffer(2, 64, 3 * WIDTH, kind=F32),
            buffer(2, 64, WIDTH, kind=F32),
            buffer(64, 4 * WIDTH, kind=F32),
            buffer(256, WIDTH, kind=F32),
            sem((SUMS + 13,)),
        ],
        compiler_params=pltpu.CompilerParams(vmem_limit_bytes=VMEM_LIMIT),
    )(mixed, tokens_grad, sums, small)
    return (
        outs[0].reshape(tokens.shape),
        outs[1].reshape(tokens.shape),
        *outs[2:7],
        outs[7].reshape(-1),
        outs[8],
        outs[9].reshape(-1),
    )


def solution(mesh):
    placed = (
        P("grp", None, "swap", None),
        P("grp"),
        P("grp"),
        P(),
        P(),
        P(),
        P(),
        P(),
        P(),
        P(),
        P(),
        P("grp", None, "swap", None),
    )
    def layer(*args):
        tokens, mlp_in = args[0], args[7]
        fits = (
            (mesh.shape["swap"], mesh.shape["grp"]) == (SWAP, GRP)
            and tokens.shape == (1, CHUNKS * BLOCK, 1, WIDTH)
            and mlp_in.shape == (WIDTH, 4 * WIDTH)
        )
        return fused_local(*args) if fits else local(*args)

    return jax.shard_map(
        layer,
        mesh=mesh,
        in_specs=placed,
        out_specs=(
            P("grp", None, "swap", None),
            P("grp", None, "swap", None),
            P(None, "swap", None),
            P(None, "swap", None),
            P(None, "swap"),
            P(None, "swap"),
            P("swap", None),
            P("swap"),
            P("swap", None),
            P("swap"),
        ),
        check_vma=False,
    )
```
